256 devices in a mesh: tok: 64 (over z, x, core), hv: 4 (over y).
Axes of the slice: x: 4, y: 4, z: 8, core: 2. Of those that a mesh axis runs over, the one named last changes fastest.
Arguments:
- tokens: bfloat16 [16384, 2048], P(('tok', 'hv')), may hold values from -6 to 6
- prompt_lengths: int32 [33], replicated, may hold values from 1 to 10922, 16384 in all
- query_weight: bfloat16 [2048, 1024], P(None, 'hv'), may hold values from -0.125 to 0.125
- key_weight: bfloat16 [2048, 1024], P(None, 'hv'), may hold values from -0.125 to 0.125
- value_weight: bfloat16 [2048, 2048], P(None, 'hv'), may hold values from -0.125 to 0.125
- query_conv: bfloat16 [4, 1024], P(None, 'hv'), may hold values from -3 to 3
- key_conv: bfloat16 [4, 1024], P(None, 'hv'), may hold values from -3 to 3
- value_conv: bfloat16 [4, 2048], P(None, 'hv'), may hold values from -3 to 3
- decay_down: bfloat16 [2048, 16], replicated, may hold values from -0.125 to 0.125
- decay_up: bfloat16 [16, 1024], P(None, 'hv'), may hold values from -3 to 3
- decay_bias: float32 [1024], P('hv')
- gate_weight: bfloat16 [2048, 2048], P(None, 'hv'), may hold values from -0.125 to 0.125
- norm_gain: float32 [512], replicated, may hold values from 0.1 to 1.9
- out_weight: bfloat16 [2048, 2048], P('hv'), may hold values from -0.125 to 0.125
Outputs:
- mixed: bfloat16 [16384, 2048], P(('tok', 'hv'))
- segment_states: float32 [64, 4, 256, 512], P('tok', 'hv')
- conv_edges: bfloat16 [64, 3, 4, 1024], P('tok', None, 'hv')
The draws below stay inside these ranges and needn't reach their ends.
Inputs may be any that keep to these rules, and one draw needn't show every extreme that they name: `prompt_lengths`: the rows of 33 prompts that fill all 16384 packed rows; exactly one prompt has 10922 rows.
All inputs are finite; a program needn't handle non-finite values.
Results may differ from the reference program's by a relative error of at most 0.022.
Values may be sent and summed in bfloat16 or wider, within the bound.
A program may use at most 128 MiB of HBM per device.

```python
import math
import jax
import jax.numpy as jnp
import numpy as np
from jax import lax

D = 2048
H = 4
DK = 256
DV = 512
RANK = 16
CONV = 4
SPAN = 64
TOK_DEV = 256
TOKENS = 16384
PROMPTS = 33
LONG = 10922
HK = 1024
HV = 2048
N_TOK = 64


def draw_decay_bias(key, part):
    choose_key, slow_key, fast_key = jax.random.split(key, 3)
    share = 0.5
    slow_mask = jax.random.uniform(choose_key, (HK,)) < share
    slow_bias = math.log(LONG / 2.0) + jax.random.uniform(slow_key, (HK,), minval=0.0, maxval=1.5)
    fast_bias = jax.random.uniform(fast_key, (HK,), minval=-0.5, maxval=1.0)
    return jnp.where(slow_mask, slow_bias, fast_bias).astype(jnp.float32)


def levels(rng, dims, cuts, least, largest):
    level, own = 1.0, jax.random.fold_in(rng, 6)
    for dim, blocks in cuts:
        heights = jnp.exp(jax.random.uniform(jax.random.fold_in(own, dim), (blocks,), jnp.float32, least / len(cuts), largest / len(cuts)))
        level = level * jnp.repeat(heights, dims[dim] // blocks).reshape([-1 if axis == dim else 1 for axis in range(len(dims))])
    return level


def split_up(count, total, most, lean):
    weights = [(1 << 20) // math.isqrt(standing ** lean) + 1 for standing in range(2, count + 1)]
    spare, counts = total - most - (count - 1), [1] * (count - 1)
    while spare > 0:
        movable = [i for i in range(count - 1) if counts[i] < most]
        pool, left = sum([weights[i] for i in movable]), spare
        for i in movable:
            more = min(most - counts[i], max(1, left * weights[i] // pool), spare)
            counts[i] = counts[i] + more
            spare = spare - more
    return np.array([most] + counts)


def uneven_parts(rng, number_of, total, limit, skew):
    if number_of == 2:
        one = jax.random.randint(rng, (), max(1, total - limit), min(limit, total - 1) + 1)
        return jnp.stack([one, total - one])
    tallies = jnp.asarray(split_up(number_of, total, limit, skew), jnp.int32)
    couples = (number_of - 1) // 2
    donor, sink = tallies[1:1 + 2 * couples:2], tallies[2:2 + 2 * couples:2]
    margin = jnp.minimum(donor - 1, limit - sink)
    moved = jax.random.randint(jax.random.fold_in(rng, 1), (couples,), 0, 1 << 20) % (margin + 1)
    tallies = tallies.at[1:1 + 2 * couples:2].set(donor - moved).at[2:2 + 2 * couples:2].set(sink + moved)
    return tallies[jax.random.permutation(jax.random.fold_in(rng, 2), number_of)]


def gaussian(rng, shape, spread, most, shards=(), kind=jnp.bfloat16):
    loudness = levels(rng, shape, shards, -0.22, 0.18) if shards else 1.0
    result = jax.random.normal(rng, shape, jnp.float32) * spread * loudness
    return jnp.minimum(jnp.maximum(result, -most), most).astype(kind)


def setup_inputs(seed: int = 0) -> dict:
    arg_keys = jax.random.split(jax.random.key(seed), 15)
    return {
        "tokens": gaussian(arg_keys[0], (TOKENS, D), 1.0, 6.0, ((0, 256),)),
        "prompt_lengths": uneven_parts(arg_keys[1], PROMPTS, TOKENS, LONG, 2).astype(jnp.int32),
        "query_weight": gaussian(arg_keys[2], (D, HK), D ** -0.5, 0.125, ((1, 4),)),
        "key_weight": gaussian(arg_keys[3], (D, HK), D ** -0.5, 0.125, ((1, 4),)),
        "value_weight": gaussian(arg_keys[4], (D, HV), D ** -0.5, 0.125, ((1, 4),)),
        "query_conv": gaussian(arg_keys[5], (CONV, HK), CONV ** -0.5, 3.0, ((1, 4),)),
        "key_conv": gaussian(arg_keys[6], (CONV, HK), CONV ** -0.5, 3.0, ((1, 4),)),
        "value_conv": gaussian(arg_keys[7], (CONV, HV), CONV ** -0.5, 3.0, ((1, 4),)),
        "decay_down": gaussian(arg_keys[8], (D, RANK), D ** -0.5, 0.125),
        "decay_up": gaussian(arg_keys[9], (RANK, HK), (RANK // 4) ** -0.5, 3.0, ((1, 4),)),
        "decay_bias": draw_decay_bias(jax.random.fold_in(arg_keys[14], 71), 0),
        "gate_weight": gaussian(arg_keys[11], (D, HV), D ** -0.5, 0.125, ((1, 4),)),
        "norm_gain": jnp.clip(1.0 + 0.18 * jax.random.normal(arg_keys[12], (DV,), jnp.float32), 0.1, 1.9),
        "out_weight": gaussian(arg_keys[13], (HV, D), HV ** -0.5, 0.125, ((0, 4),)),
    }


HIGHEST_PRECISION = lax.Precision.HIGHEST

def prompt_marks(positions, offsets):
    before = offsets[None, :] <= positions[:, None]
    prompt_first = lax.optimization_barrier(jnp.max(jnp.where(before, offsets[None, :], 0), axis=1)).astype(jnp.int32)
    return (prompt_first, (prompt_first == positions).astype(jnp.float32))

def short_conv(raw_rows, before_rows, weight, positions, prompt_first):
    tap_count = weight.shape[0]
    extended = jnp.concatenate([before_rows, raw_rows], axis=0)
    summed = jnp.zeros(raw_rows.shape, jnp.float32)
    for tap_index in range(tap_count):
        lag_rows = tap_count - 1 - tap_index
        inside_prompt = (positions - lag_rows >= prompt_first).astype(jnp.float32)
        window = lax.slice_in_dim(extended, tap_index, tap_index + raw_rows.shape[0], axis=0)
        summed = summed + weight[tap_index].astype(jnp.float32)[None, :] * window.astype(jnp.float32) * inside_prompt[:, None]
    return jax.nn.silu(summed).astype(jnp.bfloat16)

def span_parts(head_keys, head_values, decays, starts):
    cumulative = jnp.cumsum(decays, axis=0)
    groups = jnp.cumsum(starts)
    intact = (groups == 0.0).astype(jnp.float32)
    final_log = cumulative[-1]
    in_tail = (groups == groups[-1]).astype(jnp.float32)
    weighted = (head_keys.astype(jnp.float32) * jnp.exp(final_log[None, :] - cumulative) * in_tail[:, None]).astype(jnp.bfloat16)
    update = lax.dot_general(weighted, head_values, (((0,), (0,)), ((), ())), preferred_element_type=jnp.float32)
    step_decay = jnp.exp(final_log) * intact[-1]
    return (cumulative, groups, intact, update, step_decay)

def span_step(carried, pieces):
    memory, product = carried
    queries, head_keys, head_values, decays, starts = pieces
    cumulative, groups, intact, update, step_decay = span_parts(head_keys, head_values, decays, starts)
    index_rows = jnp.arange(queries.shape[0])
    allowed = (groups[:, None] == groups[None, :]) & (index_rows[:, None] >= index_rows[None, :])
    lifted = queries.astype(jnp.float32) * jnp.exp(cumulative)
    lowered = (head_keys.astype(jnp.float32) * jnp.exp(-cumulative)).astype(jnp.bfloat16)
    raw_scores = lax.dot_general(lifted.astype(jnp.bfloat16), lowered, (((1,), (1,)), ((), ())), preferred_element_type=jnp.float32)
    scores = jnp.where(allowed, raw_scores, 0.0).astype(jnp.bfloat16)
    inside = jnp.dot(scores, head_values, preferred_element_type=jnp.float32)
    outside = jnp.dot(lifted * intact[:, None], memory, precision=HIGHEST_PRECISION)
    reaches = product[None, :] * jnp.exp(cumulative) * intact[:, None]
    return ((step_decay[:, None] * memory + update, product * step_decay), (inside + outside, reaches))

def sweep(queries, head_keys, head_values, decays, starts, memory):
    block_count = queries.shape[0] // SPAN

    def blocked(array_in):
        return array_in.reshape((block_count, SPAN) + array_in.shape[1:])
    initial = (memory, jnp.ones((decays.shape[1],), jnp.float32))
    (closing, product), (outputs, reaches) = lax.scan(span_step, initial, (blocked(queries), blocked(head_keys), blocked(head_values), blocked(decays), blocked(starts)))
    row_count = queries.shape[0]
    return (outputs.reshape((row_count, head_values.shape[1])), reaches.reshape((row_count, decays.shape[1])), closing, product)

def run_head(queries, head_keys, head_values, decays, starts):

    def cut(array_in):
        return array_in.reshape((N_TOK, TOK_DEV) + array_in.shape[1:])

    def block_step(memory, pieces):
        outputs, _, closing, _ = sweep(pieces[0], pieces[1], pieces[2], pieces[3], pieces[4], memory)
        return (closing, (outputs, closing))
    initial = jnp.zeros((DK, DV), jnp.float32)
    _, (outputs, closings) = lax.scan(block_step, initial, (cut(queries), cut(head_keys), cut(head_values), cut(decays), cut(starts)))
    return (outputs.reshape((TOKENS, DV)), closings)

def reference(tokens, prompt_lengths, query_weight, key_weight, value_weight, query_conv, key_conv, value_conv, decay_down, decay_up, decay_bias, gate_weight, norm_gain, out_weight):
    positions = jnp.arange(TOKENS, dtype=jnp.int32)
    offsets = (jnp.cumsum(prompt_lengths) - prompt_lengths).astype(jnp.int32)
    prompt_first, starts = prompt_marks(positions, offsets)

    def project(weight):
        return jnp.dot(tokens, weight, preferred_element_type=jnp.float32).astype(jnp.bfloat16)
    raw_query = project(query_weight)
    raw_key = project(key_weight)
    raw_value = project(value_weight)
    gate_values = project(gate_weight)
    low_rank = project(decay_down)
    decays = jax.nn.log_sigmoid(jnp.dot(low_rank, decay_up, preferred_element_type=jnp.float32) + decay_bias) / 16.0
    rim_rows = CONV - 1

    def convolve(raw_rows, weight):
        before_rows = jnp.zeros((rim_rows, raw_rows.shape[1]), jnp.bfloat16)
        return short_conv(raw_rows, before_rows, weight, positions, prompt_first)
    conv_query = convolve(raw_query, query_conv)
    conv_key = convolve(raw_key, key_conv)
    conv_value = convolve(raw_value, value_conv)
    summed = jnp.zeros((TOKENS, D), jnp.float32)
    closings = []
    for head_index in range(H):
        k_lo = head_index * DK
        v_lo = head_index * DV
        heads_out, closing = run_head(conv_query[:, k_lo:k_lo + DK], conv_key[:, k_lo:k_lo + DK], conv_value[:, v_lo:v_lo + DV], decays[:, k_lo:k_lo + DK], starts)
        gate_float = gate_values[:, v_lo:v_lo + DV].astype(jnp.float32)
        rescale = lax.rsqrt(lax.optimization_barrier(jnp.mean(heads_out * heads_out, axis=1, keepdims=True)) + 1e-05)
        gated_out = (heads_out * rescale * norm_gain[None, :] * gate_float * jax.nn.sigmoid(gate_float)).astype(jnp.bfloat16)
        partial_value = jnp.dot(gated_out, out_weight[v_lo:v_lo + DV, :], preferred_element_type=jnp.float32).astype(jnp.bfloat16)
        partial_value = lax.optimization_barrier(partial_value)
        summed = summed + partial_value.astype(jnp.float32)
        closings.append(closing)
    mixed = summed.astype(jnp.bfloat16)
    segment_states = jnp.stack(closings, axis=1)
    joined = jnp.concatenate([raw_query.reshape(TOKENS, H, DK), raw_key.reshape(TOKENS, H, DK), raw_value.reshape(TOKENS, H, DV)], axis=2)
    joined = joined.reshape(N_TOK, TOK_DEV, H, 2 * DK + DV)[:, TOK_DEV - rim_rows:]
    spots = positions.reshape(N_TOK, TOK_DEV)[:, TOK_DEV - rim_rows:]
    anchor = prompt_first.reshape(N_TOK, TOK_DEV)[:, TOK_DEV - 1]
    in_prompt = spots >= anchor[:, None]
    conv_edges = jnp.where(in_prompt[:, :, None, None], joined, jnp.zeros_like(joined))
    return (mixed, segment_states, conv_edges)
```

```python
import functools

import jax
import jax.numpy as jnp
from jax import lax
from jax.experimental import pallas as pl
from jax.experimental.pallas import tpu as pltpu
from jax.sharding import PartitionSpec as P

MESH = pl.DeviceIdType.MESH
F32 = jnp.float32
BF16 = jnp.bfloat16
HIGHEST = lax.Precision.HIGHEST

HV = 4
GROUP = 8
PLANES = 8
ROWS = 64
SEG = 256
D = 2048
DK = 256
DV = 512
QKV = 2 * DK + DV
WIDE = QKV + DV
CHUNK = 512
PIECE = DK // GROUP


def dot(a, b):
    return jnp.dot(a, b, preferred_element_type=F32)


def dot_nt(a, b):
    return lax.dot_general(a, b, (((1,), (1,)), ((), ())), preferred_element_type=F32)


def dot_tn(a, b):
    return lax.dot_general(a, b, (((0,), (0,)), ((), ())), preferred_element_type=F32)


def across(a, copies):
    return jnp.concatenate([a] * copies, axis=1)


def kernel(
    tokens,
    lengths,
    wq,
    wk,
    wv,
    cq,
    ck,
    cv,
    wdown,
    wup,
    bias,
    wg,
    gain,
    wout,
    mixed,
    states,
    edges,
    xt,
    wall,
    wlow,
    wo,
    taps_q,
    taps_k,
    taps_v,
    up,
    bias_v,
    gain_v,
    lens,
    acc,
    accl,
    ext,
    halo,
    pf_col,
    pf_row,
    keep,
    cum,
    convk,
    convv,
    local,
    lifted,
    inner,
    gg,
    dsend,
    dgat,
    gsend,
    ggat,
    dmat,
    dt,
    l1s,
    l1r,
    p1,
    t2s,
    t2r,
    q2s,
    q2r,
    e1s,
    er,
    rs_s,
    relay,
    fl,
    fr,
    w_sem,
    loc_sem,
    tk_send,
    tk_recv,
    halo_sem,
    d_send,
    d_recv,
    g_send,
    g_recv,
    l1_send,
    l1_recv,
    t2_send,
    t2_recv,
    q2_send,
    q2_recv,
    e1_send,
    e1_recv,
    rs_send,
    relay_recv,
    fl_recv,
    fr_recv,
):
    tok = lax.axis_index("tok")
    y = lax.axis_index("hv")
    n_tok = GROUP * PLANES
    z = lax.div(tok, GROUP)
    g = lax.rem(tok, GROUP)
    right = lax.rem(y + 1, HV)
    left = lax.rem(y + HV - 1, HV)
    opp = lax.rem(y + 2, HV)
    after = lax.rem(tok + 1, n_tok)
    before = lax.rem(tok + n_tok - 1, n_tok)

    def remote(src, dst, ss, rs, to_tok, to_hv):
        return pltpu.make_async_remote_copy(
            src_ref=src, dst_ref=dst, send_sem=ss, recv_sem=rs, device_id=(to_tok, to_hv), device_id_type=MESH
        )

    def mate(k):
        return lax.rem(g + k, GROUP)

    def peer(k):
        return lax.rem(z + k, PLANES)

    own = pltpu.make_async_copy(tokens, xt.at[y], loc_sem.at[0])
    own.start()

    def weight_copies(c):
        rows = pl.ds(c * CHUNK, CHUNK)
        return [
            pltpu.make_async_copy(wq.at[rows], wall.at[rows, 0:DK], w_sem.at[c, 0]),
            pltpu.make_async_copy(wk.at[rows], wall.at[rows, DK : 2 * DK], w_sem.at[c, 1]),
            pltpu.make_async_copy(wv.at[rows], wall.at[rows, 2 * DK : QKV], w_sem.at[c, 2]),
            pltpu.make_async_copy(wg.at[rows], wall.at[rows, QKV:WIDE], w_sem.at[c, 3]),
        ]

    small = [
        pltpu.make_async_copy(src, dst, loc_sem.at[1 + i])
        for i, (src, dst) in enumerate(
            [
                (lengths, lens),
                (wdown, wlow),
                (wup, up),
                (bias, bias_v),
                (gain, gain_v),
                (cq, taps_q),
                (ck, taps_k),
                (cv, taps_v),
                (wout, wo),
            ]
        )
    ]

    barrier = pltpu.get_barrier_semaphore()
    pl.semaphore_signal(barrier, inc=1, device_id=(tok, right), device_id_type=MESH)
    pl.semaphore_signal(barrier, inc=1, device_id=(tok, left), device_id_type=MESH)
    pl.semaphore_signal(barrier, inc=1, device_id=(after, y), device_id_type=MESH)
    pl.semaphore_signal(barrier, inc=1, device_id=(before, y), device_id_type=MESH)
    for k in range(1, GROUP):
        pl.semaphore_signal(barrier, inc=1, device_id=(z * GROUP + mate(k), y), device_id_type=MESH)
    for k in range(1, PLANES):
        pl.semaphore_signal(barrier, inc=1, device_id=(peer(k) * GROUP + g, y), device_id_type=MESH)
    for copy in small[:2]:
        copy.start()
    for c in range(D // CHUNK):
        for copy in weight_copies(c):
            copy.start()
    for copy in small[2:]:
        copy.start()
    pl.semaphore_wait(barrier, 4 + GROUP - 1 + PLANES - 1)

    def cols(c):
        return pl.ds(pl.multiple_of(c * CHUNK, CHUNK), CHUNK)

    def own_to_right(s):
        return remote(
            tokens.at[:, cols(s)], xt.at[y, :, cols(s)], tk_send.at[0, s], tk_recv.at[0, s], tok, right
        )

    def own_to_left(s):
        c = lax.rem(s + 2, 4)
        return remote(
            tokens.at[:, cols(c)], xt.at[y, :, cols(c)], tk_send.at[1, s], tk_recv.at[1, s], tok, left
        )

    def from_left(s):
        part = xt.at[left, :, cols(s)]
        return remote(part, part, tk_send.at[0, s], tk_recv.at[0, s], tok, right)

    def from_right(s):
        part = xt.at[right, :, cols(lax.rem(s + 2, 4))]
        return remote(part, part, tk_send.at[1, s], tk_recv.at[1, s], tok, left)

    def on_to_right(f):
        part = xt.at[left, :, cols(f)]
        return remote(part, part, tk_send.at[0, 4 + f], tk_recv.at[0, 4 + f], tok, right)

    def on_to_left(f):
        part = xt.at[right, :, cols(f + 2)]
        return remote(part, part, tk_send.at[1, 4 + f], tk_recv.at[1, 4 + f], tok, left)

    def far_from_left(f):
        part = xt.at[opp, :, cols(f)]
        return remote(part, part, tk_send.at[0, 4 + f], tk_recv.at[0, 4 + f], tok, right)

    def far_from_right(f):
        part = xt.at[opp, :, cols(f + 2)]
        return remote(part, part, tk_send.at[1, 4 + f], tk_recv.at[1, 4 + f], tok, left)

    for s in range(4):
        own_to_right(s).start()
        own_to_left(s).start()

    acc[...] = jnp.zeros_like(acc)
    accl[...] = jnp.zeros_like(accl)

    for copy in small[:2]:
        copy.wait()
    first = tok * SEG
    pos_col = first + lax.broadcasted_iota(jnp.int32, (SEG, 128), 0)
    pos_row = first + lax.broadcasted_iota(jnp.int32, (8, SEG), 1)

    def mark(j, carried):
        offset, col, row = carried
        col = jnp.where(offset <= pos_col, offset, col)
        row = jnp.where(offset <= pos_row, offset, row)
        return offset + lens[j], col, row

    _, col, row = lax.fori_loop(
        0,
        lens.shape[0],
        mark,
        (jnp.int32(0), jnp.zeros((SEG, 128), jnp.int32), jnp.zeros((8, SEG), jnp.int32)),
    )
    pf_col[...] = col
    pf_row[...] = row
    for lag in range(1, 4):
        keep[lag - 1] = jnp.where(pos_col - lag >= col, 1.0, 0.0)

    def gemm(block, c):
        x = xt[block, :, cols(c)]
        for n in range(0, WIDE, CHUNK):
            acc[block, :, n : n + CHUNK] += dot(x, wall[cols(c), n : n + CHUNK])
        accl[block] += dot(x, wlow[cols(c), :])

    own.wait()

    def own_step(c, _):
        for copy in weight_copies(c):
            copy.wait()
        gemm(y, c)
        return 0

    lax.fori_loop(0, 4, own_step, 0)

    def near_step(s, _):
        from_left(s).wait_recv()
        on_to_right(s).start()
        from_right(s).wait_recv()
        on_to_left(s).start()
        gemm(left, s)
        gemm(right, s + 2)
        return 0

    lax.fori_loop(0, 2, near_step, 0)

    def near_step2(s, _):
        from_left(s).wait_recv()
        gemm(left, s)
        from_right(s).wait_recv()
        gemm(right, s - 2)
        return 0

    lax.fori_loop(2, 4, near_step2, 0)

    def far_step(f, _):
        far_from_left(f).wait_recv()
        gemm(opp, f)
        far_from_right(f).wait_recv()
        gemm(opp, f + 2)
        return 0

    lax.fori_loop(0, 2, far_step, 0)

    for b in (3, 0, 1, 2):
        ext[8 + b * ROWS : 8 + (b + 1) * ROWS, :] = acc[b, :, 0:QKV].astype(BF16).astype(F32)
        if b == 3:
            halo_copy = remote(
                ext.at[SEG : SEG + 8], halo, halo_sem.at[0], halo_sem.at[1], after, y
            )
            halo_copy.start()

    for copy in small[2:]:
        copy.wait()

    row_i = lax.broadcasted_iota(jnp.int32, (SEG, SEG), 0)
    col_i = lax.broadcasted_iota(jnp.int32, (SEG, SEG), 1)
    tri = jnp.where(row_i >= col_i, 1.0, 0.0).astype(F32)
    low = accl[...].reshape(SEG, accl.shape[2]).astype(BF16)
    v = dot(low, up[...]) + bias_v[...]
    decays = (jnp.minimum(v, 0.0) - jnp.log1p(jnp.exp(-jnp.abs(v)))) * (1.0 / 16.0)
    cum[...] = jnp.dot(tri, decays, precision=HIGHEST, preferred_element_type=F32)
    c_last = cum[SEG - 1 : SEG, :]
    pf_last = pf_col[SEG - 1 : SEG, :]
    whole = jnp.where(pf_last < first, 1.0, 0.0)
    dsend[...] = jnp.broadcast_to(jnp.exp(c_last) * across(whole, DK // 128), (8, DK))
    for k in range(1, GROUP):
        remote(dsend, dgat.at[g], d_send.at[k], d_recv.at[g], z * GROUP + mate(k), y).start()
    dgat[g] = dsend[...]

    def conv(r0, n, source, base, c0, width, taps, t0):
        tw = taps[:, t0 : t0 + width].astype(F32)
        total = tw[3:4] * source[base + r0 : base + r0 + n, c0 : c0 + width]
        for lag in range(1, 4):
            window = source[base + r0 - lag : base + r0 - lag + n, c0 : c0 + width]
            total += tw[3 - lag : 4 - lag] * window * across(keep[lag - 1, r0 : r0 + n, :], width // 128)
        half = 0.5 * total
        return (half * jnp.tanh(half) + half).astype(BF16)

    def conv_all(c0, width, taps, store):
        for r0 in [8, 16] + list(range(32, SEG, 32)):
            n = 8 if r0 == 8 else 16 if r0 == 16 else 32
            for t0 in range(0, width, 256):
                store(r0, n, t0, conv(r0, n, ext, 8, c0 + t0, 256, taps, t0))

    def conv_first(c0, width, taps, store):
        for t0 in range(0, width, 256):
            store(0, 8, t0, conv(0, 8, ext, 8, c0 + t0, 256, taps, t0))

    def store_k(r0, n, t0, value):
        convk[r0 : r0 + n, t0 : t0 + 256] = value.astype(F32)

    def store_v(r0, n, t0, value):
        convv[r0 : r0 + n, t0 : t0 + 256] = value.astype(F32)

    conv_all(DK, DK, taps_k, store_k)
    conv_all(2 * DK, DV, taps_v, store_v)

    remote(ext.at[SEG : SEG + 8], halo, halo_sem.at[0], halo_sem.at[1], after, y).wait_recv()
    ext[0:8, :] = halo[...]
    conv_first(DK, DK, taps_k, store_k)
    conv_first(2 * DK, DV, taps_v, store_v)

    tail = jnp.where(pf_col[...] == pf_last, 1.0, 0.0)
    weighted = (convk[...] * jnp.exp(c_last - cum[...]) * across(tail, DK // 128)).astype(BF16)
    local[...] = dot_tn(weighted, convv[...].astype(BF16))
    for j in range(GROUP):
        l1s[j] = local[j * PIECE : (j + 1) * PIECE, :].astype(BF16)
    for k in range(1, GROUP):
        j = mate(k)
        remote(l1s.at[j], l1r.at[g], l1_send.at[k], l1_recv.at[g], z * GROUP + j, y).start()
    l1r[g] = l1s[g]

    for k in range(1, GROUP):
        j = mate(k)
        remote(dsend, dgat.at[j], d_send.at[k], d_recv.at[j], z * GROUP + j, y).wait_recv()
    prod = dgat[0]
    for j in range(1, GROUP):
        prod = prod * dgat[j]
    gsend[...] = prod
    for k in range(1, PLANES):
        remote(gsend, ggat.at[z], g_send.at[k], g_recv.at[z], peer(k) * GROUP + g, y).start()
    ggat[z] = gsend[...]

    def store_q(r0, n, t0, value):
        inner[r0 : r0 + n, 0:DK] = value.astype(F32)

    conv_all(0, DK, taps_q, store_q)
    conv_first(0, DK, taps_q, store_q)

    for k in range(1, PLANES):
        j = peer(k)
        remote(gsend, ggat.at[j], g_send.at[k], g_recv.at[j], j * GROUP + g, y).wait_recv()
    sub = lax.broadcasted_iota(jnp.int32, (8, DK), 0)
    d8 = dgat[0]
    g8 = ggat[0]
    for j in range(1, 8):
        d8 = jnp.where(sub == j, dgat[j], d8)
        g8 = jnp.where(sub == j, ggat[j], g8)
    dmat[...] = jnp.zeros_like(dmat)
    dmat[0:8, :] = d8
    dmat[8:16, :] = g8
    dmat[16:24, :] = dsend[...]
    dt[...] = jnp.transpose(dmat[...])

    for k in range(1, GROUP):
        j = mate(k)
        remote(l1s.at[j], l1r.at[j], l1_send.at[k], l1_recv.at[j], z * GROUP + j, y).wait_recv()
    mine = dt[pl.ds(pl.multiple_of(g * PIECE, PIECE), PIECE), :]
    run = l1r[0].astype(F32)
    for j in range(1, GROUP):
        p1[j - 1] = run
        run = run * mine[:, j : j + 1] + l1r[j].astype(F32)
    total = run.astype(BF16)
    for k in range(PLANES):
        t2s[k] = total[16 * (k // 4) : 16 * (k // 4) + 16, 128 * (k % 4) : 128 * (k % 4) + 128]
    for k in range(1, PLANES):
        j = peer(k)
        remote(t2s.at[j], t2r.at[z], t2_send.at[k], t2_recv.at[z], j * GROUP + g, y).start()
    t2r[z] = t2s[z]

    for b in range(SEG // ROWS):
        r0, r1 = b * ROWS, (b + 1) * ROWS
        q = inner[r0:r1, 0:DK]
        if b == 0:
            start = jnp.zeros((1, DK), F32)
        else:
            start = cum[r0 - 1 : r0, :]
        up_q = q * jnp.exp(cum[r0:r1, :] - start)
        intact = jnp.where(pf_col[r0:r1, :] < first, 1.0, 0.0)
        lifted[b] = (up_q * jnp.exp(start) * across(intact, DK // 128)).astype(BF16)
        down_k = (convk[0:r1, :] * jnp.exp(start - cum[0:r1, :])).astype(BF16)
        scores = dot_nt(up_q.astype(BF16), down_k)
        ri = r0 + lax.broadcasted_iota(jnp.int32, (ROWS, r1), 0)
        ci = lax.broadcasted_iota(jnp.int32, (ROWS, r1), 1)
        same = pf_col[r0:r1, 0:1] == pf_row[0:1, 0:r1]
        scores = jnp.where((ri >= ci) & same, scores, 0.0).astype(BF16)
        inner[r0:r1, :] = dot(scores, convv[0:r1, :].astype(BF16))

    for k in range(1, PLANES):
        j = peer(k)
        remote(t2s.at[j], t2r.at[j], t2_send.at[k], t2_recv.at[j], j * GROUP + g, y).wait_recv()
    tile_rows = pl.ds(pl.multiple_of(g * PIECE + 16 * lax.div(z, 4), 16), 16)
    mine2 = dt[tile_rows, :]
    run2 = jnp.zeros((16, 128), F32)
    for j in range(PLANES):
        q2s[j] = run2.astype(BF16)
        run2 = run2 * mine2[:, 8 + j : 9 + j] + t2r[j].astype(F32)
    for k in range(1, PLANES):
        j = peer(k)
        remote(q2s.at[j], q2r.at[z], q2_send.at[k], q2_recv.at[z], j * GROUP + g, y).start()
    q2r[z] = q2s[z]

    for b in range(SEG // ROWS):
        gate = acc[b, :, QKV:WIDE].astype(BF16).astype(F32)
        half = 0.5 * gate
        gg[b] = (half * jnp.tanh(half) + half) * gain_v[...]

    for k in range(1, PLANES):
        j = peer(k)
        remote(q2s.at[j], q2r.at[j], q2_send.at[k], q2_recv.at[j], j * GROUP + g, y).wait_recv()
    entry = jnp.concatenate(
        [jnp.concatenate([q2r[4 * a + c].astype(F32) for c in range(4)], axis=1) for a in range(2)],
        axis=0,
    )
    e1s[0] = entry.astype(BF16)
    for j in range(1, GROUP):
        entry = entry * mine[:, j - 1 : j]
        e1s[j] = (p1[j - 1] + entry).astype(BF16)
    for k in range(1, GROUP):
        j = mate(k)
        remote(e1s.at[j], er.at[g], e1_send.at[k], e1_recv.at[g], z * GROUP + j, y).start()
    er[g] = e1s[g]
    for k in range(1, GROUP):
        j = mate(k)
        remote(e1s.at[j], er.at[j], e1_send.at[k], e1_recv.at[j], z * GROUP + j, y).wait_recv()

    def heads(block):
        rows = pl.ds(pl.multiple_of(block * ROWS, ROWS), ROWS)
        out = inner[rows, :] + dot(lifted[block], er[...].reshape(DK, DV))
        scale = lax.rsqrt(jnp.mean(out * out, axis=1, keepdims=True) + 1e-05)
        return (out * scale * gg[block]).astype(BF16)

    def project(gated, c):
        return dot(gated, wo[:, c * CHUNK : (c + 1) * CHUNK])

    def to_right(slot, dst, sem):
        return remote(rs_s.at[slot], dst, rs_send.at[slot], sem, tok, right)

    def to_left(slot, dst, sem):
        return remote(rs_s.at[slot], dst, rs_send.at[slot], sem, tok, left)

    gated = heads(opp)
    for c in (0, 2, 1, 3):
        rs_s[c] = project(gated, c).astype(BF16)
        (to_right if c < 2 else to_left)(c, relay.at[c], relay_recv.at[c]).start()
    gated_r = heads(right)
    gated_l = heads(left)
    for i in range(2):
        c = 2 + i
        rs_s[4 + c] = project(gated_r, c).astype(BF16)
        to_right(4 + c, fl.at[c], fl_recv.at[c]).start()
        c = i
        rs_s[4 + c] = project(gated_l, c).astype(BF16)
        to_left(4 + c, fr.at[c], fr_recv.at[c]).start()
    for i in range(2):
        c = i
        part = project(gated_r, c)
        to_right(c, relay.at[c], relay_recv.at[c]).wait_recv()
        rs_s[8 + c] = (part + relay[c].astype(F32)).astype(BF16)
        to_right(8 + c, fl.at[c], fl_recv.at[c]).start()
        c = 2 + i
        part = project(gated_l, c)
        to_left(c, relay.at[c], relay_recv.at[c]).wait_recv()
        rs_s[8 + c] = (part + relay[c].astype(F32)).astype(BF16)
        to_left(8 + c, fr.at[c], fr_recv.at[c]).start()

    states[...] = er[...].reshape(DK, DV).astype(F32) * dt[:, 16:17] + local[...]
    for j in range(3):
        r = SEG - 3 + j
        inside = jnp.where(first + r >= pf_last, 1.0, 0.0)
        edges[0, j] = (ext[8 + r : 9 + r, :] * across(inside, QKV // 128)).astype(BF16)

    gated = heads(y)
    for c in (2, 3, 0, 1):
        part = project(gated, c)
        to_right(0, fl.at[c], fl_recv.at[c]).wait_recv()
        to_right(0, fr.at[c], fr_recv.at[c]).wait_recv()
        mixed[:, c * CHUNK : (c + 1) * CHUNK] = (
            part + fl[c].astype(F32) + fr[c].astype(F32)
        ).astype(BF16)

    for s in range(4):
        own_to_right(s).wait_send()
        own_to_left(s).wait_send()
    for f in range(2):
        on_to_right(f).wait_send()
        on_to_left(f).wait_send()
    halo_copy.wait_send()
    for k in range(1, 8):
        remote(dsend, dgat.at[g], d_send.at[k], d_recv.at[g], tok, y).wait_send()
        remote(gsend, ggat.at[z], g_send.at[k], g_recv.at[z], tok, y).wait_send()
        remote(l1s.at[0], l1r.at[g], l1_send.at[k], l1_recv.at[g], tok, y).wait_send()
        remote(t2s.at[0], t2r.at[z], t2_send.at[k], t2_recv.at[z], tok, y).wait_send()
        remote(q2s.at[0], q2r.at[z], q2_send.at[k], q2_recv.at[z], tok, y).wait_send()
        remote(e1s.at[0], er.at[g], e1_send.at[k], e1_recv.at[g], tok, y).wait_send()
    for slot in range(12):
        to_right(slot, fl.at[0], fl_recv.at[0]).wait_send()


def shards(
    tokens,
    prompt_lengths,
    query_weight,
    key_weight,
    value_weight,
    query_conv,
    key_conv,
    value_conv,
    decay_down,
    decay_up,
    decay_bias,
    gate_weight,
    norm_gain,
    out_weight,
):
    rank = decay_down.shape[1]
    dma = pltpu.SemaphoreType.DMA
    anywhere = pl.BlockSpec(memory_space=pl.ANY)
    vmem = pl.BlockSpec(memory_space=pltpu.VMEM)
    mixed, states, edges = pl.pallas_call(
        kernel,
        out_shape=(
            jax.ShapeDtypeStruct((ROWS, D), BF16),
            jax.ShapeDtypeStruct((DK, DV), F32),
            jax.ShapeDtypeStruct((1, 3, 1, QKV), BF16),
        ),
        in_specs=[anywhere] * 14,
        out_specs=(vmem, vmem, vmem),
        scratch_shapes=[
            pltpu.VMEM((HV, ROWS, D), BF16),
            pltpu.VMEM((D, WIDE), BF16),
            pltpu.VMEM((D, rank), BF16),
            pltpu.VMEM((DV, D), BF16),
            pltpu.VMEM((4, DK), BF16),
            pltpu.VMEM((4, DK), BF16),
            pltpu.VMEM((4, DV), BF16),
            pltpu.VMEM((rank, DK), BF16),
            pltpu.VMEM((1, DK), F32),
            pltpu.VMEM((1, DV), F32),
            pltpu.SMEM(prompt_lengths.shape, jnp.int32),
            pltpu.VMEM((HV, ROWS, WIDE), F32),
            pltpu.VMEM((HV, ROWS, rank), F32),
            pltpu.VMEM((8 + SEG, QKV), F32),
            pltpu.VMEM((8, QKV), F32),
            pltpu.VMEM((SEG, 128), jnp.int32),
            pltpu.VMEM((8, SEG), jnp.int32),
            pltpu.VMEM((3, SEG, 128), F32),
            pltpu.VMEM((SEG, DK), F32),
            pltpu.VMEM((SEG, DK), F32),
            pltpu.VMEM((SEG, DV), F32),
            pltpu.VMEM((DK, DV), F32),
            pltpu.VMEM((HV, ROWS, DK), BF16),
            pltpu.VMEM((SEG, DV), F32),
            pltpu.VMEM((HV, ROWS, DV), F32),
            pltpu.VMEM((8, DK), F32),
            pltpu.VMEM((GROUP, 8, DK), F32),
            pltpu.VMEM((8, DK), F32),
            pltpu.VMEM((PLANES, 8, DK), F32),
            pltpu.VMEM((128, DK), F32),
            pltpu.VMEM((DK, 128), F32),
            pltpu.VMEM((GROUP, PIECE, DV), BF16),
            pltpu.VMEM((GROUP, PIECE, DV), BF16),
            pltpu.VMEM((GROUP - 1, PIECE, DV), F32),
            pltpu.VMEM((PLANES, 16, 128), BF16),
            pltpu.VMEM((PLANES, 16, 128), BF16),
            pltpu.VMEM((PLANES, 16, 128), BF16),
            pltpu.VMEM((PLANES, 16, 128), BF16),
            pltpu.VMEM((GROUP, PIECE, DV), BF16),
            pltpu.VMEM((GROUP, PIECE, DV), BF16),
            pltpu.VMEM((12, ROWS, CHUNK), BF16),
            pltpu.VMEM((4, ROWS, CHUNK), BF16),
            pltpu.VMEM((4, ROWS, CHUNK), BF16),
            pltpu.VMEM((4, ROWS, CHUNK), BF16),
            dma((4, 4)),
            dma((10,)),
            dma((2, 6)),
            dma((2, 6)),
            dma((2,)),
            dma((8,)),
            dma((8,)),
            dma((8,)),
            dma((8,)),
            dma((8,)),
            dma((8,)),
            dma((8,)),
            dma((8,)),
            dma((8,)),
            dma((8,)),
            dma((8,)),
            dma((8,)),
            dma((12,)),
            dma((4,)),
            dma((4,)),
            dma((4,)),
        ],
        compiler_params=pltpu.CompilerParams(
            collective_id=0, has_side_effects=True, vmem_limit_bytes=48 * 1024 * 1024
        ),
        name="gla",
    )(
        tokens,
        prompt_lengths,
        query_weight,
        key_weight,
        value_weight,
        query_conv,
        key_conv,
        value_conv,
        decay_down,
        decay_up,
        decay_bias.reshape(1, DK),
        gate_weight,
        norm_gain.reshape(1, DV),
        out_weight,
    )
    return mixed, states[None, None], edges


def solution(mesh):
    in_specs = (
        P(("tok", "hv"), None),
        P(),
        P(None, "hv"),
        P(None, "hv"),
        P(None, "hv"),
        P(None, "hv"),
        P(None, "hv"),
        P(None, "hv"),
        P(),
        P(None, "hv"),
        P("hv"),
        P(None, "hv"),
        P(),
        P("hv", None),
    )
    out_specs = (P(("tok", "hv"), None), P("tok", "hv", None, None), P("tok", None, "hv", None))
    return jax.shard_map(shards, mesh=mesh, in_specs=in_specs, out_specs=out_specs, check_vma=False)
```

```python
import functools

import jax
import jax.numpy as jnp
from jax import lax
from jax.experimental import pallas as pl
from jax.experimental.pallas import tpu as pltpu
from jax.sharding import PartitionSpec as P

MESH = pl.DeviceIdType.MESH
F32 = jnp.float32
BF16 = jnp.bfloat16
HIGHEST = lax.Precision.HIGHEST

HV = 4
GROUP = 8
PLANES = 8
ROWS = 64
SEG = 256
D = 2048
DK = 256
DV = 512
QKV = 2 * DK + DV
WIDE = QKV + DV
CHUNK = 512
HALF = DK // 2
XS = 4
CHIPS = XS * PLANES
OTHERS = sorted(
    [(dz, dx) for dz in range(PLANES) for dx in range(XS) if (dz, dx) != (0, 0)],
    key=lambda d: -(min(d[0], PLANES - d[0]) + min(d[1], XS - d[1])),
)


def dot(a, b):
    return jnp.dot(a, b, preferred_element_type=F32)


def dot_nt(a, b):
    return lax.dot_general(a, b, (((1,), (1,)), ((), ())), preferred_element_type=F32)


def dot_tn(a, b):
    return lax.dot_general(a, b, (((0,), (0,)), ((), ())), preferred_element_type=F32)


def across(a, copies):
    return jnp.concatenate([a] * copies, axis=1)


def kernel(
    tokens,
    lengths,
    wq,
    wk,
    wv,
    cq,
    ck,
    cv,
    wdown,
    wup,
    bias,
    wg,
    gain,
    wout,
    mixed,
    states,
    edges,
    xt,
    wall,
    wlow,
    wo,
    taps_q,
    taps_k,
    taps_v,
    up,
    bias_v,
    gain_v,
    lens,
    acc,
    accl,
    ext,
    halo,
    pf_col,
    pf_row,
    keep,
    cum,
    convk,
    convv,
    local,
    lifted,
    inner,
    gg,
    dsend,
    dgat,
    gsend,
    ggat,
    dmat,
    dts,
    dt,
    pair_s,
    pair_r,
    first_l,
    ts,
    tr,
    qs,
    qr,
    pe_s,
    er,
    rs_s,
    relay,
    fl,
    fr,
    w_sem,
    loc_sem,
    tk_send,
    tk_recv,
    halo_sem,
    d_send,
    d_recv,
    g_send,
    g_recv,
    pair_sem,
    t_send,
    t_recv,
    q_send,
    q_recv,
    pe_sem,
    rs_send,
    relay_recv,
    fl_recv,
    fr_recv,
):
    tok = lax.axis_index("tok")
    y = lax.axis_index("hv")
    n_tok = GROUP * PLANES
    z = lax.div(tok, GROUP)
    g = lax.rem(tok, GROUP)
    x = lax.div(g, 2)
    core = lax.rem(tok, 2)
    sib = tok + 1 - 2 * core
    right = lax.rem(y + 1, HV)
    left = lax.rem(y + HV - 1, HV)
    opp = lax.rem(y + 2, HV)
    after = lax.rem(tok + 1, n_tok)
    before = lax.rem(tok + n_tok - 1, n_tok)

    def remote(src, dst, ss, rs, to_tok, to_hv):
        return pltpu.make_async_remote_copy(
            src_ref=src, dst_ref=dst, send_sem=ss, recv_sem=rs, device_id=(to_tok, to_hv), device_id_type=MESH
        )

    def mate(k):
        return lax.rem(g + k, GROUP)

    def peer(k):
        return lax.rem(z + k, PLANES)

    def chip(d):
        other_z, other_x = lax.rem(z + d[0], PLANES), lax.rem(x + d[1], XS)
        return other_z * XS + other_x, other_z * GROUP + other_x * 2 + core

    own = pltpu.make_async_copy(tokens, xt.at[y], loc_sem.at[0])
    own.start()

    def weight_copies(c):
        rows = pl.ds(c * CHUNK, CHUNK)
        return [
            pltpu.make_async_copy(wq.at[rows], wall.at[rows, 0:DK], w_sem.at[c, 0]),
            pltpu.make_async_copy(wk.at[rows], wall.at[rows, DK : 2 * DK], w_sem.at[c, 1]),
            pltpu.make_async_copy(wv.at[rows], wall.at[rows, 2 * DK : QKV], w_sem.at[c, 2]),
            pltpu.make_async_copy(wg.at[rows], wall.at[rows, QKV:WIDE], w_sem.at[c, 3]),
        ]

    small = [
        pltpu.make_async_copy(src, dst, loc_sem.at[1 + i])
        for i, (src, dst) in enumerate(
            [
                (lengths, lens),
                (wdown, wlow),
                (wup, up),
                (bias, bias_v),
                (gain, gain_v),
                (cq, taps_q),
                (ck, taps_k),
                (cv, taps_v),
                (wout, wo),
            ]
        )
    ]

    barrier = pltpu.get_barrier_semaphore()
    pl.semaphore_signal(barrier, inc=1, device_id=(tok, right), device_id_type=MESH)
    pl.semaphore_signal(barrier, inc=1, device_id=(tok, left), device_id_type=MESH)
    pl.semaphore_signal(barrier, inc=1, device_id=(after, y), device_id_type=MESH)
    pl.semaphore_signal(barrier, inc=1, device_id=(before, y), device_id_type=MESH)
    for k in range(1, GROUP):
        pl.semaphore_signal(barrier, inc=1, device_id=(z * GROUP + mate(k), y), device_id_type=MESH)
    for d in OTHERS:
        pl.semaphore_signal(barrier, inc=1, device_id=(chip(d)[1], y), device_id_type=MESH)
    for copy in small[:2]:
        copy.start()
    for c in range(D // CHUNK):
        for copy in weight_copies(c):
            copy.start()
    for copy in small[2:]:
        copy.start()
    pl.semaphore_wait(barrier, 4 + GROUP - 1 + len(OTHERS))

    def cols(c):
        return pl.ds(pl.multiple_of(c * CHUNK, CHUNK), CHUNK)

    def own_to_right(s):
        return remote(
            tokens.at[:, cols(s)], xt.at[y, :, cols(s)], tk_send.at[0, s], tk_recv.at[0, s], tok, right
        )

    def own_to_left(s):
        c = lax.rem(s + 2, 4)
        return remote(
            tokens.at[:, cols(c)], xt.at[y, :, cols(c)], tk_send.at[1, s], tk_recv.at[1, s], tok, left
        )

    def from_left(s):
        part = xt.at[left, :, cols(s)]
        return remote(part, part, tk_send.at[0, s], tk_recv.at[0, s], tok, right)

    def from_right(s):
        part = xt.at[right, :, cols(lax.rem(s + 2, 4))]
        return remote(part, part, tk_send.at[1, s], tk_recv.at[1, s], tok, left)

    def on_to_right(f):
        part = xt.at[left, :, cols(f)]
        return remote(part, part, tk_send.at[0, 4 + f], tk_recv.at[0, 4 + f], tok, right)

    def on_to_left(f):
        part = xt.at[right, :, cols(f + 2)]
        return remote(part, part, tk_send.at[1, 4 + f], tk_recv.at[1, 4 + f], tok, left)

    def far_from_left(f):
        part = xt.at[opp, :, cols(f)]
        return remote(part, part, tk_send.at[0, 4 + f], tk_recv.at[0, 4 + f], tok, right)

    def far_from_right(f):
        part = xt.at[opp, :, cols(f + 2)]
        return remote(part, part, tk_send.at[1, 4 + f], tk_recv.at[1, 4 + f], tok, left)

    for s in range(4):
        own_to_right(s).start()
        own_to_left(s).start()

    acc[...] = jnp.zeros_like(acc)
    accl[...] = jnp.zeros_like(accl)

    for copy in small[:2]:
        copy.wait()
    first = tok * SEG
    pos_col = first + lax.broadcasted_iota(jnp.int32, (SEG, 128), 0)
    pos_row = first + lax.broadcasted_iota(jnp.int32, (8, SEG), 1)

    def mark(j, carried):
        offset, col, row = carried
        col = jnp.where(offset <= pos_col, offset, col)
        row = jnp.where(offset <= pos_row, offset, row)
        return offset + lens[j], col, row

    _, col, row = lax.fori_loop(
        0,
        lens.shape[0],
        mark,
        (jnp.int32(0), jnp.zeros((SEG, 128), jnp.int32), jnp.zeros((8, SEG), jnp.int32)),
    )
    pf_col[...] = col
    pf_row[...] = row
    for lag in range(1, 4):
        keep[lag - 1] = jnp.where(pos_col - lag >= col, 1.0, 0.0)

    def gemm(block, c):
        x = xt[block, :, cols(c)]
        for n in range(0, WIDE, CHUNK):
            acc[block, :, n : n + CHUNK] += dot(x, wall[cols(c), n : n + CHUNK])
        accl[block] += dot_nt(x, wlow[:, cols(c)])

    own.wait()

    def own_step(c, _):
        for copy in weight_copies(c):
            copy.wait()
        gemm(y, c)
        return 0

    lax.fori_loop(0, 4, own_step, 0)

    def near_step(s, _):
        from_left(s).wait_recv()
        on_to_right(s).start()
        from_right(s).wait_recv()
        on_to_left(s).start()
        gemm(left, s)
        gemm(right, s + 2)
        return 0

    lax.fori_loop(0, 2, near_step, 0)

    def near_step2(s, _):
        from_left(s).wait_recv()
        gemm(left, s)
        from_right(s).wait_recv()
        gemm(right, s - 2)
        return 0

    lax.fori_loop(2, 4, near_step2, 0)

    def far_step(f, _):
        far_from_left(f).wait_recv()
        gemm(opp, f)
        far_from_right(f).wait_recv()
        gemm(opp, f + 2)
        return 0

    lax.fori_loop(0, 2, far_step, 0)

    for b in (3, 0, 1, 2):
        ext[8 + b * ROWS : 8 + (b + 1) * ROWS, :] = acc[b, :, 0:QKV].astype(BF16).astype(F32)
        if b == 3:
            halo_copy = remote(
                ext.at[SEG : SEG + 8], halo, halo_sem.at[0], halo_sem.at[1], after, y
            )
            halo_copy.start()

    for copy in small[2:]:
        copy.wait()

    row_i = lax.broadcasted_iota(jnp.int32, (SEG, SEG), 0)
    col_i = lax.broadcasted_iota(jnp.int32, (SEG, SEG), 1)
    tri = jnp.where(row_i >= col_i, 1.0, 0.0).astype(F32)
    low = accl[...].reshape(SEG, accl.shape[2]).astype(BF16)
    v = dot(low, up[...]) + bias_v[...]
    decays = (jnp.minimum(v, 0.0) - jnp.log1p(jnp.exp(-jnp.abs(v)))) * (1.0 / 16.0)
    cum[...] = jnp.dot(tri, decays, precision=HIGHEST, preferred_element_type=F32)
    c_last = cum[SEG - 1 : SEG, :]
    pf_last = pf_col[SEG - 1 : SEG, :]
    whole = jnp.where(pf_last < first, 1.0, 0.0)
    dsend[...] = jnp.broadcast_to(jnp.exp(c_last) * across(whole, DK // 128), (8, DK))
    remote(dsend, dgat.at[g], d_send.at[0], d_recv.at[g], sib, y).start()
    for dx in (2, 1, 3):
        for dc in range(2):
            to = z * GROUP + lax.rem(x + dx, XS) * 2 + lax.rem(core + dc, 2)
            remote(dsend, dgat.at[g], d_send.at[2 * dx + dc], d_recv.at[g], to, y).start()
    dgat[g] = dsend[...]

    def conv(r0, n, source, base, c0, width, taps, t0):
        tw = taps[:, t0 : t0 + width].astype(F32)
        total = tw[3:4] * source[base + r0 : base + r0 + n, c0 : c0 + width]
        for lag in range(1, 4):
            window = source[base + r0 - lag : base + r0 - lag + n, c0 : c0 + width]
            total += tw[3 - lag : 4 - lag] * window * across(keep[lag - 1, r0 : r0 + n, :], width // 128)
        half = 0.5 * total
        return (half * jnp.tanh(half) + half).astype(BF16)

    def conv_all(c0, width, taps, store):
        for r0 in [8, 16] + list(range(32, SEG, 32)):
            n = 8 if r0 == 8 else 16 if r0 == 16 else 32
            for t0 in range(0, width, 256):
                store(r0, n, t0, conv(r0, n, ext, 8, c0 + t0, 256, taps, t0))

    def conv_first(c0, width, taps, store):
        for t0 in range(0, width, 256):
            store(0, 8, t0, conv(0, 8, ext, 8, c0 + t0, 256, taps, t0))

    def store_k(r0, n, t0, value):
        convk[r0 : r0 + n, t0 : t0 + 256] = value.astype(F32)

    def store_v(r0, n, t0, value):
        convv[r0 : r0 + n, t0 : t0 + 256] = value.astype(F32)

    conv_all(DK, DK, taps_k, store_k)
    conv_all(2 * DK, DV, taps_v, store_v)

    remote(ext.at[SEG : SEG + 8], halo, halo_sem.at[0], halo_sem.at[1], after, y).wait_recv()
    ext[0:8, :] = halo[...]
    conv_first(DK, DK, taps_k, store_k)
    conv_first(2 * DK, DV, taps_v, store_v)

    tail = jnp.where(pf_col[...] == pf_last, 1.0, 0.0)
    weighted = (convk[...] * jnp.exp(c_last - cum[...]) * across(tail, DK // 128)).astype(BF16)
    local[...] = dot_tn(weighted, convv[...].astype(BF16))

    def half_rows(which):
        return pl.ds(pl.multiple_of(which * HALF, HALF), HALF)

    pair_s[...] = local[half_rows(1 - core), :].astype(BF16)
    to_sib = remote(pair_s, pair_r, pair_sem.at[0], pair_sem.at[1], sib, y)
    to_sib.start()
    sib_g = g + 1 - 2 * core
    remote(dsend, dgat.at[sib_g], d_send.at[0], d_recv.at[sib_g], sib, y).wait_recv()
    dmat[0:8, :] = dsend[...]
    dmat[8:16, :] = dgat[sib_g]
    dts[...] = jnp.transpose(dmat[...])
    mine_d = dts[half_rows(core), :]
    own_d, sib_d = mine_d[:, 0:1], mine_d[:, 8:9]
    is_first = core == 0
    d_first = jnp.where(is_first, own_d, sib_d)
    d_second = jnp.where(is_first, sib_d, own_d)
    to_sib.wait_recv()
    own_l = local[half_rows(core), :]
    sib_l = pair_r[...].astype(F32)
    l_first = jnp.where(is_first, own_l, sib_l)
    first_l[...] = l_first
    chip_l = (l_first * d_second + jnp.where(is_first, sib_l, own_l)).astype(BF16)
    for k in range(CHIPS):
        ts[k] = chip_l[16 * (k // XS) : 16 * (k // XS) + 16, 128 * (k % XS) : 128 * (k % XS) + 128]
    me = z * XS + x

    def to_chip(i, d, src, dst, ss, rs):
        k, device = chip(d)
        return remote(src.at[k], dst.at[me], ss.at[i], rs.at[me], device, y)

    def from_chip(d, dst, ss, rs):
        k, device = chip(d)
        return remote(dst.at[k], dst.at[k], ss.at[0], rs.at[k], device, y)

    for i, d in enumerate(OTHERS):
        to_chip(i, d, ts, tr, t_send, t_recv).start()
    tr[me] = ts[me]

    for dx in (1, 3, 2):
        for dc in range(2):
            j = lax.rem(x + dx, XS) * 2 + lax.rem(core + dc, 2)
            remote(dsend, dgat.at[j], d_send.at[0], d_recv.at[j], z * GROUP + j, y).wait_recv()

    sub = lax.broadcasted_iota(jnp.int32, (8, HALF), 0)
    chips_d = jnp.zeros((8, HALF), F32)
    for j in range(XS):
        both = dgat[2 * j] * dgat[2 * j + 1]
        chips_d = jnp.where(sub == j, jnp.where(is_first, both[:, 0:HALF], both[:, HALF:DK]), chips_d)
    gsend[...] = chips_d
    for k in (4, 3, 5, 2, 6, 1, 7):
        remote(gsend, ggat.at[z], g_send.at[k], g_recv.at[z], peer(k) * GROUP + g, y).start()
    ggat[z] = gsend[...]

    def store_q(r0, n, t0, value):
        inner[r0 : r0 + n, 0:DK] = value.astype(F32)

    conv_all(0, DK, taps_q, store_q)
    conv_first(0, DK, taps_q, store_q)

    for b in range(SEG // ROWS):
        r0, r1 = b * ROWS, (b + 1) * ROWS
        q = inner[r0:r1, 0:DK]
        if b == 0:
            start = jnp.zeros((1, DK), F32)
        else:
            start = cum[r0 - 1 : r0, :]
        up_q = q * jnp.exp(cum[r0:r1, :] - start)
        intact = jnp.where(pf_col[r0:r1, :] < first, 1.0, 0.0)
        reach = (up_q * jnp.exp(start) * across(intact, DK // 128)).astype(BF16)
        lifted[0, b] = reach[:, 0:HALF]
        lifted[1, b] = reach[:, HALF:DK]
        down_k = (convk[0:r1, :] * jnp.exp(start - cum[0:r1, :])).astype(BF16)
        scores = dot_nt(up_q.astype(BF16), down_k)
        ri = r0 + lax.broadcasted_iota(jnp.int32, (ROWS, r1), 0)
        ci = lax.broadcasted_iota(jnp.int32, (ROWS, r1), 1)
        same = pf_col[r0:r1, 0:1] == pf_row[0:1, 0:r1]
        scores = jnp.where((ri >= ci) & same, scores, 0.0).astype(BF16)
        inner[r0:r1, :] = dot(scores, convv[0:r1, :].astype(BF16))

    for k in range(1, PLANES):
        j = peer(k)
        remote(gsend, ggat.at[j], g_send.at[k], g_recv.at[j], j * GROUP + g, y).wait_recv()
    padded = jnp.concatenate([ggat[...].reshape(8 * PLANES, HALF), jnp.zeros((64, HALF), F32)], axis=0)
    dt[...] = jnp.transpose(padded)

    for d in OTHERS:
        from_chip(d, tr, t_send, t_recv).wait_recv()
    tile_d = dt[pl.ds(pl.multiple_of(16 * z, 16), 16), :]
    run = jnp.zeros((16, 128), F32)
    for k in range(CHIPS):
        qs[k] = run.astype(BF16)
        lane = 8 * (k // XS) + k % XS
        run = run * tile_d[:, lane : lane + 1] + tr[k].astype(F32)
    for i, d in enumerate(OTHERS):
        to_chip(i, d, qs, qr, q_send, q_recv).start()
    qr[me] = qs[me]

    for b in range(SEG // ROWS):
        gate = acc[b, :, QKV:WIDE].astype(BF16).astype(F32)
        half = 0.5 * gate
        gg[b] = (half * jnp.tanh(half) + half) * gain_v[...]

    for d in OTHERS:
        from_chip(d, qr, q_send, q_recv).wait_recv()
    at_first = jnp.concatenate(
        [jnp.concatenate([qr[XS * a + b].astype(F32) for b in range(XS)], axis=1) for a in range(PLANES)],
        axis=0,
    )
    at_second = at_first * d_first + first_l[...]
    pe_s[...] = jnp.where(is_first, at_second, at_first).astype(BF16)
    sib_e = remote(pe_s, er.at[core], pe_sem.at[0], pe_sem.at[1], sib, y)
    sib_e.start()
    er[core] = jnp.where(is_first, at_first, at_second).astype(BF16)
    for b in range(SEG // ROWS):
        inner[b * ROWS : (b + 1) * ROWS, :] += dot(lifted[core, b], er[core])
    remote(pe_s, er.at[1 - core], pe_sem.at[0], pe_sem.at[1], sib, y).wait_recv()

    def heads(block):
        rows = pl.ds(pl.multiple_of(block * ROWS, ROWS), ROWS)
        out = inner[rows, :] + dot(lifted[1 - core, block], er[1 - core])
        scale = lax.rsqrt(jnp.mean(out * out, axis=1, keepdims=True) + 1e-05)
        return (out * scale * gg[block]).astype(BF16)

    def project(gated, c):
        return dot(gated, wo[:, c * CHUNK : (c + 1) * CHUNK])

    def to_right(slot, dst, sem):
        return remote(rs_s.at[slot], dst, rs_send.at[slot], sem, tok, right)

    def to_left(slot, dst, sem):
        return remote(rs_s.at[slot], dst, rs_send.at[slot], sem, tok, left)

    gated = heads(opp)
    for c in (0, 2, 1, 3):
        rs_s[c] = project(gated, c).astype(BF16)
        (to_right if c < 2 else to_left)(c, relay.at[c], relay_recv.at[c]).start()
    gated_r = heads(right)
    gated_l = heads(left)
    for i in range(2):
        c = 2 + i
        rs_s[4 + c] = project(gated_r, c).astype(BF16)
        to_right(4 + c, fl.at[c], fl_recv.at[c]).start()
        c = i
        rs_s[4 + c] = project(gated_l, c).astype(BF16)
        to_left(4 + c, fr.at[c], fr_recv.at[c]).start()
    for i in range(2):
        c = i
        part = project(gated_r, c)
        to_right(c, relay.at[c], relay_recv.at[c]).wait_recv()
        rs_s[8 + c] = (part + relay[c].astype(F32)).astype(BF16)
        to_right(8 + c, fl.at[c], fl_recv.at[c]).start()
        c = 2 + i
        part = project(gated_l, c)
        to_left(c, relay.at[c], relay_recv.at[c]).wait_recv()
        rs_s[8 + c] = (part + relay[c].astype(F32)).astype(BF16)
        to_left(8 + c, fr.at[c], fr_recv.at[c]).start()

    states[...] = er[...].reshape(DK, DV).astype(F32) * dts[:, 0:1] + local[...]
    for j in range(3):
        r = SEG - 3 + j
        inside = jnp.where(first + r >= pf_last, 1.0, 0.0)
        edges[0, 0, j : j + 1, :] = (ext[8 + r : 9 + r, :] * across(inside, QKV // 128)).astype(BF16)

    gated = heads(y)
    for c in (2, 3, 0, 1):
        part = project(gated, c)
        to_right(0, fl.at[c], fl_recv.at[c]).wait_recv()
        to_right(0, fr.at[c], fr_recv.at[c]).wait_recv()
        mixed[:, c * CHUNK : (c + 1) * CHUNK] = (
            part + fl[c].astype(F32) + fr[c].astype(F32)
        ).astype(BF16)

    for s in range(4):
        own_to_right(s).wait_send()
        own_to_left(s).wait_send()
    for f in range(2):
        on_to_right(f).wait_send()
        on_to_left(f).wait_send()
    halo_copy.wait_send()
    for k in [0] + list(range(2, 8)):
        remote(dsend, dgat.at[g], d_send.at[k], d_recv.at[g], sib, y).wait_send()
    for k in range(1, PLANES):
        remote(gsend, ggat.at[z], g_send.at[k], g_recv.at[z], sib, y).wait_send()
    to_sib.wait_send()
    sib_e.wait_send()
    for i, d in enumerate(OTHERS):
        to_chip(i, d, ts, tr, t_send, t_recv).wait_send()
        to_chip(i, d, qs, qr, q_send, q_recv).wait_send()
    for slot in range(12):
        to_right(slot, fl.at[0], fl_recv.at[0]).wait_send()


def write_out(mixed, states, edges, mixed_out, states_out, edges_out, sem):
    copies = [
        pltpu.make_async_copy(src, dst, sem.at[i])
        for i, (src, dst) in enumerate([(states, states_out), (mixed, mixed_out), (edges, edges_out)])
    ]
    for copy in copies:
        copy.start()
    for copy in copies:
        copy.wait()


def shards(
    tokens,
    prompt_lengths,
    query_weight,
    key_weight,
    value_weight,
    query_conv,
    key_conv,
    value_conv,
    decay_down,
    decay_up,
    decay_bias,
    gate_weight,
    norm_gain,
    out_weight,
):
    rank = decay_down.shape[1]
    dma = pltpu.SemaphoreType.DMA
    anywhere = pl.BlockSpec(memory_space=pl.ANY)
    vmem = pl.BlockSpec(memory_space=pltpu.VMEM)
    mixed, states, edges = pl.pallas_call(
        kernel,
        out_shape=(
            jax.ShapeDtypeStruct((ROWS, D), BF16),
            jax.ShapeDtypeStruct((DK, DV), F32),
            jax.ShapeDtypeStruct((1, 1, 3, QKV), BF16),
        ),
        in_specs=[anywhere] * 14,
        out_specs=(vmem, vmem, vmem),
        scratch_shapes=[
            pltpu.VMEM((HV, ROWS, D), BF16),
            pltpu.VMEM((D, WIDE), BF16),
            pltpu.VMEM((rank, D), BF16),
            pltpu.VMEM((DV, D), BF16),
            pltpu.VMEM((4, DK), BF16),
            pltpu.VMEM((4, DK), BF16),
            pltpu.VMEM((4, DV), BF16),
            pltpu.VMEM((rank, DK), BF16),
            pltpu.VMEM((1, DK), F32),
            pltpu.VMEM((1, DV), F32),
            pltpu.SMEM(prompt_lengths.shape, jnp.int32),
            pltpu.VMEM((HV, ROWS, WIDE), F32),
            pltpu.VMEM((HV, ROWS, rank), F32),
            pltpu.VMEM((8 + SEG, QKV), F32),
            pltpu.VMEM((8, QKV), F32),
            pltpu.VMEM((SEG, 128), jnp.int32),
            pltpu.VMEM((8, SEG), jnp.int32),
            pltpu.VMEM((3, SEG, 128), F32),
            pltpu.VMEM((SEG, DK), F32),
            pltpu.VMEM((SEG, DK), F32),
            pltpu.VMEM((SEG, DV), F32),
            pltpu.VMEM((DK, DV), F32),
            pltpu.VMEM((2, HV, ROWS, HALF), BF16),
            pltpu.VMEM((SEG, DV), F32),
            pltpu.VMEM((HV, ROWS, DV), F32),
            pltpu.VMEM((8, DK), F32),
            pltpu.VMEM((GROUP, 8, DK), F32),
            pltpu.VMEM((8, HALF), F32),
            pltpu.VMEM((PLANES, 8, HALF), F32),
            pltpu.VMEM((128, DK), F32),
            pltpu.VMEM((DK, 128), F32),
            pltpu.VMEM((HALF, 128), F32),
            pltpu.VMEM((HALF, DV), BF16),
            pltpu.VMEM((HALF, DV), BF16),
            pltpu.VMEM((HALF, DV), F32),
            pltpu.VMEM((CHIPS, 16, 128), BF16),
            pltpu.VMEM((CHIPS, 16, 128), BF16),
            pltpu.VMEM((CHIPS, 16, 128), BF16),
            pltpu.VMEM((CHIPS, 16, 128), BF16),
            pltpu.VMEM((HALF, DV), BF16),
            pltpu.VMEM((2, HALF, DV), BF16),
            pltpu.VMEM((12, ROWS, CHUNK), BF16),
            pltpu.VMEM((4, ROWS, CHUNK), BF16),
            pltpu.VMEM((4, ROWS, CHUNK), BF16),
            pltpu.VMEM((4, ROWS, CHUNK), BF16),
            dma((4, 4)),
            dma((10,)),
            dma((2, 6)),
            dma((2, 6)),
            dma((2,)),
            dma((8,)),
            dma((8,)),
            dma((8,)),
            dma((8,)),
            dma((2,)),
            dma((CHIPS,)),
            dma((CHIPS,)),
            dma((CHIPS,)),
            dma((CHIPS,)),
            dma((2,)),
            dma((12,)),
            dma((4,)),
            dma((4,)),
            dma((4,)),
        ],
        compiler_params=pltpu.CompilerParams(
            collective_id=0, has_side_effects=True, vmem_limit_bytes=63 * 1024 * 1024
        ),
        name="gla",
    )(
        tokens,
        prompt_lengths,
        query_weight,
        key_weight,
        value_weight,
        query_conv,
        key_conv,
        value_conv,
        decay_down.T,
        decay_up,
        decay_bias.reshape(1, DK),
        gate_weight,
        norm_gain.reshape(1, DV),
        out_weight,
    )
    parts = (mixed, states, edges)
    mixed, states, edges = pl.pallas_call(
        write_out,
        out_shape=tuple(jax.ShapeDtypeStruct(a.shape, a.dtype) for a in parts),
        in_specs=[anywhere] * 3,
        out_specs=(anywhere,) * 3,
        scratch_shapes=[dma((3,))],
        name="write_out",
    )(*parts)
    return mixed, states[None, None], edges.transpose(0, 2, 1, 3)


def solution(mesh):
    in_specs = (
        P(("tok", "hv"), None),
        P(),
        P(None, "hv"),
        P(None, "hv"),
        P(None, "hv"),
        P(None, "hv"),
        P(None, "hv"),
        P(None, "hv"),
        P(),
        P(None, "hv"),
        P("hv"),
        P(None, "hv"),
        P(),
        P("hv", None),
    )
    out_specs = (P(("tok", "hv"), None), P("tok", "hv", None, None), P("tok", None, "hv", None))
    return jax.shard_map(shards, mesh=mesh, in_specs=in_specs, out_specs=out_specs, check_vma=False)
```

```python
import functools

import jax
import jax.numpy as jnp
from jax import lax
from jax.experimental import pallas as pl
from jax.experimental.pallas import tpu as pltpu
from jax.sharding import PartitionSpec as P

MESH = pl.DeviceIdType.MESH
F32 = jnp.float32
BF16 = jnp.bfloat16
HIGHEST = lax.Precision.HIGHEST

HV = 4
GROUP = 8
PLANES = 8
ROWS = 64
SEG = 256
D = 2048
DK = 256
DV = 512
QKV = 2 * DK + DV
WIDE = QKV + DV
CHUNK = 512
HALF = DK // 2
XS = 4
CHIPS = XS * PLANES
OTHERS = sorted(
    [(dz, dx) for dz in range(PLANES) for dx in range(XS) if (dz, dx) != (0, 0)],
    key=lambda d: -(min(d[0], PLANES - d[0]) + min(d[1], XS - d[1])),
)


def dot(a, b):
    return jnp.dot(a, b, preferred_element_type=F32)


def dot_nt(a, b):
    return lax.dot_general(a, b, (((1,), (1,)), ((), ())), preferred_element_type=F32)


def dot_tn(a, b):
    return lax.dot_general(a, b, (((0,), (0,)), ((), ())), preferred_element_type=F32)


def across(a, copies):
    return jnp.concatenate([a] * copies, axis=1)


def kernel(
    tokens,
    lengths,
    wq,
    wk,
    wv,
    cq,
    ck,
    cv,
    wdown,
    wup,
    bias,
    wg,
    gain,
    wout,
    mixed_out,
    states_out,
    edges_out,
    mixed,
    states,
    edges,
    xt,
    wall,
    wlow,
    wo,
    taps_q,
    taps_k,
    taps_v,
    up,
    bias_v,
    gain_v,
    lens,
    acc,
    accl,
    ext,
    halo,
    pf_col,
    pf_row,
    keep,
    cum,
    convk,
    convv,
    local,
    lifted,
    inner,
    gg,
    dsend,
    dgat,
    gsend,
    ggat,
    dmat,
    dts,
    dt,
    pair_s,
    pair_r,
    first_l,
    ts,
    tr,
    qs,
    qr,
    pe_s,
    er,
    rs_s,
    relay,
    fl,
    fr,
    w_sem,
    loc_sem,
    tk_send,
    tk_recv,
    halo_sem,
    d_send,
    d_recv,
    g_send,
    g_recv,
    pair_sem,
    t_send,
    t_recv,
    q_send,
    q_recv,
    pe_sem,
    rs_send,
    relay_recv,
    fl_recv,
    fr_recv,
    out_sem,
):
    tok = lax.axis_index("tok")
    y = lax.axis_index("hv")
    n_tok = GROUP * PLANES
    z = lax.div(tok, GROUP)
    g = lax.rem(tok, GROUP)
    x = lax.div(g, 2)
    core = lax.rem(tok, 2)
    sib = tok + 1 - 2 * core
    right = lax.rem(y + 1, HV)
    left = lax.rem(y + HV - 1, HV)
    opp = lax.rem(y + 2, HV)
    after = lax.rem(tok + 1, n_tok)
    before = lax.rem(tok + n_tok - 1, n_tok)

    def remote(src, dst, ss, rs, to_tok, to_hv):
        return pltpu.make_async_remote_copy(
            src_ref=src, dst_ref=dst, send_sem=ss, recv_sem=rs, device_id=(to_tok, to_hv), device_id_type=MESH
        )

    def mate(k):
        return lax.rem(g + k, GROUP)

    def peer(k):
        return lax.rem(z + k, PLANES)

    def chip(d):
        other_z, other_x = lax.rem(z + d[0], PLANES), lax.rem(x + d[1], XS)
        return other_z * XS + other_x, other_z * GROUP + other_x * 2 + core

    own = pltpu.make_async_copy(tokens, xt.at[y], loc_sem.at[0])
    own.start()

    def weight_copies(c):
        rows = pl.ds(c * CHUNK, CHUNK)
        return [
            pltpu.make_async_copy(wq.at[rows], wall.at[rows, 0:DK], w_sem.at[c, 0]),
            pltpu.make_async_copy(wk.at[rows], wall.at[rows, DK : 2 * DK], w_sem.at[c, 1]),
            pltpu.make_async_copy(wv.at[rows], wall.at[rows, 2 * DK : QKV], w_sem.at[c, 2]),
            pltpu.make_async_copy(wg.at[rows], wall.at[rows, QKV:WIDE], w_sem.at[c, 3]),
        ]

    small = [
        pltpu.make_async_copy(src, dst, loc_sem.at[1 + i])
        for i, (src, dst) in enumerate(
            [
                (lengths, lens),
                (wdown, wlow),
                (wup, up),
                (bias, bias_v),
                (gain, gain_v),
                (cq, taps_q),
                (ck, taps_k),
                (cv, taps_v),
                (wout, wo),
            ]
        )
    ]

    barrier = pltpu.get_barrier_semaphore()
    pl.semaphore_signal(barrier, inc=1, device_id=(tok, right), device_id_type=MESH)
    pl.semaphore_signal(barrier, inc=1, device_id=(tok, left), device_id_type=MESH)
    pl.semaphore_signal(barrier, inc=1, device_id=(after, y), device_id_type=MESH)
    pl.semaphore_signal(barrier, inc=1, device_id=(before, y), device_id_type=MESH)
    for k in range(1, GROUP):
        pl.semaphore_signal(barrier, inc=1, device_id=(z * GROUP + mate(k), y), device_id_type=MESH)
    for d in OTHERS:
        pl.semaphore_signal(barrier, inc=1, device_id=(chip(d)[1], y), device_id_type=MESH)
    for copy in small[:2]:
        copy.start()
    for c in range(D // CHUNK):
        for copy in weight_copies(c):
            copy.start()
    for copy in small[2:]:
        copy.start()
    pl.semaphore_wait(barrier, 4 + GROUP - 1 + len(OTHERS))

    def cols(c):
        return pl.ds(pl.multiple_of(c * CHUNK, CHUNK), CHUNK)

    def own_to_right(s):
        return remote(
            tokens.at[:, cols(s)], xt.at[y, :, cols(s)], tk_send.at[0, s], tk_recv.at[0, s], tok, right
        )

    def own_to_left(s):
        c = lax.rem(s + 2, 4)
        return remote(
            tokens.at[:, cols(c)], xt.at[y, :, cols(c)], tk_send.at[1, s], tk_recv.at[1, s], tok, left
        )

    def from_left(s):
        part = xt.at[left, :, cols(s)]
        return remote(part, part, tk_send.at[0, s], tk_recv.at[0, s], tok, right)

    def from_right(s):
        part = xt.at[right, :, cols(lax.rem(s + 2, 4))]
        return remote(part, part, tk_send.at[1, s], tk_recv.at[1, s], tok, left)

    def on_to_right(f):
        part = xt.at[left, :, cols(f)]
        return remote(part, part, tk_send.at[0, 4 + f], tk_recv.at[0, 4 + f], tok, right)

    def on_to_left(f):
        part = xt.at[right, :, cols(f + 2)]
        return remote(part, part, tk_send.at[1, 4 + f], tk_recv.at[1, 4 + f], tok, left)

    def far_from_left(f):
        part = xt.at[opp, :, cols(f)]
        return remote(part, part, tk_send.at[0, 4 + f], tk_recv.at[0, 4 + f], tok, right)

    def far_from_right(f):
        part = xt.at[opp, :, cols(f + 2)]
        return remote(part, part, tk_send.at[1, 4 + f], tk_recv.at[1, 4 + f], tok, left)

    for s in range(4):
        own_to_right(s).start()
        own_to_left(s).start()

    acc[...] = jnp.zeros_like(acc)
    accl[...] = jnp.zeros_like(accl)

    for copy in small[:2]:
        copy.wait()
    first = tok * SEG
    pos_col = first + lax.broadcasted_iota(jnp.int32, (SEG, 128), 0)
    pos_row = first + lax.broadcasted_iota(jnp.int32, (8, SEG), 1)

    def mark(j, carried):
        offset, col, row = carried
        col = jnp.where(offset <= pos_col, offset, col)
        row = jnp.where(offset <= pos_row, offset, row)
        return offset + lens[j], col, row

    _, col, row = lax.fori_loop(
        0,
        lens.shape[0],
        mark,
        (jnp.int32(0), jnp.zeros((SEG, 128), jnp.int32), jnp.zeros((8, SEG), jnp.int32)),
    )
    pf_col[...] = col
    pf_row[...] = row
    for lag in range(1, 4):
        keep[lag - 1] = jnp.where(pos_col - lag >= col, 1.0, 0.0)

    def gemm(block, c):
        x = xt[block, :, cols(c)]
        for n in range(0, WIDE, CHUNK):
            acc[block, :, n : n + CHUNK] += dot(x, wall[cols(c), n : n + CHUNK])
        accl[block] += dot_nt(x, wlow[:, cols(c)])

    own.wait()

    def own_step(c, _):
        for copy in weight_copies(c):
            copy.wait()
        gemm(y, c)
        return 0

    lax.fori_loop(0, 4, own_step, 0)

    def near_step(s, _):
        from_left(s).wait_recv()
        on_to_right(s).start()
        from_right(s).wait_recv()
        on_to_left(s).start()
        gemm(left, s)
        gemm(right, s + 2)
        return 0

    lax.fori_loop(0, 2, near_step, 0)

    def near_step2(s, _):
        from_left(s).wait_recv()
        gemm(left, s)
        from_right(s).wait_recv()
        gemm(right, s - 2)
        return 0

    lax.fori_loop(2, 4, near_step2, 0)

    def far_step(f, _):
        far_from_left(f).wait_recv()
        gemm(opp, f)
        far_from_right(f).wait_recv()
        gemm(opp, f + 2)
        return 0

    lax.fori_loop(0, 2, far_step, 0)

    for b in (3, 0, 1, 2):
        ext[8 + b * ROWS : 8 + (b + 1) * ROWS, :] = acc[b, :, 0:QKV].astype(BF16).astype(F32)
        if b == 3:
            halo_copy = remote(
                ext.at[SEG : SEG + 8], halo, halo_sem.at[0], halo_sem.at[1], after, y
            )
            halo_copy.start()

    for copy in small[2:]:
        copy.wait()

    row_i = lax.broadcasted_iota(jnp.int32, (SEG, SEG), 0)
    col_i = lax.broadcasted_iota(jnp.int32, (SEG, SEG), 1)
    tri = jnp.where(row_i >= col_i, 1.0, 0.0).astype(F32)
    low = accl[...].reshape(SEG, accl.shape[2]).astype(BF16)
    v = dot(low, up[...]) + bias_v[...]
    decays = (jnp.minimum(v, 0.0) - jnp.log1p(jnp.exp(-jnp.abs(v)))) * (1.0 / 16.0)
    cum[...] = jnp.dot(tri, decays, precision=HIGHEST, preferred_element_type=F32)
    c_last = cum[SEG - 1 : SEG, :]
    pf_last = pf_col[SEG - 1 : SEG, :]
    whole = jnp.where(pf_last < first, 1.0, 0.0)
    dsend[...] = jnp.broadcast_to(jnp.exp(c_last) * across(whole, DK // 128), (8, DK))
    remote(dsend, dgat.at[g], d_send.at[0], d_recv.at[g], sib, y).start()
    for dx in (2, 1, 3):
        for dc in range(2):
            to = z * GROUP + lax.rem(x + dx, XS) * 2 + lax.rem(core + dc, 2)
            remote(dsend, dgat.at[g], d_send.at[2 * dx + dc], d_recv.at[g], to, y).start()
    dgat[g] = dsend[...]

    def conv(r0, n, source, base, c0, width, taps, t0):
        tw = taps[:, t0 : t0 + width].astype(F32)
        total = tw[3:4] * source[base + r0 : base + r0 + n, c0 : c0 + width]
        for lag in range(1, 4):
            window = source[base + r0 - lag : base + r0 - lag + n, c0 : c0 + width]
            total += tw[3 - lag : 4 - lag] * window * across(keep[lag - 1, r0 : r0 + n, :], width // 128)
        half = 0.5 * total
        return (half * jnp.tanh(half) + half).astype(BF16)

    def conv_all(c0, width, taps, store):
        for r0 in [8, 16] + list(range(32, SEG, 32)):
            n = 8 if r0 == 8 else 16 if r0 == 16 else 32
            for t0 in range(0, width, 256):
                store(r0, n, t0, conv(r0, n, ext, 8, c0 + t0, 256, taps, t0))

    def conv_first(c0, width, taps, store):
        for t0 in range(0, width, 256):
            store(0, 8, t0, conv(0, 8, ext, 8, c0 + t0, 256, taps, t0))

    def store_k(r0, n, t0, value):
        convk[r0 : r0 + n, t0 : t0 + 256] = value.astype(F32)

    def store_v(r0, n, t0, value):
        convv[r0 : r0 + n, t0 : t0 + 256] = value.astype(F32)

    conv_all(DK, DK, taps_k, store_k)
    conv_all(2 * DK, DV, taps_v, store_v)

    remote(ext.at[SEG : SEG + 8], halo, halo_sem.at[0], halo_sem.at[1], after, y).wait_recv()
    ext[0:8, :] = halo[...]
    conv_first(DK, DK, taps_k, store_k)
    conv_first(2 * DK, DV, taps_v, store_v)

    tail = jnp.where(pf_col[...] == pf_last, 1.0, 0.0)
    weighted = (convk[...] * jnp.exp(c_last - cum[...]) * across(tail, DK // 128)).astype(BF16)
    local[...] = dot_tn(weighted, convv[...].astype(BF16))

    def half_rows(which):
        return pl.ds(pl.multiple_of(which * HALF, HALF), HALF)

    pair_s[...] = local[half_rows(1 - core), :].astype(BF16)
    to_sib = remote(pair_s, pair_r, pair_sem.at[0], pair_sem.at[1], sib, y)
    to_sib.start()
    sib_g = g + 1 - 2 * core
    remote(dsend, dgat.at[sib_g], d_send.at[0], d_recv.at[sib_g], sib, y).wait_recv()
    dmat[0:8, :] = dsend[...]
    dmat[8:16, :] = dgat[sib_g]
    dts[...] = jnp.transpose(dmat[...])
    mine_d = dts[half_rows(core), :]
    own_d, sib_d = mine_d[:, 0:1], mine_d[:, 8:9]
    is_first = core == 0
    d_first = jnp.where(is_first, own_d, sib_d)
    d_second = jnp.where(is_first, sib_d, own_d)
    to_sib.wait_recv()
    own_l = local[half_rows(core), :]
    sib_l = pair_r[...].astype(F32)
    l_first = jnp.where(is_first, own_l, sib_l)
    first_l[...] = l_first
    chip_l = (l_first * d_second + jnp.where(is_first, sib_l, own_l)).astype(BF16)
    for k in range(CHIPS):
        ts[k] = chip_l[16 * (k // XS) : 16 * (k // XS) + 16, 128 * (k % XS) : 128 * (k % XS) + 128]
    me = z * XS + x

    def to_chip(i, d, src, dst, ss, rs):
        k, device = chip(d)
        return remote(src.at[k], dst.at[me], ss.at[i], rs.at[me], device, y)

    def from_chip(d, dst, ss, rs):
        k, device = chip(d)
        return remote(dst.at[k], dst.at[k], ss.at[0], rs.at[k], device, y)

    for i, d in enumerate(OTHERS):
        to_chip(i, d, ts, tr, t_send, t_recv).start()
    tr[me] = ts[me]

    for dx in (1, 3, 2):
        for dc in range(2):
            j = lax.rem(x + dx, XS) * 2 + lax.rem(core + dc, 2)
            remote(dsend, dgat.at[j], d_send.at[0], d_recv.at[j], z * GROUP + j, y).wait_recv()

    sub = lax.broadcasted_iota(jnp.int32, (8, HALF), 0)
    chips_d = jnp.zeros((8, HALF), F32)
    for j in range(XS):
        both = dgat[2 * j] * dgat[2 * j + 1]
        chips_d = jnp.where(sub == j, jnp.where(is_first, both[:, 0:HALF], both[:, HALF:DK]), chips_d)
    gsend[...] = chips_d
    for k in (4, 3, 5, 2, 6, 1, 7):
        remote(gsend, ggat.at[z], g_send.at[k], g_recv.at[z], peer(k) * GROUP + g, y).start()
    ggat[z] = gsend[...]

    def store_q(r0, n, t0, value):
        inner[r0 : r0 + n, 0:DK] = value.astype(F32)

    conv_all(0, DK, taps_q, store_q)
    conv_first(0, DK, taps_q, store_q)

    for b in range(SEG // ROWS):
        r0, r1 = b * ROWS, (b + 1) * ROWS
        q = inner[r0:r1, 0:DK]
        if b == 0:
            start = jnp.zeros((1, DK), F32)
        else:
            start = cum[r0 - 1 : r0, :]
        up_q = q * jnp.exp(cum[r0:r1, :] - start)
        intact = jnp.where(pf_col[r0:r1, :] < first, 1.0, 0.0)
        reach = (up_q * jnp.exp(start) * across(intact, DK // 128)).astype(BF16)
        lifted[0, b] = reach[:, 0:HALF]
        lifted[1, b] = reach[:, HALF:DK]
        down_k = (convk[0:r1, :] * jnp.exp(start - cum[0:r1, :])).astype(BF16)
        scores = dot_nt(up_q.astype(BF16), down_k)
        ri = r0 + lax.broadcasted_iota(jnp.int32, (ROWS, r1), 0)
        ci = lax.broadcasted_iota(jnp.int32, (ROWS, r1), 1)
        same = pf_col[r0:r1, 0:1] == pf_row[0:1, 0:r1]
        scores = jnp.where((ri >= ci) & same, scores, 0.0).astype(BF16)
        inner[r0:r1, :] = dot(scores, convv[0:r1, :].astype(BF16))

    for k in range(1, PLANES):
        j = peer(k)
        remote(gsend, ggat.at[j], g_send.at[k], g_recv.at[j], j * GROUP + g, y).wait_recv()
    padded = jnp.concatenate([ggat[...].reshape(8 * PLANES, HALF), jnp.zeros((64, HALF), F32)], axis=0)
    dt[...] = jnp.transpose(padded)

    for d in OTHERS:
        from_chip(d, tr, t_send, t_recv).wait_recv()
    tile_d = dt[pl.ds(pl.multiple_of(16 * z, 16), 16), :]
    run = jnp.zeros((16, 128), F32)
    for k in range(CHIPS):
        qs[k] = run.astype(BF16)
        lane = 8 * (k // XS) + k % XS
        run = run * tile_d[:, lane : lane + 1] + tr[k].astype(F32)
    for i, d in enumerate(OTHERS):
        to_chip(i, d, qs, qr, q_send, q_recv).start()
    qr[me] = qs[me]

    for b in range(SEG // ROWS):
        gate = acc[b, :, QKV:WIDE].astype(BF16).astype(F32)
        half = 0.5 * gate
        gg[b] = (half * jnp.tanh(half) + half) * gain_v[...]

    for d in OTHERS:
        from_chip(d, qr, q_send, q_recv).wait_recv()
    at_first = jnp.concatenate(
        [jnp.concatenate([qr[XS * a + b].astype(F32) for b in range(XS)], axis=1) for a in range(PLANES)],
        axis=0,
    )
    at_second = at_first * d_first + first_l[...]
    pe_s[...] = jnp.where(is_first, at_second, at_first).astype(BF16)
    sib_e = remote(pe_s, er.at[core], pe_sem.at[0], pe_sem.at[1], sib, y)
    sib_e.start()
    er[core] = jnp.where(is_first, at_first, at_second).astype(BF16)
    for b in range(SEG // ROWS):
        inner[b * ROWS : (b + 1) * ROWS, :] += dot(lifted[core, b], er[core])
    remote(pe_s, er.at[1 - core], pe_sem.at[0], pe_sem.at[1], sib, y).wait_recv()

    def heads(block):
        rows = pl.ds(pl.multiple_of(block * ROWS, ROWS), ROWS)
        out = inner[rows, :] + dot(lifted[1 - core, block], er[1 - core])
        scale = lax.rsqrt(jnp.mean(out * out, axis=1, keepdims=True) + 1e-05)
        return (out * scale * gg[block]).astype(BF16)

    def project(gated, c):
        return dot(gated, wo[:, c * CHUNK : (c + 1) * CHUNK])

    def to_right(slot, dst, sem):
        return remote(rs_s.at[slot], dst, rs_send.at[slot], sem, tok, right)

    def to_left(slot, dst, sem):
        return remote(rs_s.at[slot], dst, rs_send.at[slot], sem, tok, left)

    gated = heads(opp)
    for c in (0, 2, 1, 3):
        rs_s[c] = project(gated, c).astype(BF16)
        (to_right if c < 2 else to_left)(c, relay.at[c], relay_recv.at[c]).start()
    gated_r = heads(right)
    gated_l = heads(left)
    for i in range(2):
        c = 2 + i
        rs_s[4 + c] = project(gated_r, c).astype(BF16)
        to_right(4 + c, fl.at[c], fl_recv.at[c]).start()
        c = i
        rs_s[4 + c] = project(gated_l, c).astype(BF16)
        to_left(4 + c, fr.at[c], fr_recv.at[c]).start()
    for i in range(2):
        c = i
        part = project(gated_r, c)
        to_right(c, relay.at[c], relay_recv.at[c]).wait_recv()
        rs_s[8 + c] = (part + relay[c].astype(F32)).astype(BF16)
        to_right(8 + c, fl.at[c], fl_recv.at[c]).start()
        c = 2 + i
        part = project(gated_l, c)
        to_left(c, relay.at[c], relay_recv.at[c]).wait_recv()
        rs_s[8 + c] = (part + relay[c].astype(F32)).astype(BF16)
        to_left(8 + c, fr.at[c], fr_recv.at[c]).start()

    states[...] = er[...].reshape(DK, DV).astype(F32) * dts[:, 0:1] + local[...]
    for j in range(3):
        r = SEG - 3 + j
        inside = jnp.where(first + r >= pf_last, 1.0, 0.0)
        edges[0, 0, j : j + 1, :] = (ext[8 + r : 9 + r, :] * across(inside, QKV // 128)).astype(BF16)

    outs = [
        pltpu.make_async_copy(states, states_out, out_sem.at[0]),
        pltpu.make_async_copy(edges, edges_out, out_sem.at[1]),
    ]
    for out in outs:
        out.start()

    gated = heads(y)
    for c in (2, 3, 0, 1):
        part = project(gated, c)
        to_right(0, fl.at[c], fl_recv.at[c]).wait_recv()
        to_right(0, fr.at[c], fr_recv.at[c]).wait_recv()
        mixed[:, c * CHUNK : (c + 1) * CHUNK] = (
            part + fl[c].astype(F32) + fr[c].astype(F32)
        ).astype(BF16)
        chunk = slice(c * CHUNK, (c + 1) * CHUNK)
        out = pltpu.make_async_copy(mixed.at[:, chunk], mixed_out.at[:, chunk], out_sem.at[2 + c])
        out.start()
        outs.append(out)

    for out in outs:
        out.wait()
    for s in range(4):
        own_to_right(s).wait_send()
        own_to_left(s).wait_send()
    for f in range(2):
        on_to_right(f).wait_send()
        on_to_left(f).wait_send()
    halo_copy.wait_send()
    for k in [0] + list(range(2, 8)):
        remote(dsend, dgat.at[g], d_send.at[k], d_recv.at[g], sib, y).wait_send()
    for k in range(1, PLANES):
        remote(gsend, ggat.at[z], g_send.at[k], g_recv.at[z], sib, y).wait_send()
    to_sib.wait_send()
    sib_e.wait_send()
    for i, d in enumerate(OTHERS):
        to_chip(i, d, ts, tr, t_send, t_recv).wait_send()
        to_chip(i, d, qs, qr, q_send, q_recv).wait_send()
    for slot in range(12):
        to_right(slot, fl.at[0], fl_recv.at[0]).wait_send()


def write_out(mixed, states, edges, mixed_out, states_out, edges_out, mixed_v, states_v, edges_v, sem):
    def copies(src, dst, i):
        parts = [(src, dst)]
        if src.shape[0] == DK:
            parts = [(src.at[r : r + ROWS], dst.at[r : r + ROWS]) for r in range(0, DK, ROWS)]
        return [pltpu.make_async_copy(a, b, sem.at[i + k]) for k, (a, b) in enumerate(parts)]

    loads = copies(states, states_v, 0) + copies(mixed, mixed_v, 4) + copies(edges, edges_v, 5)
    stores = copies(states_v, states_out, 6) + copies(mixed_v, mixed_out, 10) + copies(edges_v, edges_out, 11)
    for load in loads:
        load.start()
    for load, store in zip(loads, stores):
        load.wait()
        store.start()
    for store in stores:
        store.wait()


def shards(
    tokens,
    prompt_lengths,
    query_weight,
    key_weight,
    value_weight,
    query_conv,
    key_conv,
    value_conv,
    decay_down,
    decay_up,
    decay_bias,
    gate_weight,
    norm_gain,
    out_weight,
):
    rank = decay_down.shape[1]
    dma = pltpu.SemaphoreType.DMA
    anywhere = pl.BlockSpec(memory_space=pl.ANY)
    mixed, states, edges = pl.pallas_call(
        kernel,
        out_shape=(
            jax.ShapeDtypeStruct((ROWS, D), BF16),
            jax.ShapeDtypeStruct((DK, DV), F32),
            jax.ShapeDtypeStruct((1, 1, 3, QKV), BF16),
        ),
        in_specs=[anywhere] * 14,
        out_specs=(anywhere,) * 3,
        scratch_shapes=[
            pltpu.VMEM((ROWS, D), BF16),
            pltpu.VMEM((DK, DV), F32),
            pltpu.VMEM((1, 1, 3, QKV), BF16),
            pltpu.VMEM((HV, ROWS, D), BF16),
            pltpu.VMEM((D, WIDE), BF16),
            pltpu.VMEM((rank, D), BF16),
            pltpu.VMEM((DV, D), BF16),
            pltpu.VMEM((4, DK), BF16),
            pltpu.VMEM((4, DK), BF16),
            pltpu.VMEM((4, DV), BF16),
            pltpu.VMEM((rank, DK), BF16),
            pltpu.VMEM((1, DK), F32),
            pltpu.VMEM((1, DV), F32),
            pltpu.SMEM(prompt_lengths.shape, jnp.int32),
            pltpu.VMEM((HV, ROWS, WIDE), F32),
            pltpu.VMEM((HV, ROWS, rank), F32),
            pltpu.VMEM((8 + SEG, QKV), F32),
            pltpu.VMEM((8, QKV), F32),
            pltpu.VMEM((SEG, 128), jnp.int32),
            pltpu.VMEM((8, SEG), jnp.int32),
            pltpu.VMEM((3, SEG, 128), F32),
            pltpu.VMEM((SEG, DK), F32),
            pltpu.VMEM((SEG, DK), F32),
            pltpu.VMEM((SEG, DV), F32),
            pltpu.VMEM((DK, DV), F32),
            pltpu.VMEM((2, HV, ROWS, HALF), BF16),
            pltpu.VMEM((SEG, DV), F32),
            pltpu.VMEM((HV, ROWS, DV), F32),
            pltpu.VMEM((8, DK), F32),
            pltpu.VMEM((GROUP, 8, DK), F32),
            pltpu.VMEM((8, HALF), F32),
            pltpu.VMEM((PLANES, 8, HALF), F32),
            pltpu.VMEM((128, DK), F32),
            pltpu.VMEM((DK, 128), F32),
            pltpu.VMEM((HALF, 128), F32),
            pltpu.VMEM((HALF, DV), BF16),
            pltpu.VMEM((HALF, DV), BF16),
            pltpu.VMEM((HALF, DV), F32),
            pltpu.VMEM((CHIPS, 16, 128), BF16),
            pltpu.VMEM((CHIPS, 16, 128), BF16),
            pltpu.VMEM((CHIPS, 16, 128), BF16),
            pltpu.VMEM((CHIPS, 16, 128), BF16),
            pltpu.VMEM((HALF, DV), BF16),
            pltpu.VMEM((2, HALF, DV), BF16),
            pltpu.VMEM((12, ROWS, CHUNK), BF16),
            pltpu.VMEM((4, ROWS, CHUNK), BF16),
            pltpu.VMEM((4, ROWS, CHUNK), BF16),
            pltpu.VMEM((4, ROWS, CHUNK), BF16),
            dma((4, 4)),
            dma((10,)),
            dma((2, 6)),
            dma((2, 6)),
            dma((2,)),
            dma((8,)),
            dma((8,)),
            dma((8,)),
            dma((8,)),
            dma((2,)),
            dma((CHIPS,)),
            dma((CHIPS,)),
            dma((CHIPS,)),
            dma((CHIPS,)),
            dma((2,)),
            dma((12,)),
            dma((4,)),
            dma((4,)),
            dma((4,)),
            dma((6,)),
        ],
        compiler_params=pltpu.CompilerParams(
            collective_id=0, has_side_effects=True, vmem_limit_bytes=63 * 1024 * 1024
        ),
        name="gla",
    )(
        tokens,
        prompt_lengths,
        query_weight,
        key_weight,
        value_weight,
        query_conv,
        key_conv,
        value_conv,
        decay_down.T,
        decay_up,
        decay_bias.reshape(1, DK),
        gate_weight,
        norm_gain.reshape(1, DV),
        out_weight,
    )
    parts = (mixed, states, edges)
    mixed, states, edges = pl.pallas_call(
        write_out,
        out_shape=tuple(jax.ShapeDtypeStruct(a.shape, a.dtype) for a in parts),
        in_specs=[anywhere] * 3,
        out_specs=(anywhere,) * 3,
        scratch_shapes=[pltpu.VMEM(a.shape, a.dtype) for a in parts] + [dma((12,))],
        name="write_out",
    )(*parts)
    return mixed, states[None, None], edges.transpose(0, 2, 1, 3)


def solution(mesh):
    in_specs = (
        P(("tok", "hv"), None),
        P(),
        P(None, "hv"),
        P(None, "hv"),
        P(None, "hv"),
        P(None, "hv"),
        P(None, "hv"),
        P(None, "hv"),
        P(),
        P(None, "hv"),
        P("hv"),
        P(None, "hv"),
        P(),
        P("hv", None),
    )
    out_specs = (P(("tok", "hv"), None), P("tok", "hv", None, None), P("tok", None, "hv", None))
    return jax.shard_map(shards, mesh=mesh, in_specs=in_specs, out_specs=out_specs, check_vma=False)
```

```python
import functools

import jax
import jax.numpy as jnp
from jax import lax
from jax.experimental import pallas as pl
from jax.experimental.pallas import tpu as pltpu
from jax.sharding import PartitionSpec as P

MESH = pl.DeviceIdType.MESH
F32 = jnp.float32
BF16 = jnp.bfloat16
HIGHEST = lax.Precision.HIGHEST

HV = 4
GROUP = 8
PLANES = 8
ROWS = 64
SEG = 256
D = 2048
DK = 256
DV = 512
QKV = 2 * DK + DV
WIDE = QKV + DV
CHUNK = 512
HALF = DK // 2
XS = 4
CHIPS = XS * PLANES
OTHERS = sorted(
    [(dz, dx) for dz in range(PLANES) for dx in range(XS) if (dz, dx) != (0, 0)],
    key=lambda d: -(min(d[0], PLANES - d[0]) + min(d[1], XS - d[1])),
)


def dot(a, b):
    return jnp.dot(a, b, preferred_element_type=F32)


def dot_nt(a, b):
    return lax.dot_general(a, b, (((1,), (1,)), ((), ())), preferred_element_type=F32)


def dot_tn(a, b):
    return lax.dot_general(a, b, (((0,), (0,)), ((), ())), preferred_element_type=F32)


def across(a, copies):
    return jnp.concatenate([a] * copies, axis=1)


def kernel(
    tokens,
    lengths,
    wq,
    wk,
    wv,
    cq,
    ck,
    cv,
    wdown,
    wup,
    bias,
    wg,
    gain,
    wout,
    mixed,
    states,
    edges,
    xt,
    wall,
    wlow,
    wo,
    taps_q,
    taps_k,
    taps_v,
    up,
    bias_v,
    gain_v,
    lens,
    acc,
    accl,
    ext,
    halo,
    pf_col,
    pf_row,
    keep,
    cum,
    convk,
    convv,
    local,
    lifted,
    inner,
    gg,
    dsend,
    dgat,
    gsend,
    ggat,
    dmat,
    dts,
    dt,
    pair_s,
    pair_r,
    first_l,
    ts,
    tr,
    qs,
    qr,
    pe_s,
    er,
    rs_s,
    relay,
    fl,
    fr,
    w_sem,
    loc_sem,
    tk_send,
    tk_recv,
    halo_sem,
    d_send,
    d_recv,
    g_send,
    g_recv,
    pair_sem,
    t_send,
    t_recv,
    q_send,
    q_recv,
    pe_sem,
    rs_send,
    relay_recv,
    fl_recv,
    fr_recv,
    groups_in,
):
    tok = lax.axis_index("tok")
    y = lax.axis_index("hv")
    n_tok = GROUP * PLANES
    z = lax.div(tok, GROUP)
    g = lax.rem(tok, GROUP)
    x = lax.div(g, 2)
    core = lax.rem(tok, 2)
    sib = tok + 1 - 2 * core
    right = lax.rem(y + 1, HV)
    left = lax.rem(y + HV - 1, HV)
    opp = lax.rem(y + 2, HV)
    after = lax.rem(tok + 1, n_tok)
    before = lax.rem(tok + n_tok - 1, n_tok)

    def remote(src, dst, ss, rs, to_tok, to_hv):
        return pltpu.make_async_remote_copy(
            src_ref=src, dst_ref=dst, send_sem=ss, recv_sem=rs, device_id=(to_tok, to_hv), device_id_type=MESH
        )

    def mate(k):
        return lax.rem(g + k, GROUP)

    def peer(k):
        return lax.rem(z + k, PLANES)

    def chip(d):
        other_z, other_x = lax.rem(z + d[0], PLANES), lax.rem(x + d[1], XS)
        return other_z * XS + other_x, other_z * GROUP + other_x * 2 + core

    own = pltpu.make_async_copy(tokens, xt.at[y], loc_sem.at[0])
    own.start()

    def weight_copies(c):
        rows = pl.ds(c * CHUNK, CHUNK)
        return [
            pltpu.make_async_copy(wq.at[rows], wall.at[rows, 0:DK], w_sem.at[c, 0]),
            pltpu.make_async_copy(wk.at[rows], wall.at[rows, DK : 2 * DK], w_sem.at[c, 1]),
            pltpu.make_async_copy(wv.at[rows], wall.at[rows, 2 * DK : QKV], w_sem.at[c, 2]),
            pltpu.make_async_copy(wg.at[rows], wall.at[rows, QKV:WIDE], w_sem.at[c, 3]),
        ]

    small = [
        pltpu.make_async_copy(src, dst, loc_sem.at[1 + i])
        for i, (src, dst) in enumerate(
            [
                (lengths, lens),
                (wdown, wlow),
                (wup, up),
                (bias, bias_v),
                (gain, gain_v),
                (cq, taps_q),
                (ck, taps_k),
                (cv, taps_v),
                (wout, wo),
            ]
        )
    ]

    barrier = pltpu.get_barrier_semaphore()
    pl.semaphore_signal(barrier, inc=1, device_id=(tok, right), device_id_type=MESH)
    pl.semaphore_signal(barrier, inc=1, device_id=(tok, left), device_id_type=MESH)
    pl.semaphore_signal(barrier, inc=1, device_id=(after, y), device_id_type=MESH)
    pl.semaphore_signal(barrier, inc=1, device_id=(before, y), device_id_type=MESH)
    for k in range(1, GROUP):
        pl.semaphore_signal(barrier, inc=1, device_id=(z * GROUP + mate(k), y), device_id_type=MESH)
    for k in range(1, PLANES):
        pl.semaphore_signal(barrier, inc=1, device_id=(peer(k) * GROUP + g, y), device_id_type=MESH)
    for copy in small[:2]:
        copy.start()
    for c in range(D // CHUNK):
        for copy in weight_copies(c):
            copy.start()
    for copy in small[2:]:
        copy.start()
    pl.semaphore_wait(barrier, 4 + GROUP - 1 + PLANES - 1)

    def cols(c):
        return pl.ds(pl.multiple_of(c * CHUNK, CHUNK), CHUNK)

    def own_to_right(s):
        return remote(
            tokens.at[:, cols(s)], xt.at[y, :, cols(s)], tk_send.at[0, s], tk_recv.at[0, s], tok, right
        )

    def own_to_left(s):
        c = lax.rem(s + 2, 4)
        return remote(
            tokens.at[:, cols(c)], xt.at[y, :, cols(c)], tk_send.at[1, s], tk_recv.at[1, s], tok, left
        )

    def from_left(s):
        part = xt.at[left, :, cols(s)]
        return remote(part, part, tk_send.at[0, s], tk_recv.at[0, s], tok, right)

    def from_right(s):
        part = xt.at[right, :, cols(lax.rem(s + 2, 4))]
        return remote(part, part, tk_send.at[1, s], tk_recv.at[1, s], tok, left)

    def on_to_right(f):
        part = xt.at[left, :, cols(f)]
        return remote(part, part, tk_send.at[0, 4 + f], tk_recv.at[0, 4 + f], tok, right)

    def on_to_left(f):
        part = xt.at[right, :, cols(f + 2)]
        return remote(part, part, tk_send.at[1, 4 + f], tk_recv.at[1, 4 + f], tok, left)

    def far_from_left(f):
        part = xt.at[opp, :, cols(f)]
        return remote(part, part, tk_send.at[0, 4 + f], tk_recv.at[0, 4 + f], tok, right)

    def far_from_right(f):
        part = xt.at[opp, :, cols(f + 2)]
        return remote(part, part, tk_send.at[1, 4 + f], tk_recv.at[1, 4 + f], tok, left)

    for s in range(4):
        own_to_right(s).start()
        own_to_left(s).start()

    for k in range(1, PLANES):
        pl.semaphore_signal(groups_in, inc=1, device_id=(peer(k) * GROUP + g, y), device_id_type=MESH)

    acc[...] = jnp.zeros_like(acc)
    accl[...] = jnp.zeros_like(accl)

    for copy in small[:2]:
        copy.wait()
    first = tok * SEG
    pos_col = first + lax.broadcasted_iota(jnp.int32, (SEG, 128), 0)
    pos_row = first + lax.broadcasted_iota(jnp.int32, (8, SEG), 1)

    def mark(j, carried):
        offset, col, row = carried
        col = jnp.where(offset <= pos_col, offset, col)
        row = jnp.where(offset <= pos_row, offset, row)
        return offset + lens[j], col, row

    _, col, row = lax.fori_loop(
        0,
        lens.shape[0],
        mark,
        (jnp.int32(0), jnp.zeros((SEG, 128), jnp.int32), jnp.zeros((8, SEG), jnp.int32)),
    )
    pf_col[...] = col
    pf_row[...] = row
    for lag in range(1, 4):
        keep[lag - 1] = jnp.where(pos_col - lag >= col, 1.0, 0.0)

    def gemm(block, c):
        x = xt[block, :, cols(c)]
        for n in range(0, WIDE, CHUNK):
            acc[block, :, n : n + CHUNK] += dot(x, wall[cols(c), n : n + CHUNK])
        accl[block] += dot_nt(x, wlow[:, cols(c)])

    own.wait()

    def own_step(c, _):
        for copy in weight_copies(c):
            copy.wait()
        gemm(y, c)
        return 0

    lax.fori_loop(0, 4, own_step, 0)

    def near_step(s, _):
        from_left(s).wait_recv()
        on_to_right(s).start()
        from_right(s).wait_recv()
        on_to_left(s).start()
        gemm(left, s)
        gemm(right, s + 2)
        return 0

    lax.fori_loop(0, 2, near_step, 0)

    def near_step2(s, _):
        from_left(s).wait_recv()
        gemm(left, s)
        from_right(s).wait_recv()
        gemm(right, s - 2)
        return 0

    lax.fori_loop(2, 4, near_step2, 0)

    def far_step(f, _):
        far_from_left(f).wait_recv()
        gemm(opp, f)
        far_from_right(f).wait_recv()
        gemm(opp, f + 2)
        return 0

    lax.fori_loop(0, 2, far_step, 0)

    for b in (3, 0, 1, 2):
        ext[8 + b * ROWS : 8 + (b + 1) * ROWS, :] = acc[b, :, 0:QKV].astype(BF16).astype(F32)
        if b == 3:
            halo_copy = remote(
                ext.at[SEG : SEG + 8], halo, halo_sem.at[0], halo_sem.at[1], after, y
            )
            halo_copy.start()

    for copy in small[2:]:
        copy.wait()

    row_i = lax.broadcasted_iota(jnp.int32, (SEG, SEG), 0)
    col_i = lax.broadcasted_iota(jnp.int32, (SEG, SEG), 1)
    tri = jnp.where(row_i >= col_i, 1.0, 0.0).astype(F32)
    low = accl[...].reshape(SEG, accl.shape[2]).astype(BF16)
    v = dot(low, up[...]) + bias_v[...]
    decays = (jnp.minimum(v, 0.0) - jnp.log1p(jnp.exp(-jnp.abs(v)))) * (1.0 / 16.0)
    cum[...] = jnp.dot(tri, decays, precision=HIGHEST, preferred_element_type=F32)
    c_last = cum[SEG - 1 : SEG, :]
    pf_last = pf_col[SEG - 1 : SEG, :]
    whole = jnp.where(pf_last < first, 1.0, 0.0)
    dsend[...] = jnp.broadcast_to(jnp.exp(c_last) * across(whole, DK // 128), (8, DK))
    remote(dsend, dgat.at[g], d_send.at[0], d_recv.at[g], sib, y).start()
    for dx in (2, 1, 3):
        for dc in range(2):
            to = z * GROUP + lax.rem(x + dx, XS) * 2 + lax.rem(core + dc, 2)
            remote(dsend, dgat.at[g], d_send.at[2 * dx + dc], d_recv.at[g], to, y).start()
    dgat[g] = dsend[...]

    def conv(r0, n, source, base, c0, width, taps, t0):
        tw = taps[:, t0 : t0 + width].astype(F32)
        total = tw[3:4] * source[base + r0 : base + r0 + n, c0 : c0 + width]
        for lag in range(1, 4):
            window = source[base + r0 - lag : base + r0 - lag + n, c0 : c0 + width]
            total += tw[3 - lag : 4 - lag] * window * across(keep[lag - 1, r0 : r0 + n, :], width // 128)
        half = 0.5 * total
        return (half * jnp.tanh(half) + half).astype(BF16)

    def conv_all(c0, width, taps, store):
        for r0 in [8, 16] + list(range(32, SEG, 32)):
            n = 8 if r0 == 8 else 16 if r0 == 16 else 32
            for t0 in range(0, width, 256):
                store(r0, n, t0, conv(r0, n, ext, 8, c0 + t0, 256, taps, t0))

    def conv_first(c0, width, taps, store):
        for t0 in range(0, width, 256):
            store(0, 8, t0, conv(0, 8, ext, 8, c0 + t0, 256, taps, t0))

    def store_k(r0, n, t0, value):
        convk[r0 : r0 + n, t0 : t0 + 256] = value.astype(F32)

    def store_v(r0, n, t0, value):
        convv[r0 : r0 + n, t0 : t0 + 256] = value.astype(F32)

    conv_all(DK, DK, taps_k, store_k)
    conv_all(2 * DK, DV, taps_v, store_v)

    remote(ext.at[SEG : SEG + 8], halo, halo_sem.at[0], halo_sem.at[1], after, y).wait_recv()
    ext[0:8, :] = halo[...]
    conv_first(DK, DK, taps_k, store_k)
    conv_first(2 * DK, DV, taps_v, store_v)

    tail = jnp.where(pf_col[...] == pf_last, 1.0, 0.0)
    weighted = (convk[...] * jnp.exp(c_last - cum[...]) * across(tail, DK // 128)).astype(BF16)
    local[...] = dot_tn(weighted, convv[...].astype(BF16))

    def half_rows(which):
        return pl.ds(pl.multiple_of(which * HALF, HALF), HALF)

    pair_s[...] = local[half_rows(1 - core), :].astype(BF16)
    to_sib = remote(pair_s, pair_r, pair_sem.at[0], pair_sem.at[1], sib, y)
    to_sib.start()
    sib_g = g + 1 - 2 * core
    remote(dsend, dgat.at[sib_g], d_send.at[0], d_recv.at[sib_g], sib, y).wait_recv()
    dmat[0:8, :] = dsend[...]
    dmat[8:16, :] = dgat[sib_g]
    dts[...] = jnp.transpose(dmat[...])
    mine_d = dts[half_rows(core), :]
    own_d, sib_d = mine_d[:, 0:1], mine_d[:, 8:9]
    is_first = core == 0
    d_first = jnp.where(is_first, own_d, sib_d)
    d_second = jnp.where(is_first, sib_d, own_d)
    to_sib.wait_recv()
    own_l = local[half_rows(core), :]
    sib_l = pair_r[...].astype(F32)
    l_first = jnp.where(is_first, own_l, sib_l)
    first_l[...] = l_first
    chip_l = (l_first * d_second + jnp.where(is_first, sib_l, own_l)).astype(BF16)
    for k in range(CHIPS):
        ts[k] = chip_l[16 * (k // XS) : 16 * (k // XS) + 16, 128 * (k % XS) : 128 * (k % XS) + 128]
    me = z * XS + x

    def to_chip(i, d, src, dst, ss, rs):
        k, device = chip(d)
        return remote(src.at[k], dst.at[me], ss.at[i], rs.at[me], device, y)

    def from_chip(d, dst, ss, rs):
        k, device = chip(d)
        return remote(dst.at[k], dst.at[k], ss.at[0], rs.at[k], device, y)

    pl.semaphore_wait(groups_in, PLANES - 1)
    for i, d in enumerate(OTHERS):
        to_chip(i, d, ts, tr, t_send, t_recv).start()
    tr[me] = ts[me]

    for dx in (1, 3, 2):
        for dc in range(2):
            j = lax.rem(x + dx, XS) * 2 + lax.rem(core + dc, 2)
            remote(dsend, dgat.at[j], d_send.at[0], d_recv.at[j], z * GROUP + j, y).wait_recv()

    sub = lax.broadcasted_iota(jnp.int32, (8, HALF), 0)
    chips_d = jnp.zeros((8, HALF), F32)
    for j in range(XS):
        both = dgat[2 * j] * dgat[2 * j + 1]
        chips_d = jnp.where(sub == j, jnp.where(is_first, both[:, 0:HALF], both[:, HALF:DK]), chips_d)
    gsend[...] = chips_d
    for k in (4, 3, 5, 2, 6, 1, 7):
        remote(gsend, ggat.at[z], g_send.at[k], g_recv.at[z], peer(k) * GROUP + g, y).start()
    ggat[z] = gsend[...]

    def store_q(r0, n, t0, value):
        inner[r0 : r0 + n, 0:DK] = value.astype(F32)

    conv_all(0, DK, taps_q, store_q)
    conv_first(0, DK, taps_q, store_q)

    for b in range(SEG // ROWS):
        r0, r1 = b * ROWS, (b + 1) * ROWS
        q = inner[r0:r1, 0:DK]
        if b == 0:
            start = jnp.zeros((1, DK), F32)
        else:
            start = cum[r0 - 1 : r0, :]
        up_q = q * jnp.exp(cum[r0:r1, :] - start)
        intact = jnp.where(pf_col[r0:r1, :] < first, 1.0, 0.0)
        reach = (up_q * jnp.exp(start) * across(intact, DK // 128)).astype(BF16)
        lifted[0, b] = reach[:, 0:HALF]
        lifted[1, b] = reach[:, HALF:DK]
        down_k = (convk[0:r1, :] * jnp.exp(start - cum[0:r1, :])).astype(BF16)
        scores = dot_nt(up_q.astype(BF16), down_k)
        ri = r0 + lax.broadcasted_iota(jnp.int32, (ROWS, r1), 0)
        ci = lax.broadcasted_iota(jnp.int32, (ROWS, r1), 1)
        same = pf_col[r0:r1, 0:1] == pf_row[0:1, 0:r1]
        scores = jnp.where((ri >= ci) & same, scores, 0.0).astype(BF16)
        inner[r0:r1, :] = dot(scores, convv[0:r1, :].astype(BF16))

    for k in range(1, PLANES):
        j = peer(k)
        remote(gsend, ggat.at[j], g_send.at[k], g_recv.at[j], j * GROUP + g, y).wait_recv()
    padded = jnp.concatenate([ggat[...].reshape(8 * PLANES, HALF), jnp.zeros((64, HALF), F32)], axis=0)
    dt[...] = jnp.transpose(padded)

    for d in OTHERS:
        from_chip(d, tr, t_send, t_recv).wait_recv()
    tile_d = dt[pl.ds(pl.multiple_of(16 * z, 16), 16), :]
    run = jnp.zeros((16, 128), F32)
    for k in range(CHIPS):
        qs[k] = run.astype(BF16)
        lane = 8 * (k // XS) + k % XS
        run = run * tile_d[:, lane : lane + 1] + tr[k].astype(F32)
    for i, d in enumerate(OTHERS):
        to_chip(i, d, qs, qr, q_send, q_recv).start()
    qr[me] = qs[me]

    for b in range(SEG // ROWS):
        gate = acc[b, :, QKV:WIDE].astype(BF16).astype(F32)
        half = 0.5 * gate
        gg[b] = (half * jnp.tanh(half) + half) * gain_v[...]

    for d in OTHERS:
        from_chip(d, qr, q_send, q_recv).wait_recv()
    at_first = jnp.concatenate(
        [jnp.concatenate([qr[XS * a + b].astype(F32) for b in range(XS)], axis=1) for a in range(PLANES)],
        axis=0,
    )
    at_second = at_first * d_first + first_l[...]
    pe_s[...] = jnp.where(is_first, at_second, at_first).astype(BF16)
    sib_e = remote(pe_s, er.at[core], pe_sem.at[0], pe_sem.at[1], sib, y)
    sib_e.start()
    er[core] = jnp.where(is_first, at_first, at_second).astype(BF16)
    for b in range(SEG // ROWS):
        inner[b * ROWS : (b + 1) * ROWS, :] += dot(lifted[core, b], er[core])
    remote(pe_s, er.at[1 - core], pe_sem.at[0], pe_sem.at[1], sib, y).wait_recv()

    def heads(block):
        rows = pl.ds(pl.multiple_of(block * ROWS, ROWS), ROWS)
        out = inner[rows, :] + dot(lifted[1 - core, block], er[1 - core])
        scale = lax.rsqrt(jnp.mean(out * out, axis=1, keepdims=True) + 1e-05)
        return (out * scale * gg[block]).astype(BF16)

    def project(gated, c):
        return dot(gated, wo[:, c * CHUNK : (c + 1) * CHUNK])

    def to_right(slot, dst, sem):
        return remote(rs_s.at[slot], dst, rs_send.at[slot], sem, tok, right)

    def to_left(slot, dst, sem):
        return remote(rs_s.at[slot], dst, rs_send.at[slot], sem, tok, left)

    gated = heads(opp)
    for c in (0, 2, 1, 3):
        rs_s[c] = project(gated, c).astype(BF16)
        (to_right if c < 2 else to_left)(c, relay.at[c], relay_recv.at[c]).start()
    gated_r = heads(right)
    gated_l = heads(left)
    for i in range(2):
        c = 2 + i
        rs_s[4 + c] = project(gated_r, c).astype(BF16)
        to_right(4 + c, fl.at[c], fl_recv.at[c]).start()
        c = i
        rs_s[4 + c] = project(gated_l, c).astype(BF16)
        to_left(4 + c, fr.at[c], fr_recv.at[c]).start()
    for i in range(2):
        c = i
        part = project(gated_r, c)
        to_right(c, relay.at[c], relay_recv.at[c]).wait_recv()
        rs_s[8 + c] = (part + relay[c].astype(F32)).astype(BF16)
        to_right(8 + c, fl.at[c], fl_recv.at[c]).start()
        c = 2 + i
        part = project(gated_l, c)
        to_left(c, relay.at[c], relay_recv.at[c]).wait_recv()
        rs_s[8 + c] = (part + relay[c].astype(F32)).astype(BF16)
        to_left(8 + c, fr.at[c], fr_recv.at[c]).start()

    states[...] = er[...].reshape(DK, DV).astype(F32) * dts[:, 0:1] + local[...]
    for j in range(3):
        r = SEG - 3 + j
        inside = jnp.where(first + r >= pf_last, 1.0, 0.0)
        edges[0, 0, j : j + 1, :] = (ext[8 + r : 9 + r, :] * across(inside, QKV // 128)).astype(BF16)

    gated = heads(y)
    for c in (2, 3, 0, 1):
        part = project(gated, c)
        to_right(0, fl.at[c], fl_recv.at[c]).wait_recv()
        to_right(0, fr.at[c], fr_recv.at[c]).wait_recv()
        mixed[:, c * CHUNK : (c + 1) * CHUNK] = (
            part + fl[c].astype(F32) + fr[c].astype(F32)
        ).astype(BF16)

    for s in range(4):
        own_to_right(s).wait_send()
        own_to_left(s).wait_send()
    for f in range(2):
        on_to_right(f).wait_send()
        on_to_left(f).wait_send()
    halo_copy.wait_send()
    for k in [0] + list(range(2, 8)):
        remote(dsend, dgat.at[g], d_send.at[k], d_recv.at[g], sib, y).wait_send()
    for k in range(1, PLANES):
        remote(gsend, ggat.at[z], g_send.at[k], g_recv.at[z], sib, y).wait_send()
    to_sib.wait_send()
    sib_e.wait_send()
    for i, d in enumerate(OTHERS):
        to_chip(i, d, ts, tr, t_send, t_recv).wait_send()
        to_chip(i, d, qs, qr, q_send, q_recv).wait_send()
    for slot in range(12):
        to_right(slot, fl.at[0], fl_recv.at[0]).wait_send()


def write_out(mixed, states, edges, mixed_out, states_out, edges_out, sem):
    def copies(src, dst, i, step):
        rows = src.shape[0]
        return [
            pltpu.make_async_copy(src.at[r : r + step], dst.at[r : r + step], sem.at[i + r // step])
            for r in range(0, rows, step)
        ]

    stores = copies(states, states_out, 0, ROWS) + copies(mixed, mixed_out, 4, 32) + copies(edges, edges_out, 6, 1)
    for store in stores:
        store.start()
    for store in stores:
        store.wait()


def shards(
    tokens,
    prompt_lengths,
    query_weight,
    key_weight,
    value_weight,
    query_conv,
    key_conv,
    value_conv,
    decay_down,
    decay_up,
    decay_bias,
    gate_weight,
    norm_gain,
    out_weight,
):
    rank = decay_down.shape[1]
    dma = pltpu.SemaphoreType.DMA
    anywhere = pl.BlockSpec(memory_space=pl.ANY)
    vmem = pl.BlockSpec(memory_space=pltpu.VMEM)
    mixed, states, edges = pl.pallas_call(
        kernel,
        out_shape=(
            pltpu.VMEM((ROWS, D), BF16),
            pltpu.VMEM((DK, DV), F32),
            pltpu.VMEM((1, 1, 3, QKV), BF16),
        ),
        in_specs=[anywhere] * 14,
        out_specs=(vmem, vmem, vmem),
        scratch_shapes=[
            pltpu.VMEM((HV, ROWS, D), BF16),
            pltpu.VMEM((D, WIDE), BF16),
            pltpu.VMEM((rank, D), BF16),
            pltpu.VMEM((DV, D), BF16),
            pltpu.VMEM((4, DK), BF16),
            pltpu.VMEM((4, DK), BF16),
            pltpu.VMEM((4, DV), BF16),
            pltpu.VMEM((rank, DK), BF16),
            pltpu.VMEM((1, DK), F32),
            pltpu.VMEM((1, DV), F32),
            pltpu.SMEM(prompt_lengths.shape, jnp.int32),
            pltpu.VMEM((HV, ROWS, WIDE), F32),
            pltpu.VMEM((HV, ROWS, rank), F32),
            pltpu.VMEM((8 + SEG, QKV), F32),
            pltpu.VMEM((8, QKV), F32),
            pltpu.VMEM((SEG, 128), jnp.int32),
            pltpu.VMEM((8, SEG), jnp.int32),
            pltpu.VMEM((3, SEG, 128), F32),
            pltpu.VMEM((SEG, DK), F32),
            pltpu.VMEM((SEG, DK), F32),
            pltpu.VMEM((SEG, DV), F32),
            pltpu.VMEM((DK, DV), F32),
            pltpu.VMEM((2, HV, ROWS, HALF), BF16),
            pltpu.VMEM((SEG, DV), F32),
            pltpu.VMEM((HV, ROWS, DV), F32),
            pltpu.VMEM((8, DK), F32),
            pltpu.VMEM((GROUP, 8, DK), F32),
            pltpu.VMEM((8, HALF), F32),
            pltpu.VMEM((PLANES, 8, HALF), F32),
            pltpu.VMEM((128, DK), F32),
            pltpu.VMEM((DK, 128), F32),
            pltpu.VMEM((HALF, 128), F32),
            pltpu.VMEM((HALF, DV), BF16),
            pltpu.VMEM((HALF, DV), BF16),
            pltpu.VMEM((HALF, DV), F32),
            pltpu.VMEM((CHIPS, 16, 128), BF16),
            pltpu.VMEM((CHIPS, 16, 128), BF16),
            pltpu.VMEM((CHIPS, 16, 128), BF16),
            pltpu.VMEM((CHIPS, 16, 128), BF16),
            pltpu.VMEM((HALF, DV), BF16),
            pltpu.VMEM((2, HALF, DV), BF16),
            pltpu.VMEM((12, ROWS, CHUNK), BF16),
            pltpu.VMEM((4, ROWS, CHUNK), BF16),
            pltpu.VMEM((4, ROWS, CHUNK), BF16),
            pltpu.VMEM((4, ROWS, CHUNK), BF16),
            dma((4, 4)),
            dma((10,)),
            dma((2, 6)),
            dma((2, 6)),
            dma((2,)),
            dma((8,)),
            dma((8,)),
            dma((8,)),
            dma((8,)),
            dma((2,)),
            dma((CHIPS,)),
            dma((CHIPS,)),
            dma((CHIPS,)),
            dma((CHIPS,)),
            dma((2,)),
            dma((12,)),
            dma((4,)),
            dma((4,)),
            dma((4,)),
            pltpu.SemaphoreType.REGULAR,
        ],
        compiler_params=pltpu.CompilerParams(
            collective_id=0, has_side_effects=True, vmem_limit_bytes=48 * 1024 * 1024
        ),
        name="gla",
    )(
        *[
            pltpu.with_memory_space_constraint(a, pltpu.HBM)
            for a in (
                tokens,
                prompt_lengths,
                query_weight,
                key_weight,
                value_weight,
                query_conv,
                key_conv,
                value_conv,
                decay_down.T,
                decay_up,
                decay_bias.reshape(1, DK),
                gate_weight,
                norm_gain.reshape(1, DV),
                out_weight,
            )
        ]
    )
    parts = (mixed, states, edges)
    mixed, states, edges = pl.pallas_call(
        write_out,
        out_shape=tuple(jax.ShapeDtypeStruct(a.shape, a.dtype) for a in parts),
        in_specs=[vmem] * 3,
        out_specs=(anywhere,) * 3,
        scratch_shapes=[dma((7,))],
        name="write_out",
    )(*[pltpu.with_memory_space_constraint(a, pltpu.VMEM) for a in parts])
    return mixed, states[None, None], edges.transpose(0, 2, 1, 3)


def solution(mesh):
    in_specs = (
        P(("tok", "hv"), None),
        P(),
        P(None, "hv"),
        P(None, "hv"),
        P(None, "hv"),
        P(None, "hv"),
        P(None, "hv"),
        P(None, "hv"),
        P(),
        P(None, "hv"),
        P("hv"),
        P(None, "hv"),
        P(),
        P("hv", None),
    )
    out_specs = (P(("tok", "hv"), None), P("tok", "hv", None, None), P("tok", None, "hv", None))
    return jax.shard_map(shards, mesh=mesh, in_specs=in_specs, out_specs=out_specs, check_vma=False)
```

```python
import functools

import jax
import jax.numpy as jnp
from jax import lax
from jax.experimental import pallas as pl
from jax.experimental.pallas import tpu as pltpu
from jax.sharding import PartitionSpec as P

MESH = pl.DeviceIdType.MESH
F32 = jnp.float32
BF16 = jnp.bfloat16
HIGHEST = lax.Precision.HIGHEST

HV = 4
GROUP = 8
PLANES = 8
ROWS = 64
SEG = 256
D = 2048
DK = 256
DV = 512
QKV = 2 * DK + DV
WIDE = QKV + DV
CHUNK = 512
HALF = DK // 2
XS = 4
CHIPS = XS * PLANES
OTHERS = sorted(
    [(dz, dx) for dz in range(PLANES) for dx in range(XS) if (dz, dx) != (0, 0)],
    key=lambda d: -(min(d[0], PLANES - d[0]) + min(d[1], XS - d[1])),
)


def dot(a, b):
    return jnp.dot(a, b, preferred_element_type=F32)


def dot_nt(a, b):
    return lax.dot_general(a, b, (((1,), (1,)), ((), ())), preferred_element_type=F32)


def dot_tn(a, b):
    return lax.dot_general(a, b, (((0,), (0,)), ((), ())), preferred_element_type=F32)


def across(a, copies):
    return jnp.concatenate([a] * copies, axis=1)


def kernel(
    tokens,
    lengths,
    wq,
    wk,
    wv,
    cq,
    ck,
    cv,
    wdown,
    wup,
    bias,
    wg,
    gain,
    wout,
    mixed,
    states,
    edges,
    xt,
    wall,
    wlow,
    wo,
    taps_q,
    taps_k,
    taps_v,
    up,
    bias_v,
    gain_v,
    lens,
    acc,
    accl,
    ext,
    halo,
    pf_col,
    pf_row,
    keep,
    cum,
    convk,
    convv,
    local,
    lifted,
    inner,
    gg,
    dsend,
    dgat,
    gsend,
    ggat,
    dmat,
    dts,
    dt,
    pair_s,
    pair_r,
    first_l,
    ts,
    tr,
    qs,
    qr,
    pe_s,
    er,
    rs_s,
    relay,
    fin,
    w_sem,
    loc_sem,
    tk_send,
    tk_recv,
    halo_sem,
    d_send,
    d_recv,
    g_send,
    g_recv,
    pair_sem,
    t_send,
    t_recv,
    q_send,
    q_recv,
    pe_sem,
    rs_send,
    relay_recv,
    f_recv,
    groups_in,
):
    tok = lax.axis_index("tok")
    y = lax.axis_index("hv")
    n_tok = GROUP * PLANES
    z = lax.div(tok, GROUP)
    g = lax.rem(tok, GROUP)
    x = lax.div(g, 2)
    core = lax.rem(tok, 2)
    sib = tok + 1 - 2 * core
    right = lax.rem(y + 1, HV)
    left = lax.rem(y + HV - 1, HV)
    opp = lax.rem(y + 2, HV)
    after = lax.rem(tok + 1, n_tok)
    before = lax.rem(tok + n_tok - 1, n_tok)

    def remote(src, dst, ss, rs, to_tok, to_hv):
        return pltpu.make_async_remote_copy(
            src_ref=src, dst_ref=dst, send_sem=ss, recv_sem=rs, device_id=(to_tok, to_hv), device_id_type=MESH
        )

    def batch(ref, n, ss, rs):
        part = ref.at[pl.ds(0, n)]
        return remote(part, part, ss, rs, sib, y)

    def mate(k):
        return lax.rem(g + k, GROUP)

    def peer(k):
        return lax.rem(z + k, PLANES)

    def chip(d):
        other_z, other_x = lax.rem(z + d[0], PLANES), lax.rem(x + d[1], XS)
        return other_z * XS + other_x, other_z * GROUP + other_x * 2 + core

    own = pltpu.make_async_copy(tokens, xt.at[y], loc_sem.at[0])
    own.start()

    def weight_copies(c):
        rows = pl.ds(c * CHUNK, CHUNK)
        return [
            pltpu.make_async_copy(wq.at[rows], wall.at[rows, 0:DK], w_sem.at[c]),
            pltpu.make_async_copy(wk.at[rows], wall.at[rows, DK : 2 * DK], w_sem.at[c]),
            pltpu.make_async_copy(wv.at[rows], wall.at[rows, 2 * DK : QKV], w_sem.at[c]),
            pltpu.make_async_copy(wg.at[rows], wall.at[rows, QKV:WIDE], w_sem.at[c]),
        ]

    small = [
        pltpu.make_async_copy(src, dst, loc_sem.at[1 + i])
        for i, (src, dst) in enumerate(
            [
                (lengths, lens),
                (wdown, wlow),
                (wup, up),
                (bias, bias_v),
                (gain, gain_v),
                (cq, taps_q),
                (ck, taps_k),
                (cv, taps_v),
                (wout, wo),
            ]
        )
    ]

    barrier = pltpu.get_barrier_semaphore()
    pl.semaphore_signal(barrier, inc=1, device_id=(tok, right), device_id_type=MESH)
    pl.semaphore_signal(barrier, inc=1, device_id=(tok, left), device_id_type=MESH)
    pl.semaphore_signal(barrier, inc=1, device_id=(after, y), device_id_type=MESH)
    pl.semaphore_signal(barrier, inc=1, device_id=(before, y), device_id_type=MESH)
    for k in range(1, GROUP):
        pl.semaphore_signal(barrier, inc=1, device_id=(z * GROUP + mate(k), y), device_id_type=MESH)
    for k in range(1, PLANES):
        pl.semaphore_signal(barrier, inc=1, device_id=(peer(k) * GROUP + g, y), device_id_type=MESH)
    for copy in small[:2]:
        copy.start()
    for c in range(D // CHUNK):
        for copy in weight_copies(c):
            copy.start()
    for copy in small[2:]:
        copy.start()
    pl.semaphore_wait(barrier, 4 + GROUP - 1 + PLANES - 1)

    def cols(c):
        return pl.ds(pl.multiple_of(c * CHUNK, CHUNK), CHUNK)

    def own_to_right(s):
        return remote(
            tokens.at[:, cols(s)], xt.at[y, :, cols(s)], tk_send.at[0], tk_recv.at[0, s], tok, right
        )

    def own_to_left(s):
        c = lax.rem(s + 2, 4)
        return remote(
            tokens.at[:, cols(c)], xt.at[y, :, cols(c)], tk_send.at[0], tk_recv.at[1, s], tok, left
        )

    def from_left(s):
        part = xt.at[left, :, cols(s)]
        return remote(part, part, tk_send.at[0], tk_recv.at[0, s], tok, right)

    def from_right(s):
        part = xt.at[right, :, cols(lax.rem(s + 2, 4))]
        return remote(part, part, tk_send.at[0], tk_recv.at[1, s], tok, left)

    def on_to_right(f):
        part = xt.at[left, :, cols(f)]
        return remote(part, part, tk_send.at[0], tk_recv.at[0, 4 + f], tok, right)

    def on_to_left(f):
        part = xt.at[right, :, cols(f + 2)]
        return remote(part, part, tk_send.at[0], tk_recv.at[1, 4 + f], tok, left)

    def far_from_left(f):
        part = xt.at[opp, :, cols(f)]
        return remote(part, part, tk_send.at[0], tk_recv.at[0, 4 + f], tok, right)

    def far_from_right(f):
        part = xt.at[opp, :, cols(f + 2)]
        return remote(part, part, tk_send.at[0], tk_recv.at[1, 4 + f], tok, left)

    for s in range(4):
        own_to_right(s).start()
        own_to_left(s).start()

    for k in range(1, PLANES):
        pl.semaphore_signal(groups_in, inc=1, device_id=(peer(k) * GROUP + g, y), device_id_type=MESH)

    acc[...] = jnp.zeros_like(acc)
    accl[...] = jnp.zeros_like(accl)

    for copy in small[:2]:
        copy.wait()
    first = tok * SEG
    pos_col = first + lax.broadcasted_iota(jnp.int32, (SEG, 128), 0)
    pos_row = first + lax.broadcasted_iota(jnp.int32, (8, SEG), 1)

    def mark(j, carried):
        offset, col, row = carried
        col = jnp.where(offset <= pos_col, offset, col)
        row = jnp.where(offset <= pos_row, offset, row)
        return offset + lens[j], col, row

    _, col, row = lax.fori_loop(
        0,
        lens.shape[0],
        mark,
        (jnp.int32(0), jnp.zeros((SEG, 128), jnp.int32), jnp.zeros((8, SEG), jnp.int32)),
    )
    pf_col[...] = col
    pf_row[...] = row
    for lag in range(1, 4):
        keep[lag - 1] = jnp.where(pos_col - lag >= col, 1.0, 0.0)

    def gemm(block, c):
        x = xt[block, :, cols(c)]
        for n in range(0, WIDE, CHUNK):
            acc[block, :, n : n + CHUNK] += dot(x, wall[cols(c), n : n + CHUNK])
        accl[block] += dot_nt(x, wlow[:, cols(c)])

    own.wait()

    def own_step(c, _):
        part = wall.at[pl.ds(c * CHUNK, CHUNK)]
        pltpu.make_async_copy(part, part, w_sem.at[c]).wait()
        gemm(y, c)
        return 0

    lax.fori_loop(0, 4, own_step, 0)

    def near_step(s, _):
        from_left(s).wait_recv()
        on_to_right(s).start()
        from_right(s).wait_recv()
        on_to_left(s).start()
        gemm(left, s)
        gemm(right, s + 2)
        return 0

    lax.fori_loop(0, 2, near_step, 0)

    def near_step2(s, _):
        from_left(s).wait_recv()
        gemm(left, s)
        from_right(s).wait_recv()
        gemm(right, s - 2)
        return 0

    lax.fori_loop(2, 4, near_step2, 0)

    def far_step(f, _):
        far_from_left(f).wait_recv()
        gemm(opp, f)
        far_from_right(f).wait_recv()
        gemm(opp, f + 2)
        return 0

    lax.fori_loop(0, 2, far_step, 0)

    for b in (3, 0, 1, 2):
        ext[8 + b * ROWS : 8 + (b + 1) * ROWS, :] = acc[b, :, 0:QKV].astype(BF16).astype(F32)
        if b == 3:
            halo_copy = remote(
                ext.at[SEG : SEG + 8], halo, halo_sem.at[0], halo_sem.at[1], after, y
            )
            halo_copy.start()

    for copy in small[2:]:
        copy.wait()

    row_i = lax.broadcasted_iota(jnp.int32, (SEG, SEG), 0)
    col_i = lax.broadcasted_iota(jnp.int32, (SEG, SEG), 1)
    tri = jnp.where(row_i >= col_i, 1.0, 0.0).astype(F32)
    low = accl[...].reshape(SEG, accl.shape[2]).astype(BF16)
    v = dot(low, up[...]) + bias_v[...]
    decays = (jnp.minimum(v, 0.0) - jnp.log1p(jnp.exp(-jnp.abs(v)))) * (1.0 / 16.0)
    cum[...] = jnp.dot(tri, decays, precision=HIGHEST, preferred_element_type=F32)
    c_last = cum[SEG - 1 : SEG, :]
    pf_last = pf_col[SEG - 1 : SEG, :]
    whole = jnp.where(pf_last < first, 1.0, 0.0)
    dsend[...] = jnp.broadcast_to(jnp.exp(c_last) * across(whole, DK // 128), (8, DK))
    remote(dsend, dgat.at[g], d_send.at[0], d_recv.at[0], sib, y).start()
    for dx in (2, 1, 3):
        for dc in range(2):
            to = z * GROUP + lax.rem(x + dx, XS) * 2 + lax.rem(core + dc, 2)
            remote(dsend, dgat.at[g], d_send.at[0], d_recv.at[1], to, y).start()
    dgat[g] = dsend[...]

    def conv(r0, n, source, base, c0, width, taps, t0):
        tw = taps[:, t0 : t0 + width].astype(F32)
        total = tw[3:4] * source[base + r0 : base + r0 + n, c0 : c0 + width]
        for lag in range(1, 4):
            window = source[base + r0 - lag : base + r0 - lag + n, c0 : c0 + width]
            total += tw[3 - lag : 4 - lag] * window * across(keep[lag - 1, r0 : r0 + n, :], width // 128)
        half = 0.5 * total
        return (half * jnp.tanh(half) + half).astype(BF16)

    def conv_all(c0, width, taps, store, t_from=0):
        for r0 in [8, 16] + list(range(32, SEG, 32)):
            n = 8 if r0 == 8 else 16 if r0 == 16 else 32
            for t0 in range(t_from, width, 256):
                store(r0, n, t0, conv(r0, n, ext, 8, c0 + t0, 256, taps, t0))

    def conv_first(c0, width, taps, store, t_from=0):
        for t0 in range(t_from, width, 256):
            store(0, 8, t0, conv(0, 8, ext, 8, c0 + t0, 256, taps, t0))

    def store_k(r0, n, t0, value):
        convk[r0 : r0 + n, t0 : t0 + 256] = value.astype(F32)

    def store_v(r0, n, t0, value):
        convv[r0 : r0 + n, t0 : t0 + 256] = value.astype(F32)

    conv_all(DK, DK, taps_k, store_k)
    conv_all(2 * DK, DV // 2, taps_v, store_v)

    remote(ext.at[SEG : SEG + 8], halo, halo_sem.at[0], halo_sem.at[1], after, y).wait_recv()
    ext[0:8, :] = halo[...]
    conv_first(DK, DK, taps_k, store_k)
    conv_first(2 * DK, DV // 2, taps_v, store_v)

    tail = jnp.where(pf_col[...] == pf_last, 1.0, 0.0)
    weighted = (convk[...] * jnp.exp(c_last - cum[...]) * across(tail, DK // 128)).astype(BF16)

    def half_rows(which):
        return pl.ds(pl.multiple_of(which * HALF, HALF), HALF)

    def part_cols(p):
        return slice(p * (DV // 2), (p + 1) * (DV // 2))

    to_sib = [remote(pair_s.at[p], pair_r.at[p], pair_sem.at[0, p], pair_sem.at[1, p], sib, y) for p in range(2)]
    for p in range(2):
        if p == 1:
            conv_all(2 * DK, DV, taps_v, store_v, DV // 2)
            conv_first(2 * DK, DV, taps_v, store_v, DV // 2)
        local[:, part_cols(p)] = dot_tn(weighted, convv[:, part_cols(p)].astype(BF16))
        pair_s[p] = local[half_rows(1 - core), part_cols(p)].astype(BF16)
        to_sib[p].start()
    sib_g = g + 1 - 2 * core
    remote(dsend, dgat.at[sib_g], d_send.at[0], d_recv.at[0], sib, y).wait_recv()
    dmat[0:8, :] = dsend[...]
    dmat[8:16, :] = dgat[sib_g]
    dts[...] = jnp.transpose(dmat[...])
    mine_d = dts[half_rows(core), :]
    own_d, sib_d = mine_d[:, 0:1], mine_d[:, 8:9]
    is_first = core == 0
    d_first = jnp.where(is_first, own_d, sib_d)
    d_second = jnp.where(is_first, sib_d, own_d)
    me = z * XS + x

    def to_chip(d, src, dst, ss, rs):
        k, device = chip(d)
        return remote(src.at[k], dst.at[me], ss.at[0], rs.at[0], device, y)

    def tile_to(dz, to_x):
        to_z = lax.rem(z + dz, PLANES)
        k = to_z * XS + to_x
        return remote(ts.at[k], tr.at[me], t_send.at[0], t_recv.at[0], to_z * GROUP + to_x * 2 + core, y)

    def send_tiles(to_xs):
        for dz in (4, 3, 5, 2, 6, 1, 7):
            for to_x in to_xs:
                tile_to(dz, to_x).start()
        for to_x in to_xs:

            @pl.when(x != to_x)
            def _():
                tile_to(0, to_x).start()

    pl.semaphore_wait(groups_in, PLANES - 1)
    for p in range(2):
        to_sib[p].wait_recv()
        own_l = local[half_rows(core), part_cols(p)]
        sib_l = pair_r[p].astype(F32)
        l_first = jnp.where(is_first, own_l, sib_l)
        first_l[:, part_cols(p)] = l_first
        chip_l = (l_first * d_second + jnp.where(is_first, sib_l, own_l)).astype(BF16)
        for to_z in range(PLANES):
            for i in range(2):
                ts[to_z * XS + 2 * p + i] = chip_l[16 * to_z : 16 * to_z + 16, 128 * i : 128 * i + 128]
        send_tiles((2 * p, 2 * p + 1))
    tr[me] = ts[me]

    batch(dgat, GROUP - 2, d_send.at[0], d_recv.at[1]).wait_recv()

    sub = lax.broadcasted_iota(jnp.int32, (8, HALF), 0)
    chips_d = jnp.zeros((8, HALF), F32)
    for j in range(XS):
        both = dgat[2 * j] * dgat[2 * j + 1]
        chips_d = jnp.where(sub == j, jnp.where(is_first, both[:, 0:HALF], both[:, HALF:DK]), chips_d)
    gsend[...] = chips_d
    for k in (4, 3, 5, 2, 6, 1, 7):
        remote(gsend, ggat.at[z], g_send.at[0], g_recv.at[0], peer(k) * GROUP + g, y).start()
    ggat[z] = gsend[...]

    def store_q(r0, n, t0, value):
        inner[r0 : r0 + n, 0:DK] = value.astype(F32)

    conv_all(0, DK, taps_q, store_q)
    conv_first(0, DK, taps_q, store_q)

    for b in range(SEG // ROWS):
        r0, r1 = b * ROWS, (b + 1) * ROWS
        q = inner[r0:r1, 0:DK]
        if b == 0:
            start = jnp.zeros((1, DK), F32)
        else:
            start = cum[r0 - 1 : r0, :]
        up_q = q * jnp.exp(cum[r0:r1, :] - start)
        intact = jnp.where(pf_col[r0:r1, :] < first, 1.0, 0.0)
        reach = (up_q * jnp.exp(start) * across(intact, DK // 128)).astype(BF16)
        lifted[0, b] = reach[:, 0:HALF]
        lifted[1, b] = reach[:, HALF:DK]
        down_k = (convk[0:r1, :] * jnp.exp(start - cum[0:r1, :])).astype(BF16)
        scores = dot_nt(up_q.astype(BF16), down_k)
        ri = r0 + lax.broadcasted_iota(jnp.int32, (ROWS, r1), 0)
        ci = lax.broadcasted_iota(jnp.int32, (ROWS, r1), 1)
        same = pf_col[r0:r1, 0:1] == pf_row[0:1, 0:r1]
        scores = jnp.where((ri >= ci) & same, scores, 0.0).astype(BF16)
        inner[r0:r1, :] = dot(scores, convv[0:r1, :].astype(BF16))

    batch(ggat, PLANES - 1, g_send.at[0], g_recv.at[0]).wait_recv()
    padded = jnp.concatenate([ggat[...].reshape(8 * PLANES, HALF), jnp.zeros((64, HALF), F32)], axis=0)
    dt[...] = jnp.transpose(padded)

    batch(tr, CHIPS - 1, t_send.at[0], t_recv.at[0]).wait_recv()
    tile_d = dt[pl.ds(pl.multiple_of(16 * z, 16), 16), :]
    run = jnp.zeros((16, 128), F32)
    for k in range(CHIPS):
        qs[k] = run.astype(BF16)
        lane = 8 * (k // XS) + k % XS
        run = run * tile_d[:, lane : lane + 1] + tr[k].astype(F32)
    for d in OTHERS:
        to_chip(d, qs, qr, q_send, q_recv).start()
    qr[me] = qs[me]

    for b in range(SEG // ROWS):
        gate = acc[b, :, QKV:WIDE].astype(BF16).astype(F32)
        half = 0.5 * gate
        gg[b] = (half * jnp.tanh(half) + half) * gain_v[...]

    batch(qr, CHIPS - 1, q_send.at[0], q_recv.at[0]).wait_recv()
    at_first = jnp.concatenate(
        [jnp.concatenate([qr[XS * a + b].astype(F32) for b in range(XS)], axis=1) for a in range(PLANES)],
        axis=0,
    )
    at_second = at_first * d_first + first_l[...]
    pe_s[...] = jnp.where(is_first, at_second, at_first).astype(BF16)
    sib_e = remote(pe_s, er.at[core], pe_sem.at[0], pe_sem.at[1], sib, y)
    sib_e.start()
    er[core] = jnp.where(is_first, at_first, at_second).astype(BF16)
    for b in range(SEG // ROWS):
        inner[b * ROWS : (b + 1) * ROWS, :] += dot(lifted[core, b], er[core])
    remote(pe_s, er.at[1 - core], pe_sem.at[0], pe_sem.at[1], sib, y).wait_recv()

    def heads(block):
        rows = pl.ds(pl.multiple_of(block * ROWS, ROWS), ROWS)
        out = inner[rows, :] + dot(lifted[1 - core, block], er[1 - core])
        scale = lax.rsqrt(jnp.mean(out * out, axis=1, keepdims=True) + 1e-05)
        return (out * scale * gg[block]).astype(BF16)

    def project(gated, c):
        return dot(gated, wo[:, c * CHUNK : (c + 1) * CHUNK])

    def to_right(slot, dst, sem):
        return remote(rs_s.at[slot], dst, rs_send.at[0], sem, tok, right)

    def to_left(slot, dst, sem):
        return remote(rs_s.at[slot], dst, rs_send.at[0], sem, tok, left)

    gated = heads(opp)
    for c in (0, 2, 1, 3):
        rs_s[c] = project(gated, c).astype(BF16)
        (to_right if c < 2 else to_left)(c, relay.at[c], relay_recv.at[c]).start()
    gated_r = heads(right)
    gated_l = heads(left)
    for i in range(2):
        c = 2 + i
        rs_s[4 + c] = project(gated_r, c).astype(BF16)
        to_right(4 + c, fin.at[c, 0], f_recv.at[c]).start()
        c = i
        rs_s[4 + c] = project(gated_l, c).astype(BF16)
        to_left(4 + c, fin.at[c, 1], f_recv.at[c]).start()
    for i in range(2):
        c = i
        part = project(gated_r, c)
        to_right(c, relay.at[c], relay_recv.at[c]).wait_recv()
        rs_s[8 + c] = (part + relay[c].astype(F32)).astype(BF16)
        to_right(8 + c, fin.at[c, 0], f_recv.at[c]).start()
        c = 2 + i
        part = project(gated_l, c)
        to_left(c, relay.at[c], relay_recv.at[c]).wait_recv()
        rs_s[8 + c] = (part + relay[c].astype(F32)).astype(BF16)
        to_left(8 + c, fin.at[c, 1], f_recv.at[c]).start()

    states[...] = er[...].reshape(DK, DV).astype(F32) * dts[:, 0:1] + local[...]
    for j in range(3):
        r = SEG - 3 + j
        inside = jnp.where(first + r >= pf_last, 1.0, 0.0)
        edges[0, 0, j : j + 1, :] = (ext[8 + r : 9 + r, :] * across(inside, QKV // 128)).astype(BF16)

    gated = heads(y)
    for c in (2, 3, 0, 1):
        part = project(gated, c)
        remote(fin.at[c], fin.at[c], rs_send.at[0], f_recv.at[c], tok, right).wait_recv()
        mixed[:, c * CHUNK : (c + 1) * CHUNK] = (
            part + fin[c, 0].astype(F32) + fin[c, 1].astype(F32)
        ).astype(BF16)

    batch(xt, HV - 1, tk_send.at[0], tk_recv.at[0, 0]).wait_send()
    halo_copy.wait_send()
    batch(dgat, GROUP - 1, d_send.at[0], d_recv.at[0]).wait_send()
    batch(ggat, PLANES - 1, g_send.at[0], g_recv.at[0]).wait_send()
    for copy in to_sib:
        copy.wait_send()
    batch(ts, CHIPS - 1, t_send.at[0], t_recv.at[0]).wait_send()
    sib_e.wait_send()
    batch(qs, CHIPS - 1, q_send.at[0], q_recv.at[0]).wait_send()
    batch(rs_s, 12, rs_send.at[0], f_recv.at[0]).wait_send()


def write_out(mixed, states, edges, mixed_out, states_out, edges_out, sem):
    def copies(src, dst, i, step):
        rows = src.shape[0]
        return [
            pltpu.make_async_copy(src.at[r : r + step], dst.at[r : r + step], sem.at[i + r // step])
            for r in range(0, rows, step)
        ]

    stores = copies(states, states_out, 0, ROWS) + copies(mixed, mixed_out, 4, 32) + copies(edges, edges_out, 6, 1)
    for store in stores:
        store.start()
    for store in stores:
        store.wait()


def shards(
    tokens,
    prompt_lengths,
    query_weight,
    key_weight,
    value_weight,
    query_conv,
    key_conv,
    value_conv,
    decay_down,
    decay_up,
    decay_bias,
    gate_weight,
    norm_gain,
    out_weight,
):
    rank = decay_down.shape[1]
    dma = pltpu.SemaphoreType.DMA
    anywhere = pl.BlockSpec(memory_space=pl.ANY)
    vmem = pl.BlockSpec(memory_space=pltpu.VMEM)
    mixed, states, edges = pl.pallas_call(
        kernel,
        out_shape=(
            pltpu.VMEM((ROWS, D), BF16),
            pltpu.VMEM((DK, DV), F32),
            pltpu.VMEM((1, 1, 3, QKV), BF16),
        ),
        in_specs=[anywhere] * 14,
        out_specs=(vmem, vmem, vmem),
        scratch_shapes=[
            pltpu.VMEM((HV, ROWS, D), BF16),
            pltpu.VMEM((D, WIDE), BF16),
            pltpu.VMEM((rank, D), BF16),
            pltpu.VMEM((DV, D), BF16),
            pltpu.VMEM((4, DK), BF16),
            pltpu.VMEM((4, DK), BF16),
            pltpu.VMEM((4, DV), BF16),
            pltpu.VMEM((rank, DK), BF16),
            pltpu.VMEM((1, DK), F32),
            pltpu.VMEM((1, DV), F32),
            pltpu.SMEM(prompt_lengths.shape, jnp.int32),
            pltpu.VMEM((HV, ROWS, WIDE), F32),
            pltpu.VMEM((HV, ROWS, rank), F32),
            pltpu.VMEM((8 + SEG, QKV), F32),
            pltpu.VMEM((8, QKV), F32),
            pltpu.VMEM((SEG, 128), jnp.int32),
            pltpu.VMEM((8, SEG), jnp.int32),
            pltpu.VMEM((3, SEG, 128), F32),
            pltpu.VMEM((SEG, DK), F32),
            pltpu.VMEM((SEG, DK), F32),
            pltpu.VMEM((SEG, DV), F32),
            pltpu.VMEM((DK, DV), F32),
            pltpu.VMEM((2, HV, ROWS, HALF), BF16),
            pltpu.VMEM((SEG, DV), F32),
            pltpu.VMEM((HV, ROWS, DV), F32),
            pltpu.VMEM((8, DK), F32),
            pltpu.VMEM((GROUP, 8, DK), F32),
            pltpu.VMEM((8, HALF), F32),
            pltpu.VMEM((PLANES, 8, HALF), F32),
            pltpu.VMEM((128, DK), F32),
            pltpu.VMEM((DK, 128), F32),
            pltpu.VMEM((HALF, 128), F32),
            pltpu.VMEM((2, HALF, DV // 2), BF16),
            pltpu.VMEM((2, HALF, DV // 2), BF16),
            pltpu.VMEM((HALF, DV), F32),
            pltpu.VMEM((CHIPS, 16, 128), BF16),
            pltpu.VMEM((CHIPS, 16, 128), BF16),
            pltpu.VMEM((CHIPS, 16, 128), BF16),
            pltpu.VMEM((CHIPS, 16, 128), BF16),
            pltpu.VMEM((HALF, DV), BF16),
            pltpu.VMEM((2, HALF, DV), BF16),
            pltpu.VMEM((12, ROWS, CHUNK), BF16),
            pltpu.VMEM((4, ROWS, CHUNK), BF16),
            pltpu.VMEM((4, 2, ROWS, CHUNK), BF16),
            dma((4,)),
            dma((10,)),
            dma((1,)),
            dma((2, 6)),
            dma((2,)),
            dma((1,)),
            dma((2,)),
            dma((1,)),
            dma((1,)),
            dma((2, 2)),
            dma((1,)),
            dma((1,)),
            dma((1,)),
            dma((1,)),
            dma((2,)),
            dma((1,)),
            dma((4,)),
            dma((4,)),
            pltpu.SemaphoreType.REGULAR,
        ],
        compiler_params=pltpu.CompilerParams(
            collective_id=0, has_side_effects=True, vmem_limit_bytes=48 * 1024 * 1024
        ),
        name="gla",
    )(
        *[
            pltpu.with_memory_space_constraint(a, pltpu.HBM)
            for a in (
                tokens,
                prompt_lengths,
                query_weight,
                key_weight,
                value_weight,
                query_conv,
                key_conv,
                value_conv,
                decay_down.T,
                decay_up,
                decay_bias.reshape(1, DK),
                gate_weight,
                norm_gain.reshape(1, DV),
                out_weight,
            )
        ]
    )
    parts = (mixed, states, edges)
    mixed, states, edges = pl.pallas_call(
        write_out,
        out_shape=tuple(jax.ShapeDtypeStruct(a.shape, a.dtype) for a in parts),
        in_specs=[vmem] * 3,
        out_specs=(anywhere,) * 3,
        scratch_shapes=[dma((7,))],
        name="write_out",
    )(*[pltpu.with_memory_space_constraint(a, pltpu.VMEM) for a in parts])
    return mixed, states[None, None], edges.transpose(0, 2, 1, 3)


def solution(mesh):
    in_specs = (
        P(("tok", "hv"), None),
        P(),
        P(None, "hv"),
        P(None, "hv"),
        P(None, "hv"),
        P(None, "hv"),
        P(None, "hv"),
        P(None, "hv"),
        P(),
        P(None, "hv"),
        P("hv"),
        P(None, "hv"),
        P(),
        P("hv", None),
    )
    out_specs = (P(("tok", "hv"), None), P("tok", "hv", None, None), P("tok", None, "hv", None))
    return jax.shard_map(shards, mesh=mesh, in_specs=in_specs, out_specs=out_specs, check_vma=False)
```

```python
import functools

import jax
import jax.numpy as jnp
from jax import lax
from jax.experimental import pallas as pl
from jax.experimental.pallas import tpu as pltpu
from jax.sharding import PartitionSpec as P

MESH = pl.DeviceIdType.MESH
F32 = jnp.float32
BF16 = jnp.bfloat16
HIGHEST = lax.Precision.HIGHEST

HV = 4
GROUP = 8
PLANES = 8
ROWS = 64
SEG = 256
D = 2048
DK = 256
DV = 512
QKV = 2 * DK + DV
WIDE = QKV + DV
CHUNK = 512
HALF = DK // 2
XS = 4
CHIPS = XS * PLANES
OTHERS = sorted(
    [(dz, dx) for dz in range(PLANES) for dx in range(XS) if (dz, dx) != (0, 0)],
    key=lambda d: -(min(d[0], PLANES - d[0]) + min(d[1], XS - d[1])),
)


def dot(a, b):
    return jnp.dot(a, b, preferred_element_type=F32)


def dot_nt(a, b):
    return lax.dot_general(a, b, (((1,), (1,)), ((), ())), preferred_element_type=F32)


def dot_tn(a, b):
    return lax.dot_general(a, b, (((0,), (0,)), ((), ())), preferred_element_type=F32)


def across(a, copies):
    return jnp.concatenate([a] * copies, axis=1)


def kernel(
    tokens,
    lengths,
    wq,
    wk,
    wv,
    cq,
    ck,
    cv,
    wdown,
    wup,
    bias,
    wg,
    gain,
    wout,
    mixed,
    states,
    edges,
    xt,
    wall,
    wlow,
    wo,
    taps_q,
    taps_k,
    taps_v,
    up,
    bias_v,
    gain_v,
    lens,
    acc,
    accl,
    ext,
    halo,
    pf_col,
    pf_row,
    keep,
    cum,
    convk,
    convv,
    local,
    lifted,
    inner,
    gg,
    dsend,
    dgat,
    gsend,
    ggat,
    dmat,
    dts,
    dt,
    pair_s,
    pair_r,
    first_l,
    ts,
    tr,
    qs,
    qr,
    pe_s,
    er,
    rs_s,
    relay,
    fin,
    w_sem,
    loc_sem,
    tk_send,
    tk_recv,
    halo_sem,
    d_send,
    d_recv,
    g_send,
    g_recv,
    pair_sem,
    t_send,
    t_recv,
    q_send,
    q_recv,
    pe_sem,
    rs_send,
    relay_recv,
    f_recv,
    groups_in,
):
    tok = lax.axis_index("tok")
    y = lax.axis_index("hv")
    n_tok = GROUP * PLANES
    z = lax.div(tok, GROUP)
    g = lax.rem(tok, GROUP)
    x = lax.div(g, 2)
    core = lax.rem(tok, 2)
    sib = tok + 1 - 2 * core
    right = lax.rem(y + 1, HV)
    left = lax.rem(y + HV - 1, HV)
    opp = lax.rem(y + 2, HV)
    after = lax.rem(tok + 1, n_tok)
    before = lax.rem(tok + n_tok - 1, n_tok)

    def remote(src, dst, ss, rs, to_tok, to_hv):
        return pltpu.make_async_remote_copy(
            src_ref=src, dst_ref=dst, send_sem=ss, recv_sem=rs, device_id=(to_tok, to_hv), device_id_type=MESH
        )

    def batch(ref, n, ss, rs):
        part = ref.at[pl.ds(0, n)]
        return remote(part, part, ss, rs, sib, y)

    def mate(k):
        return lax.rem(g + k, GROUP)

    def peer(k):
        return lax.rem(z + k, PLANES)

    def chip(d):
        other_z, other_x = lax.rem(z + d[0], PLANES), lax.rem(x + d[1], XS)
        return other_z * XS + other_x, other_z * GROUP + other_x * 2 + core

    own = pltpu.make_async_copy(tokens, xt.at[y], loc_sem.at[0])

    def weight_copies(c):
        rows = pl.ds(c * CHUNK, CHUNK)
        return [
            pltpu.make_async_copy(wq.at[rows], wall.at[rows, 0:DK], w_sem.at[c]),
            pltpu.make_async_copy(wk.at[rows], wall.at[rows, DK : 2 * DK], w_sem.at[c]),
            pltpu.make_async_copy(wv.at[rows], wall.at[rows, 2 * DK : QKV], w_sem.at[c]),
            pltpu.make_async_copy(wg.at[rows], wall.at[rows, QKV:WIDE], w_sem.at[c]),
        ]

    small = [
        pltpu.make_async_copy(src, dst, loc_sem.at[1 + i])
        for i, (src, dst) in enumerate(
            [
                (lengths, lens),
                (wdown, wlow),
                (wup, up),
                (bias, bias_v),
                (gain, gain_v),
                (cq, taps_q),
                (ck, taps_k),
                (cv, taps_v),
                (wout, wo),
            ]
        )
    ]

    barrier = pltpu.get_barrier_semaphore()
    pl.semaphore_signal(barrier, inc=1, device_id=(tok, right), device_id_type=MESH)
    pl.semaphore_signal(barrier, inc=1, device_id=(tok, left), device_id_type=MESH)
    pl.semaphore_signal(barrier, inc=1, device_id=(after, y), device_id_type=MESH)
    pl.semaphore_signal(barrier, inc=1, device_id=(before, y), device_id_type=MESH)
    for k in range(1, GROUP):
        pl.semaphore_signal(barrier, inc=1, device_id=(z * GROUP + mate(k), y), device_id_type=MESH)
    for k in range(1, PLANES):
        pl.semaphore_signal(barrier, inc=1, device_id=(peer(k) * GROUP + g, y), device_id_type=MESH)
    pl.semaphore_wait(barrier, 4 + GROUP - 1 + PLANES - 1)

    def cols(c):
        return pl.ds(pl.multiple_of(c * CHUNK, CHUNK), CHUNK)

    def own_to_right(s):
        return remote(
            tokens.at[:, cols(s)], xt.at[y, :, cols(s)], tk_send.at[0], tk_recv.at[0, s], tok, right
        )

    def own_to_left(s):
        c = lax.rem(s + 2, 4)
        return remote(
            tokens.at[:, cols(c)], xt.at[y, :, cols(c)], tk_send.at[0], tk_recv.at[1, s], tok, left
        )

    def from_left(s):
        part = xt.at[left, :, cols(s)]
        return remote(part, part, tk_send.at[0], tk_recv.at[0, s], tok, right)

    def from_right(s):
        part = xt.at[right, :, cols(lax.rem(s + 2, 4))]
        return remote(part, part, tk_send.at[0], tk_recv.at[1, s], tok, left)

    def on_to_right(f):
        part = xt.at[left, :, cols(f)]
        return remote(part, part, tk_send.at[0], tk_recv.at[0, 4 + f], tok, right)

    def on_to_left(f):
        part = xt.at[right, :, cols(f + 2)]
        return remote(part, part, tk_send.at[0], tk_recv.at[1, 4 + f], tok, left)

    def far_from_left(f):
        part = xt.at[opp, :, cols(f)]
        return remote(part, part, tk_send.at[0], tk_recv.at[0, 4 + f], tok, right)

    def far_from_right(f):
        part = xt.at[opp, :, cols(f + 2)]
        return remote(part, part, tk_send.at[0], tk_recv.at[1, 4 + f], tok, left)

    for s in range(4):
        own_to_right(s).start()
        own_to_left(s).start()
    own.start()
    for copy in small[:2]:
        copy.start()
    for c in range(D // CHUNK):
        for copy in weight_copies(c):
            copy.start()
    for copy in small[2:]:
        copy.start()

    for k in range(1, PLANES):
        pl.semaphore_signal(groups_in, inc=1, device_id=(peer(k) * GROUP + g, y), device_id_type=MESH)

    acc[...] = jnp.zeros_like(acc)
    accl[...] = jnp.zeros_like(accl)

    for copy in small[:2]:
        copy.wait()
    first = tok * SEG
    pos_col = first + lax.broadcasted_iota(jnp.int32, (SEG, 128), 0)
    pos_row = first + lax.broadcasted_iota(jnp.int32, (8, SEG), 1)

    def mark(j, carried):
        offset, col, row = carried
        col = jnp.where(offset <= pos_col, offset, col)
        row = jnp.where(offset <= pos_row, offset, row)
        return offset + lens[j], col, row

    _, col, row = lax.fori_loop(
        0,
        lens.shape[0],
        mark,
        (jnp.int32(0), jnp.zeros((SEG, 128), jnp.int32), jnp.zeros((8, SEG), jnp.int32)),
    )
    pf_col[...] = col
    pf_row[...] = row
    for lag in range(1, 4):
        keep[lag - 1] = jnp.where(pos_col - lag >= col, 1.0, 0.0)

    def gemm(block, c):
        x = xt[block, :, cols(c)]
        for n in range(0, WIDE, CHUNK):
            acc[block, :, n : n + CHUNK] += dot(x, wall[cols(c), n : n + CHUNK])
        accl[block] += dot_nt(x, wlow[:, cols(c)])

    own.wait()

    def own_step(c, _):
        part = wall.at[pl.ds(c * CHUNK, CHUNK)]
        pltpu.make_async_copy(part, part, w_sem.at[c]).wait()
        gemm(y, c)
        return 0

    lax.fori_loop(0, 4, own_step, 0)

    def near_step(s, _):
        from_left(s).wait_recv()
        on_to_right(s).start()
        from_right(s).wait_recv()
        on_to_left(s).start()
        gemm(left, s)
        gemm(right, s + 2)
        return 0

    lax.fori_loop(0, 2, near_step, 0)

    def near_step2(s, _):
        from_left(s).wait_recv()
        gemm(left, s)
        from_right(s).wait_recv()
        gemm(right, s - 2)
        return 0

    lax.fori_loop(2, 4, near_step2, 0)

    def far_step(f, _):
        far_from_left(f).wait_recv()
        gemm(opp, f)
        far_from_right(f).wait_recv()
        gemm(opp, f + 2)
        return 0

    lax.fori_loop(0, 2, far_step, 0)

    for b in (3, 0, 1, 2):
        ext[8 + b * ROWS : 8 + (b + 1) * ROWS, :] = acc[b, :, 0:QKV].astype(BF16).astype(F32)
        if b == 3:
            halo_copy = remote(
                ext.at[SEG : SEG + 8], halo, halo_sem.at[0], halo_sem.at[1], after, y
            )
            halo_copy.start()

    for copy in small[2:]:
        copy.wait()

    row_i = lax.broadcasted_iota(jnp.int32, (SEG, SEG), 0)
    col_i = lax.broadcasted_iota(jnp.int32, (SEG, SEG), 1)
    tri = jnp.where(row_i >= col_i, 1.0, 0.0).astype(F32)
    low = accl[...].reshape(SEG, accl.shape[2]).astype(BF16)
    v = dot(low, up[...]) + bias_v[...]
    decays = (jnp.minimum(v, 0.0) - jnp.log1p(jnp.exp(-jnp.abs(v)))) * (1.0 / 16.0)
    cum[...] = jnp.dot(tri, decays, precision=HIGHEST, preferred_element_type=F32)
    c_last = cum[SEG - 1 : SEG, :]
    pf_last = pf_col[SEG - 1 : SEG, :]
    whole = jnp.where(pf_last < first, 1.0, 0.0)
    dsend[...] = jnp.broadcast_to(jnp.exp(c_last) * across(whole, DK // 128), (8, DK))
    remote(dsend, dgat.at[g], d_send.at[0], d_recv.at[0], sib, y).start()
    for dx in (2, 1, 3):
        for dc in range(2):
            to = z * GROUP + lax.rem(x + dx, XS) * 2 + lax.rem(core + dc, 2)
            remote(dsend, dgat.at[g], d_send.at[0], d_recv.at[1], to, y).start()
    dgat[g] = dsend[...]

    def conv(r0, n, source, base, c0, width, taps, t0):
        tw = taps[:, t0 : t0 + width].astype(F32)
        total = tw[3:4] * source[base + r0 : base + r0 + n, c0 : c0 + width]
        for lag in range(1, 4):
            window = source[base + r0 - lag : base + r0 - lag + n, c0 : c0 + width]
            total += tw[3 - lag : 4 - lag] * window * across(keep[lag - 1, r0 : r0 + n, :], width // 128)
        half = 0.5 * total
        return (half * jnp.tanh(half) + half).astype(BF16)

    def conv_all(c0, width, taps, store, t_from=0):
        for r0 in [8, 16] + list(range(32, SEG, 32)):
            n = 8 if r0 == 8 else 16 if r0 == 16 else 32
            for t0 in range(t_from, width, 256):
                store(r0, n, t0, conv(r0, n, ext, 8, c0 + t0, 256, taps, t0))

    def conv_first(c0, width, taps, store, t_from=0):
        for t0 in range(t_from, width, 256):
            store(0, 8, t0, conv(0, 8, ext, 8, c0 + t0, 256, taps, t0))

    def store_k(r0, n, t0, value):
        convk[r0 : r0 + n, t0 : t0 + 256] = value.astype(F32)

    def store_v(r0, n, t0, value):
        convv[r0 : r0 + n, t0 : t0 + 256] = value.astype(F32)

    conv_all(DK, DK, taps_k, store_k)
    conv_all(2 * DK, DV // 2, taps_v, store_v)

    remote(ext.at[SEG : SEG + 8], halo, halo_sem.at[0], halo_sem.at[1], after, y).wait_recv()
    ext[0:8, :] = halo[...]
    conv_first(DK, DK, taps_k, store_k)
    conv_first(2 * DK, DV // 2, taps_v, store_v)

    tail = jnp.where(pf_col[...] == pf_last, 1.0, 0.0)
    weighted = jnp.transpose(convk[...] * jnp.exp(c_last - cum[...]) * across(tail, DK // 128)).astype(BF16)

    def half_rows(which):
        return pl.ds(pl.multiple_of(which * HALF, HALF), HALF)

    def part_cols(p):
        return slice(p * (DV // 2), (p + 1) * (DV // 2))

    to_sib = [remote(pair_s.at[p], pair_r.at[p], pair_sem.at[0, p], pair_sem.at[1, p], sib, y) for p in range(2)]
    for p in range(2):
        if p == 1:
            conv_all(2 * DK, DV, taps_v, store_v, DV // 2)
            conv_first(2 * DK, DV, taps_v, store_v, DV // 2)
        local[:, part_cols(p)] = dot(weighted, convv[:, part_cols(p)].astype(BF16))
        pair_s[p] = local[half_rows(1 - core), part_cols(p)].astype(BF16)
        to_sib[p].start()
    sib_g = g + 1 - 2 * core
    remote(dsend, dgat.at[sib_g], d_send.at[0], d_recv.at[0], sib, y).wait_recv()
    dmat[0:8, :] = dsend[...]
    dmat[8:16, :] = dgat[sib_g]
    dts[...] = jnp.transpose(dmat[...])
    mine_d = dts[half_rows(core), :]
    own_d, sib_d = mine_d[:, 0:1], mine_d[:, 8:9]
    is_first = core == 0
    d_first = jnp.where(is_first, own_d, sib_d)
    d_second = jnp.where(is_first, sib_d, own_d)
    me = z * XS + x

    def to_chip(d, src, dst, ss, rs):
        k, device = chip(d)
        return remote(src.at[k], dst.at[me], ss.at[0], rs.at[0], device, y)

    def tile_to(dz, to_x):
        to_z = lax.rem(z + dz, PLANES)
        k = to_z * XS + to_x
        return remote(ts.at[k], tr.at[me], t_send.at[0], t_recv.at[0], to_z * GROUP + to_x * 2 + core, y)

    def send_tiles(to_xs):
        for dz in (4, 3, 5, 2, 6, 1, 7):
            for to_x in to_xs:
                tile_to(dz, to_x).start()
        for to_x in to_xs:

            @pl.when(x != to_x)
            def _():
                tile_to(0, to_x).start()

    pl.semaphore_wait(groups_in, PLANES - 1)
    for p in range(2):
        to_sib[p].wait_recv()
        own_l = local[half_rows(core), part_cols(p)]
        sib_l = pair_r[p].astype(F32)
        l_first = jnp.where(is_first, own_l, sib_l)
        first_l[:, part_cols(p)] = l_first
        chip_l = (l_first * d_second + jnp.where(is_first, sib_l, own_l)).astype(BF16)
        for to_z in range(PLANES):
            for i in range(2):
                ts[to_z * XS + 2 * p + i] = chip_l[16 * to_z : 16 * to_z + 16, 128 * i : 128 * i + 128]
        send_tiles((2 * p, 2 * p + 1))
    tr[me] = ts[me]

    batch(dgat, GROUP - 2, d_send.at[0], d_recv.at[1]).wait_recv()

    sub = lax.broadcasted_iota(jnp.int32, (8, HALF), 0)
    chips_d = jnp.zeros((8, HALF), F32)
    for j in range(XS):
        both = dgat[2 * j] * dgat[2 * j + 1]
        chips_d = jnp.where(sub == j, jnp.where(is_first, both[:, 0:HALF], both[:, HALF:DK]), chips_d)
    gsend[...] = chips_d
    for k in (4, 3, 5, 2, 6, 1, 7):
        remote(gsend, ggat.at[z], g_send.at[0], g_recv.at[0], peer(k) * GROUP + g, y).start()
    ggat[z] = gsend[...]

    def store_q(r0, n, t0, value):
        inner[r0 : r0 + n, 0:DK] = value.astype(F32)

    conv_all(0, DK, taps_q, store_q)
    conv_first(0, DK, taps_q, store_q)

    for b in range(SEG // ROWS):
        r0, r1 = b * ROWS, (b + 1) * ROWS
        q = inner[r0:r1, 0:DK]
        if b == 0:
            start = jnp.zeros((1, DK), F32)
        else:
            start = cum[r0 - 1 : r0, :]
        up_q = q * jnp.exp(cum[r0:r1, :] - start)
        intact = jnp.where(pf_col[r0:r1, :] < first, 1.0, 0.0)
        reach = (up_q * jnp.exp(start) * across(intact, DK // 128)).astype(BF16)
        lifted[0, b] = reach[:, 0:HALF]
        lifted[1, b] = reach[:, HALF:DK]
        down_k = (convk[0:r1, :] * jnp.exp(start - cum[0:r1, :])).astype(BF16)
        scores = dot_nt(up_q.astype(BF16), down_k)
        ri = r0 + lax.broadcasted_iota(jnp.int32, (ROWS, r1), 0)
        ci = lax.broadcasted_iota(jnp.int32, (ROWS, r1), 1)
        same = pf_col[r0:r1, 0:1] == pf_row[0:1, 0:r1]
        scores = jnp.where((ri >= ci) & same, scores, 0.0).astype(BF16)
        inner[r0:r1, :] = dot(scores, convv[0:r1, :].astype(BF16))

    batch(ggat, PLANES - 1, g_send.at[0], g_recv.at[0]).wait_recv()
    padded = jnp.concatenate([ggat[...].reshape(8 * PLANES, HALF), jnp.zeros((64, HALF), F32)], axis=0)
    dt[...] = jnp.transpose(padded)

    batch(tr, CHIPS - 1, t_send.at[0], t_recv.at[0]).wait_recv()
    tile_d = dt[pl.ds(pl.multiple_of(16 * z, 16), 16), :]
    run = jnp.zeros((16, 128), F32)
    for k in range(CHIPS):
        qs[k] = run.astype(BF16)
        lane = 8 * (k // XS) + k % XS
        run = run * tile_d[:, lane : lane + 1] + tr[k].astype(F32)
    for d in OTHERS:
        to_chip(d, qs, qr, q_send, q_recv).start()
    qr[me] = qs[me]

    for b in range(SEG // ROWS):
        gate = acc[b, :, QKV:WIDE].astype(BF16).astype(F32)
        half = 0.5 * gate
        gg[b] = (half * jnp.tanh(half) + half) * gain_v[...]

    batch(qr, CHIPS - 1, q_send.at[0], q_recv.at[0]).wait_recv()
    at_first = jnp.concatenate(
        [jnp.concatenate([qr[XS * a + b].astype(F32) for b in range(XS)], axis=1) for a in range(PLANES)],
        axis=0,
    )
    at_second = at_first * d_first + first_l[...]
    pe_s[...] = jnp.where(is_first, at_second, at_first).astype(BF16)
    sib_e = remote(pe_s, er.at[core], pe_sem.at[0], pe_sem.at[1], sib, y)
    sib_e.start()
    er[core] = jnp.where(is_first, at_first, at_second).astype(BF16)
    for b in range(SEG // ROWS):
        inner[b * ROWS : (b + 1) * ROWS, :] += dot(lifted[core, b], er[core])
    remote(pe_s, er.at[1 - core], pe_sem.at[0], pe_sem.at[1], sib, y).wait_recv()

    def heads(block):
        rows = pl.ds(pl.multiple_of(block * ROWS, ROWS), ROWS)
        out = inner[rows, :] + dot(lifted[1 - core, block], er[1 - core])
        scale = lax.rsqrt(jnp.mean(out * out, axis=1, keepdims=True) + 1e-05)
        return (out * scale * gg[block]).astype(BF16)

    def project(gated, c):
        return dot(gated, wo[:, c * CHUNK : (c + 1) * CHUNK])

    def to_right(slot, dst, sem):
        return remote(rs_s.at[slot], dst, rs_send.at[0], sem, tok, right)

    def to_left(slot, dst, sem):
        return remote(rs_s.at[slot], dst, rs_send.at[0], sem, tok, left)

    gated = heads(opp)
    for c in (0, 2, 1, 3):
        rs_s[c] = project(gated, c).astype(BF16)
        (to_right if c < 2 else to_left)(c, relay.at[c], relay_recv.at[c]).start()
    gated_r = heads(right)
    gated_l = heads(left)
    for i in range(2):
        c = 2 + i
        rs_s[4 + c] = project(gated_r, c).astype(BF16)
        to_right(4 + c, fin.at[c, 0], f_recv.at[c]).start()
        c = i
        rs_s[4 + c] = project(gated_l, c).astype(BF16)
        to_left(4 + c, fin.at[c, 1], f_recv.at[c]).start()
    for i in range(2):
        c = i
        part = project(gated_r, c)
        to_right(c, relay.at[c], relay_recv.at[c]).wait_recv()
        rs_s[8 + c] = (part + relay[c].astype(F32)).astype(BF16)
        to_right(8 + c, fin.at[c, 0], f_recv.at[c]).start()
        c = 2 + i
        part = project(gated_l, c)
        to_left(c, relay.at[c], relay_recv.at[c]).wait_recv()
        rs_s[8 + c] = (part + relay[c].astype(F32)).astype(BF16)
        to_left(8 + c, fin.at[c, 1], f_recv.at[c]).start()

    states[...] = er[...].reshape(DK, DV).astype(F32) * dts[:, 0:1] + local[...]
    for j in range(3):
        r = SEG - 3 + j
        inside = jnp.where(first + r >= pf_last, 1.0, 0.0)
        edges[0, 0, j : j + 1, :] = (ext[8 + r : 9 + r, :] * across(inside, QKV // 128)).astype(BF16)

    gated = heads(y)
    for c in (2, 3, 0, 1):
        part = project(gated, c)
        remote(fin.at[c], fin.at[c], rs_send.at[0], f_recv.at[c], tok, right).wait_recv()
        mixed[:, c * CHUNK : (c + 1) * CHUNK] = (
            part + fin[c, 0].astype(F32) + fin[c, 1].astype(F32)
        ).astype(BF16)

    batch(xt, HV - 1, tk_send.at[0], tk_recv.at[0, 0]).wait_send()
    halo_copy.wait_send()
    batch(dgat, GROUP - 1, d_send.at[0], d_recv.at[0]).wait_send()
    batch(ggat, PLANES - 1, g_send.at[0], g_recv.at[0]).wait_send()
    for copy in to_sib:
        copy.wait_send()
    batch(ts, CHIPS - 1, t_send.at[0], t_recv.at[0]).wait_send()
    sib_e.wait_send()
    batch(qs, CHIPS - 1, q_send.at[0], q_recv.at[0]).wait_send()
    batch(rs_s, 12, rs_send.at[0], f_recv.at[0]).wait_send()


def write_out(mixed, states, edges, mixed_out, states_out, edges_out, sem):
    def copies(src, dst, i, step):
        rows = src.shape[0]
        return [
            pltpu.make_async_copy(src.at[r : r + step], dst.at[r : r + step], sem.at[i + r // step])
            for r in range(0, rows, step)
        ]

    stores = copies(states, states_out, 0, ROWS) + copies(mixed, mixed_out, 4, 32) + copies(edges, edges_out, 6, 1)
    for store in stores:
        store.start()
    for store in stores:
        store.wait()


def shards(
    tokens,
    prompt_lengths,
    query_weight,
    key_weight,
    value_weight,
    query_conv,
    key_conv,
    value_conv,
    decay_down,
    decay_up,
    decay_bias,
    gate_weight,
    norm_gain,
    out_weight,
):
    rank = decay_down.shape[1]
    dma = pltpu.SemaphoreType.DMA
    anywhere = pl.BlockSpec(memory_space=pl.ANY)
    vmem = pl.BlockSpec(memory_space=pltpu.VMEM)
    mixed, states, edges = pl.pallas_call(
        kernel,
        out_shape=(
            pltpu.VMEM((ROWS, D), BF16),
            pltpu.VMEM((DK, DV), F32),
            pltpu.VMEM((1, 1, 3, QKV), BF16),
        ),
        in_specs=[anywhere] * 14,
        out_specs=(vmem, vmem, vmem),
        scratch_shapes=[
            pltpu.VMEM((HV, ROWS, D), BF16),
            pltpu.VMEM((D, WIDE), BF16),
            pltpu.VMEM((rank, D), BF16),
            pltpu.VMEM((DV, D), BF16),
            pltpu.VMEM((4, DK), BF16),
            pltpu.VMEM((4, DK), BF16),
            pltpu.VMEM((4, DV), BF16),
            pltpu.VMEM((rank, DK), BF16),
            pltpu.VMEM((1, DK), F32),
            pltpu.VMEM((1, DV), F32),
            pltpu.SMEM(prompt_lengths.shape, jnp.int32),
            pltpu.VMEM((HV, ROWS, WIDE), F32),
            pltpu.VMEM((HV, ROWS, rank), F32),
            pltpu.VMEM((8 + SEG, QKV), F32),
            pltpu.VMEM((8, QKV), F32),
            pltpu.VMEM((SEG, 128), jnp.int32),
            pltpu.VMEM((8, SEG), jnp.int32),
            pltpu.VMEM((3, SEG, 128), F32),
            pltpu.VMEM((SEG, DK), F32),
            pltpu.VMEM((SEG, DK), F32),
            pltpu.VMEM((SEG, DV), F32),
            pltpu.VMEM((DK, DV), F32),
            pltpu.VMEM((2, HV, ROWS, HALF), BF16),
            pltpu.VMEM((SEG, DV), F32),
            pltpu.VMEM((HV, ROWS, DV), F32),
            pltpu.VMEM((8, DK), F32),
            pltpu.VMEM((GROUP, 8, DK), F32),
            pltpu.VMEM((8, HALF), F32),
            pltpu.VMEM((PLANES, 8, HALF), F32),
            pltpu.VMEM((128, DK), F32),
            pltpu.VMEM((DK, 128), F32),
            pltpu.VMEM((HALF, 128), F32),
            pltpu.VMEM((2, HALF, DV // 2), BF16),
            pltpu.VMEM((2, HALF, DV // 2), BF16),
            pltpu.VMEM((HALF, DV), F32),
            pltpu.VMEM((CHIPS, 16, 128), BF16),
            pltpu.VMEM((CHIPS, 16, 128), BF16),
            pltpu.VMEM((CHIPS, 16, 128), BF16),
            pltpu.VMEM((CHIPS, 16, 128), BF16),
            pltpu.VMEM((HALF, DV), BF16),
            pltpu.VMEM((2, HALF, DV), BF16),
            pltpu.VMEM((12, ROWS, CHUNK), BF16),
            pltpu.VMEM((4, ROWS, CHUNK), BF16),
            pltpu.VMEM((4, 2, ROWS, CHUNK), BF16),
            dma((4,)),
            dma((10,)),
            dma((1,)),
            dma((2, 6)),
            dma((2,)),
            dma((1,)),
            dma((2,)),
            dma((1,)),
            dma((1,)),
            dma((2, 2)),
            dma((1,)),
            dma((1,)),
            dma((1,)),
            dma((1,)),
            dma((2,)),
            dma((1,)),
            dma((4,)),
            dma((4,)),
            pltpu.SemaphoreType.REGULAR,
        ],
        compiler_params=pltpu.CompilerParams(
            collective_id=0, has_side_effects=True, vmem_limit_bytes=48 * 1024 * 1024
        ),
        name="gla",
    )(
        *[
            pltpu.with_memory_space_constraint(a, pltpu.HBM)
            for a in (
                tokens,
                prompt_lengths,
                query_weight,
                key_weight,
                value_weight,
                query_conv,
                key_conv,
                value_conv,
                decay_down.T,
                decay_up,
                decay_bias.reshape(1, DK),
                gate_weight,
                norm_gain.reshape(1, DV),
                out_weight,
            )
        ]
    )
    parts = (mixed, states, edges)
    mixed, states, edges = pl.pallas_call(
        write_out,
        out_shape=tuple(jax.ShapeDtypeStruct(a.shape, a.dtype) for a in parts),
        in_specs=[vmem] * 3,
        out_specs=(anywhere,) * 3,
        scratch_shapes=[dma((7,))],
        name="write_out",
    )(*[pltpu.with_memory_space_constraint(a, pltpu.VMEM) for a in parts])
    return mixed, states[None, None], edges.transpose(0, 2, 1, 3)


def solution(mesh):
    in_specs = (
        P(("tok", "hv"), None),
        P(),
        P(None, "hv"),
        P(None, "hv"),
        P(None, "hv"),
        P(None, "hv"),
        P(None, "hv"),
        P(None, "hv"),
        P(),
        P(None, "hv"),
        P("hv"),
        P(None, "hv"),
        P(),
        P("hv", None),
    )
    out_specs = (P(("tok", "hv"), None), P("tok", "hv", None, None), P("tok", None, "hv", None))
    return jax.shard_map(shards, mesh=mesh, in_specs=in_specs, out_specs=out_specs, check_vma=False)
```

```python
import functools

import jax
import jax.numpy as jnp
from jax import lax
from jax.experimental import pallas as pl
from jax.experimental.pallas import tpu as pltpu
from jax.sharding import PartitionSpec as P

MESH = pl.DeviceIdType.MESH
F32 = jnp.float32
BF16 = jnp.bfloat16
HIGHEST = lax.Precision.HIGHEST

HV = 4
GROUP = 8
PLANES = 8
ROWS = 64
SEG = 256
D = 2048
DK = 256
DV = 512
QKV = 2 * DK + DV
WIDE = QKV + DV
CHUNK = 512
HALF = DK // 2
XS = 4
CHIPS = XS * PLANES
OTHERS = sorted(
    [(dz, dx) for dz in range(PLANES) for dx in range(XS) if (dz, dx) != (0, 0)],
    key=lambda d: -(min(d[0], PLANES - d[0]) + min(d[1], XS - d[1])),
)


def dot(a, b):
    return jnp.dot(a, b, preferred_element_type=F32)


def dot_nt(a, b):
    return lax.dot_general(a, b, (((1,), (1,)), ((), ())), preferred_element_type=F32)


def dot_tn(a, b):
    return lax.dot_general(a, b, (((0,), (0,)), ((), ())), preferred_element_type=F32)


def across(a, copies):
    return jnp.concatenate([a] * copies, axis=1)


def kernel(
    tokens,
    lengths,
    wq,
    wk,
    wv,
    cq,
    ck,
    cv,
    wdown,
    wup,
    bias,
    wg,
    gain,
    wout,
    mixed,
    states,
    edges,
    xt,
    wall,
    wlow,
    wo,
    taps_q,
    taps_k,
    taps_v,
    up,
    bias_v,
    gain_v,
    lens,
    acc,
    accl,
    ext,
    halo,
    pf_col,
    pf_row,
    keep,
    cum,
    convk,
    convv,
    local,
    lifted,
    inner,
    gg,
    dsend,
    dgat,
    gsend,
    ggat,
    dmat,
    dts,
    dt,
    pair_s,
    pair_r,
    first_l,
    ts,
    tr,
    qs,
    qr,
    pe_s,
    er,
    rs_s,
    relay,
    fin,
    w_sem,
    loc_sem,
    tk_send,
    tk_recv,
    halo_sem,
    d_send,
    d_recv,
    g_send,
    g_recv,
    pair_sem,
    t_send,
    t_recv,
    q_send,
    q_recv,
    pe_sem,
    rs_send,
    relay_recv,
    f_recv,
    groups_in,
):
    tok = lax.axis_index("tok")
    y = lax.axis_index("hv")
    n_tok = GROUP * PLANES
    z = lax.div(tok, GROUP)
    g = lax.rem(tok, GROUP)
    x = lax.div(g, 2)
    core = lax.rem(tok, 2)
    sib = tok + 1 - 2 * core
    right = lax.rem(y + 1, HV)
    left = lax.rem(y + HV - 1, HV)
    opp = lax.rem(y + 2, HV)
    after = lax.rem(tok + 1, n_tok)
    before = lax.rem(tok + n_tok - 1, n_tok)

    def remote(src, dst, ss, rs, to_tok, to_hv):
        return pltpu.make_async_remote_copy(
            src_ref=src, dst_ref=dst, send_sem=ss, recv_sem=rs, device_id=(to_tok, to_hv), device_id_type=MESH
        )

    def batch(ref, n, ss, rs):
        part = ref.at[pl.ds(0, n)]
        return remote(part, part, ss, rs, sib, y)

    def mate(k):
        return lax.rem(g + k, GROUP)

    def peer(k):
        return lax.rem(z + k, PLANES)

    def chip(d):
        other_z, other_x = lax.rem(z + d[0], PLANES), lax.rem(x + d[1], XS)
        return other_z * XS + other_x, other_z * GROUP + other_x * 2 + core

    own = pltpu.make_async_copy(tokens, xt.at[y], loc_sem.at[0])

    def weight_copies(c):
        rows = pl.ds(c * CHUNK, CHUNK)
        return [
            pltpu.make_async_copy(wq.at[rows], wall.at[rows, 0:DK], w_sem.at[c]),
            pltpu.make_async_copy(wk.at[rows], wall.at[rows, DK : 2 * DK], w_sem.at[c]),
            pltpu.make_async_copy(wv.at[rows], wall.at[rows, 2 * DK : QKV], w_sem.at[c]),
            pltpu.make_async_copy(wg.at[rows], wall.at[rows, QKV:WIDE], w_sem.at[c]),
        ]

    small = [
        pltpu.make_async_copy(src, dst, loc_sem.at[1 + i])
        for i, (src, dst) in enumerate(
            [
                (lengths, lens),
                (wdown, wlow),
                (wup, up),
                (bias, bias_v),
                (gain, gain_v),
                (cq, taps_q),
                (ck, taps_k),
                (cv, taps_v),
                (wout, wo),
            ]
        )
    ]

    barrier = pltpu.get_barrier_semaphore()
    pl.semaphore_signal(barrier, inc=1, device_id=(tok, right), device_id_type=MESH)
    pl.semaphore_signal(barrier, inc=1, device_id=(tok, left), device_id_type=MESH)
    pl.semaphore_signal(barrier, inc=1, device_id=(after, y), device_id_type=MESH)
    pl.semaphore_signal(barrier, inc=1, device_id=(before, y), device_id_type=MESH)
    for k in range(1, GROUP):
        pl.semaphore_signal(barrier, inc=1, device_id=(z * GROUP + mate(k), y), device_id_type=MESH)
    for k in range(1, PLANES):
        pl.semaphore_signal(barrier, inc=1, device_id=(peer(k) * GROUP + g, y), device_id_type=MESH)
    pl.semaphore_wait(barrier, 4 + GROUP - 1 + PLANES - 1)

    def cols(c):
        return pl.ds(pl.multiple_of(c * CHUNK, CHUNK), CHUNK)

    def own_to_right(s):
        return remote(
            tokens.at[:, cols(s)], xt.at[y, :, cols(s)], tk_send.at[0], tk_recv.at[0, s], tok, right
        )

    def own_to_left(s):
        c = lax.rem(s + 2, 4)
        return remote(
            tokens.at[:, cols(c)], xt.at[y, :, cols(c)], tk_send.at[0], tk_recv.at[1, s], tok, left
        )

    def from_left(s):
        part = xt.at[left, :, cols(s)]
        return remote(part, part, tk_send.at[0], tk_recv.at[0, s], tok, right)

    def from_right(s):
        part = xt.at[right, :, cols(lax.rem(s + 2, 4))]
        return remote(part, part, tk_send.at[0], tk_recv.at[1, s], tok, left)

    def on_to_right(f):
        part = xt.at[left, :, cols(f)]
        return remote(part, part, tk_send.at[0], tk_recv.at[0, 4 + f], tok, right)

    def on_to_left(f):
        part = xt.at[right, :, cols(f + 2)]
        return remote(part, part, tk_send.at[0], tk_recv.at[1, 4 + f], tok, left)

    def far_from_left(f):
        part = xt.at[opp, :, cols(f)]
        return remote(part, part, tk_send.at[0], tk_recv.at[0, 4 + f], tok, right)

    def far_from_right(f):
        part = xt.at[opp, :, cols(f + 2)]
        return remote(part, part, tk_send.at[0], tk_recv.at[1, 4 + f], tok, left)

    for s in range(4):
        own_to_right(s).start()
        own_to_left(s).start()
    own.start()
    for copy in small[:2]:
        copy.start()
    for c in range(D // CHUNK):
        for copy in weight_copies(c):
            copy.start()
    for copy in small[2:]:
        copy.start()

    for k in range(1, PLANES):
        pl.semaphore_signal(groups_in, inc=1, device_id=(peer(k) * GROUP + g, y), device_id_type=MESH)

    acc[...] = jnp.zeros_like(acc)
    accl[...] = jnp.zeros_like(accl)

    for copy in small[:2]:
        copy.wait()
    first = tok * SEG
    pos_col = first + lax.broadcasted_iota(jnp.int32, (SEG, 128), 0)
    pos_row = first + lax.broadcasted_iota(jnp.int32, (8, SEG), 1)

    def mark(j, carried):
        offset, col, row = carried
        col = jnp.where(offset <= pos_col, offset, col)
        row = jnp.where(offset <= pos_row, offset, row)
        return offset + lens[j], col, row

    _, col, row = lax.fori_loop(
        0,
        lens.shape[0],
        mark,
        (jnp.int32(0), jnp.zeros((SEG, 128), jnp.int32), jnp.zeros((8, SEG), jnp.int32)),
    )
    pf_col[...] = col
    pf_row[...] = row
    for lag in range(1, 4):
        keep[lag - 1] = jnp.where(pos_col - lag >= col, 1.0, 0.0)

    def gemm(block, c):
        x = xt[block, :, cols(c)]
        for n in range(0, WIDE, CHUNK):
            acc[block, :, n : n + CHUNK] += dot(x, wall[cols(c), n : n + CHUNK])
        accl[block] += dot_nt(x, wlow[:, cols(c)])

    own.wait()

    def own_step(c, _):
        part = wall.at[pl.ds(c * CHUNK, CHUNK)]
        pltpu.make_async_copy(part, part, w_sem.at[c]).wait()
        gemm(y, c)
        return 0

    lax.fori_loop(0, 4, own_step, 0)

    def near_step(s, _):
        from_left(s).wait_recv()
        on_to_right(s).start()
        from_right(s).wait_recv()
        on_to_left(s).start()
        gemm(left, s)
        gemm(right, s + 2)
        return 0

    lax.fori_loop(0, 2, near_step, 0)

    def near_step2(s, _):
        from_left(s).wait_recv()
        gemm(left, s)
        from_right(s).wait_recv()
        gemm(right, s - 2)
        return 0

    lax.fori_loop(2, 4, near_step2, 0)

    def far_step(f, _):
        far_from_left(f).wait_recv()
        gemm(opp, f)
        far_from_right(f).wait_recv()
        gemm(opp, f + 2)
        return 0

    lax.fori_loop(0, 2, far_step, 0)

    for b in (3, 0, 1, 2):
        ext[8 + b * ROWS : 8 + (b + 1) * ROWS, :] = acc[b, :, 0:QKV].astype(BF16).astype(F32)
        if b == 3:
            halo_copy = remote(
                ext.at[SEG : SEG + 8], halo, halo_sem.at[0], halo_sem.at[1], after, y
            )
            halo_copy.start()

    for copy in small[2:]:
        copy.wait()

    row_i = lax.broadcasted_iota(jnp.int32, (SEG, SEG), 0)
    col_i = lax.broadcasted_iota(jnp.int32, (SEG, SEG), 1)
    tri = jnp.where(row_i >= col_i, 1.0, 0.0).astype(F32)
    low = accl[...].reshape(SEG, accl.shape[2]).astype(BF16)
    v = dot(low, up[...]) + bias_v[...]
    decays = (jnp.minimum(v, 0.0) - jnp.log1p(jnp.exp(-jnp.abs(v)))) * (1.0 / 16.0)
    cum[...] = jnp.dot(tri, decays, precision=HIGHEST, preferred_element_type=F32)
    c_last = cum[SEG - 1 : SEG, :]
    pf_last = pf_col[SEG - 1 : SEG, :]
    whole = jnp.where(pf_last < first, 1.0, 0.0)
    dsend[...] = jnp.broadcast_to(jnp.exp(c_last) * across(whole, DK // 128), (8, DK))
    remote(dsend, dgat.at[g], d_send.at[0], d_recv.at[0], sib, y).start()
    for dx in (2, 1, 3):
        for dc in range(2):
            to = z * GROUP + lax.rem(x + dx, XS) * 2 + lax.rem(core + dc, 2)
            remote(dsend, dgat.at[g], d_send.at[0], d_recv.at[1], to, y).start()
    dgat[g] = dsend[...]

    def conv(r0, n, source, base, c0, width, taps, t0):
        tw = taps[:, t0 : t0 + width].astype(F32)
        total = tw[3:4] * source[base + r0 : base + r0 + n, c0 : c0 + width]
        for lag in range(1, 4):
            window = source[base + r0 - lag : base + r0 - lag + n, c0 : c0 + width]
            total += tw[3 - lag : 4 - lag] * window * across(keep[lag - 1, r0 : r0 + n, :], width // 128)
        half = 0.5 * total
        return (half * jnp.tanh(half) + half).astype(BF16)

    def conv_all(c0, width, taps, store, t_from=0):
        for r0 in [8, 16] + list(range(32, SEG, 32)):
            n = 8 if r0 == 8 else 16 if r0 == 16 else 32
            for t0 in range(t_from, width, 256):
                store(r0, n, t0, conv(r0, n, ext, 8, c0 + t0, 256, taps, t0))

    def conv_first(c0, width, taps, store, t_from=0):
        for t0 in range(t_from, width, 256):
            store(0, 8, t0, conv(0, 8, ext, 8, c0 + t0, 256, taps, t0))

    def store_k(r0, n, t0, value):
        convk[r0 : r0 + n, t0 : t0 + 256] = value.astype(F32)

    def store_v(r0, n, t0, value):
        convv[r0 : r0 + n, t0 : t0 + 256] = value.astype(F32)

    conv_all(DK, DK, taps_k, store_k)
    conv_all(2 * DK, DV // 2, taps_v, store_v)

    remote(ext.at[SEG : SEG + 8], halo, halo_sem.at[0], halo_sem.at[1], after, y).wait_recv()
    ext[0:8, :] = halo[...]
    conv_first(DK, DK, taps_k, store_k)
    conv_first(2 * DK, DV // 2, taps_v, store_v)

    tail = jnp.where(pf_col[...] == pf_last, 1.0, 0.0)
    weighted = jnp.transpose(convk[...] * jnp.exp(c_last - cum[...]) * across(tail, DK // 128)).astype(BF16)

    def half_rows(which):
        return pl.ds(pl.multiple_of(which * HALF, HALF), HALF)

    def part_cols(p):
        return slice(p * (DV // 2), (p + 1) * (DV // 2))

    to_sib = [remote(pair_s.at[p], pair_r.at[p], pair_sem.at[0, p], pair_sem.at[1, p], sib, y) for p in range(2)]
    for p in range(2):
        if p == 1:
            conv_all(2 * DK, DV, taps_v, store_v, DV // 2)
            conv_first(2 * DK, DV, taps_v, store_v, DV // 2)
        local[:, part_cols(p)] = dot(weighted, convv[:, part_cols(p)].astype(BF16))
        pair_s[p] = local[half_rows(1 - core), part_cols(p)].astype(BF16)
        to_sib[p].start()
    sib_g = g + 1 - 2 * core
    remote(dsend, dgat.at[sib_g], d_send.at[0], d_recv.at[0], sib, y).wait_recv()
    dmat[0:8, :] = dsend[...]
    dmat[8:16, :] = dgat[sib_g]
    dts[...] = jnp.transpose(dmat[...])
    mine_d = dts[half_rows(core), :]
    own_d, sib_d = mine_d[:, 0:1], mine_d[:, 8:9]
    is_first = core == 0
    d_first = jnp.where(is_first, own_d, sib_d)
    d_second = jnp.where(is_first, sib_d, own_d)
    me = z * XS + x

    def to_chip(d, src, dst, ss, rs):
        k, device = chip(d)
        return remote(src.at[k], dst.at[me], ss.at[0], rs.at[0], device, y)

    def tile_to(dz, to_x):
        to_z = lax.rem(z + dz, PLANES)
        k = to_z * XS + to_x
        return remote(ts.at[k], tr.at[me], t_send.at[0], t_recv.at[0], to_z * GROUP + to_x * 2 + core, y)

    def send_tiles(to_xs):
        for dz in (4, 3, 5, 2, 6, 1, 7):
            for to_x in to_xs:
                tile_to(dz, to_x).start()
        for to_x in to_xs:

            @pl.when(x != to_x)
            def _():
                tile_to(0, to_x).start()

    pl.semaphore_wait(groups_in, PLANES - 1)
    for p in range(2):
        to_sib[p].wait_recv()
        own_l = local[half_rows(core), part_cols(p)]
        sib_l = pair_r[p].astype(F32)
        l_first = jnp.where(is_first, own_l, sib_l)
        first_l[:, part_cols(p)] = l_first
        chip_l = (l_first * d_second + jnp.where(is_first, sib_l, own_l)).astype(BF16)
        for to_z in range(PLANES):
            for i in range(2):
                ts[to_z * XS + 2 * p + i] = chip_l[16 * to_z : 16 * to_z + 16, 128 * i : 128 * i + 128]
        send_tiles((2 * p, 2 * p + 1))
    tr[me] = ts[me]

    batch(dgat, GROUP - 2, d_send.at[0], d_recv.at[1]).wait_recv()

    sub = lax.broadcasted_iota(jnp.int32, (8, HALF), 0)
    chips_d = jnp.zeros((8, HALF), F32)
    for j in range(XS):
        both = dgat[2 * j] * dgat[2 * j + 1]
        chips_d = jnp.where(sub == j, jnp.where(is_first, both[:, 0:HALF], both[:, HALF:DK]), chips_d)
    gsend[...] = chips_d
    for k in (4, 3, 5, 2, 6, 1, 7):
        remote(gsend, ggat.at[z], g_send.at[0], g_recv.at[0], peer(k) * GROUP + g, y).start()
    ggat[z] = gsend[...]

    def store_q(r0, n, t0, value):
        inner[r0 : r0 + n, 0:DK] = value.astype(F32)

    conv_all(0, DK, taps_q, store_q)
    conv_first(0, DK, taps_q, store_q)

    for b in range(SEG // ROWS):
        r0, r1 = b * ROWS, (b + 1) * ROWS
        q = inner[r0:r1, 0:DK]
        if b == 0:
            start = jnp.zeros((1, DK), F32)
        else:
            start = cum[r0 - 1 : r0, :]
        up_q = q * jnp.exp(cum[r0:r1, :] - start)
        intact = jnp.where(pf_col[r0:r1, :] < first, 1.0, 0.0)
        reach = (up_q * jnp.exp(start) * across(intact, DK // 128)).astype(BF16)
        lifted[0, b] = reach[:, 0:HALF]
        lifted[1, b] = reach[:, HALF:DK]
        down_k = (convk[0:r1, :] * jnp.exp(start - cum[0:r1, :])).astype(BF16)
        scores = dot_nt(up_q.astype(BF16), down_k)
        ri = r0 + lax.broadcasted_iota(jnp.int32, (ROWS, r1), 0)
        ci = lax.broadcasted_iota(jnp.int32, (ROWS, r1), 1)
        same = pf_col[r0:r1, 0:1] == pf_row[0:1, 0:r1]
        scores = jnp.where((ri >= ci) & same, scores, 0.0).astype(BF16)
        inner[r0:r1, :] = dot(scores, convv[0:r1, :].astype(BF16))

    batch(ggat, PLANES - 1, g_send.at[0], g_recv.at[0]).wait_recv()
    padded = jnp.concatenate([ggat[...].reshape(8 * PLANES, HALF), jnp.zeros((64, HALF), F32)], axis=0)
    dt[...] = jnp.transpose(padded)

    batch(tr, CHIPS - 1, t_send.at[0], t_recv.at[0]).wait_recv()
    tile_d = dt[pl.ds(pl.multiple_of(16 * z, 16), 16), :]
    run = jnp.zeros((16, 128), F32)
    for k in range(CHIPS):
        qs[k] = run.astype(BF16)
        lane = 8 * (k // XS) + k % XS
        run = run * tile_d[:, lane : lane + 1] + tr[k].astype(F32)
    for d in OTHERS:
        to_chip(d, qs, qr, q_send, q_recv).start()
    qr[me] = qs[me]

    for b in range(SEG // ROWS):
        gate = acc[b, :, QKV:WIDE].astype(BF16).astype(F32)
        half = 0.5 * gate
        gg[b] = (half * jnp.tanh(half) + half) * gain_v[...]

    batch(qr, CHIPS - 1, q_send.at[0], q_recv.at[0]).wait_recv()
    at_first = jnp.concatenate(
        [jnp.concatenate([qr[XS * a + b].astype(F32) for b in range(XS)], axis=1) for a in range(PLANES)],
        axis=0,
    )
    at_second = at_first * d_first + first_l[...]
    pe_s[...] = jnp.where(is_first, at_second, at_first).astype(BF16)
    sib_e = remote(pe_s, er.at[core], pe_sem.at[0], pe_sem.at[1], sib, y)
    sib_e.start()
    er[core] = jnp.where(is_first, at_first, at_second).astype(BF16)
    for b in range(SEG // ROWS):
        inner[b * ROWS : (b + 1) * ROWS, :] += dot(lifted[core, b], er[core])
    remote(pe_s, er.at[1 - core], pe_sem.at[0], pe_sem.at[1], sib, y).wait_recv()

    def heads(block):
        rows = pl.ds(pl.multiple_of(block * ROWS, ROWS), ROWS)
        out = inner[rows, :] + dot(lifted[1 - core, block], er[1 - core])
        scale = lax.rsqrt(jnp.mean(out * out, axis=1, keepdims=True) + 1e-05)
        return (out * scale * gg[block]).astype(BF16)

    def project(gated, c):
        return dot(gated, wo[:, c * CHUNK : (c + 1) * CHUNK])

    def to_right(slot, dst, sem):
        return remote(rs_s.at[slot], dst, rs_send.at[0], sem, tok, right)

    def to_left(slot, dst, sem):
        return remote(rs_s.at[slot], dst, rs_send.at[0], sem, tok, left)

    gated = heads(opp)
    for c in (0, 2, 1, 3):
        rs_s[c] = project(gated, c).astype(BF16)
        (to_right if c < 2 else to_left)(c, relay.at[c], relay_recv.at[c]).start()
    gated_r = heads(right)
    for c in (2, 3):
        rs_s[4 + c] = project(gated_r, c).astype(BF16)
        to_right(4 + c, fin.at[c, 0], f_recv.at[c]).start()
    gated_l = heads(left)
    for c in (0, 1):
        rs_s[4 + c] = project(gated_l, c).astype(BF16)
        to_left(4 + c, fin.at[c, 1], f_recv.at[c]).start()
    for i in range(2):
        c = i
        part = project(gated_r, c)
        to_right(c, relay.at[c], relay_recv.at[c]).wait_recv()
        rs_s[8 + c] = (part + relay[c].astype(F32)).astype(BF16)
        to_right(8 + c, fin.at[c, 0], f_recv.at[c]).start()
        c = 2 + i
        part = project(gated_l, c)
        to_left(c, relay.at[c], relay_recv.at[c]).wait_recv()
        rs_s[8 + c] = (part + relay[c].astype(F32)).astype(BF16)
        to_left(8 + c, fin.at[c, 1], f_recv.at[c]).start()

    states[...] = er[...].reshape(DK, DV).astype(F32) * dts[:, 0:1] + local[...]
    for j in range(3):
        r = SEG - 3 + j
        inside = jnp.where(first + r >= pf_last, 1.0, 0.0)
        edges[0, 0, j : j + 1, :] = (ext[8 + r : 9 + r, :] * across(inside, QKV // 128)).astype(BF16)

    gated = heads(y)
    for c in (2, 3, 0, 1):
        part = project(gated, c)
        remote(fin.at[c], fin.at[c], rs_send.at[0], f_recv.at[c], tok, right).wait_recv()
        mixed[:, c * CHUNK : (c + 1) * CHUNK] = (
            part + fin[c, 0].astype(F32) + fin[c, 1].astype(F32)
        ).astype(BF16)

    batch(xt, HV - 1, tk_send.at[0], tk_recv.at[0, 0]).wait_send()
    halo_copy.wait_send()
    batch(dgat, GROUP - 1, d_send.at[0], d_recv.at[0]).wait_send()
    batch(ggat, PLANES - 1, g_send.at[0], g_recv.at[0]).wait_send()
    for copy in to_sib:
        copy.wait_send()
    batch(ts, CHIPS - 1, t_send.at[0], t_recv.at[0]).wait_send()
    sib_e.wait_send()
    batch(qs, CHIPS - 1, q_send.at[0], q_recv.at[0]).wait_send()
    batch(rs_s, 12, rs_send.at[0], f_recv.at[0]).wait_send()


def write_out(mixed, states, edges, mixed_out, states_out, edges_out, sem):
    def copies(src, dst, i, step):
        rows = src.shape[0]
        return [
            pltpu.make_async_copy(src.at[r : r + step], dst.at[r : r + step], sem.at[i + r // step])
            for r in range(0, rows, step)
        ]

    stores = copies(states, states_out, 0, ROWS) + copies(mixed, mixed_out, 4, 32) + copies(edges, edges_out, 6, 1)
    for store in stores:
        store.start()
    for store in stores:
        store.wait()


def shards(
    tokens,
    prompt_lengths,
    query_weight,
    key_weight,
    value_weight,
    query_conv,
    key_conv,
    value_conv,
    decay_down,
    decay_up,
    decay_bias,
    gate_weight,
    norm_gain,
    out_weight,
):
    rank = decay_down.shape[1]
    dma = pltpu.SemaphoreType.DMA
    anywhere = pl.BlockSpec(memory_space=pl.ANY)
    vmem = pl.BlockSpec(memory_space=pltpu.VMEM)
    mixed, states, edges = pl.pallas_call(
        kernel,
        out_shape=(
            pltpu.VMEM((ROWS, D), BF16),
            pltpu.VMEM((DK, DV), F32),
            pltpu.VMEM((1, 1, 3, QKV), BF16),
        ),
        in_specs=[anywhere] * 14,
        out_specs=(vmem, vmem, vmem),
        scratch_shapes=[
            pltpu.VMEM((HV, ROWS, D), BF16),
            pltpu.VMEM((D, WIDE), BF16),
            pltpu.VMEM((rank, D), BF16),
            pltpu.VMEM((DV, D), BF16),
            pltpu.VMEM((4, DK), BF16),
            pltpu.VMEM((4, DK), BF16),
            pltpu.VMEM((4, DV), BF16),
            pltpu.VMEM((rank, DK), BF16),
            pltpu.VMEM((1, DK), F32),
            pltpu.VMEM((1, DV), F32),
            pltpu.SMEM(prompt_lengths.shape, jnp.int32),
            pltpu.VMEM((HV, ROWS, WIDE), F32),
            pltpu.VMEM((HV, ROWS, rank), F32),
            pltpu.VMEM((8 + SEG, QKV), F32),
            pltpu.VMEM((8, QKV), F32),
            pltpu.VMEM((SEG, 128), jnp.int32),
            pltpu.VMEM((8, SEG), jnp.int32),
            pltpu.VMEM((3, SEG, 128), F32),
            pltpu.VMEM((SEG, DK), F32),
            pltpu.VMEM((SEG, DK), F32),
            pltpu.VMEM((SEG, DV), F32),
            pltpu.VMEM((DK, DV), F32),
            pltpu.VMEM((2, HV, ROWS, HALF), BF16),
            pltpu.VMEM((SEG, DV), F32),
            pltpu.VMEM((HV, ROWS, DV), F32),
            pltpu.VMEM((8, DK), F32),
            pltpu.VMEM((GROUP, 8, DK), F32),
            pltpu.VMEM((8, HALF), F32),
            pltpu.VMEM((PLANES, 8, HALF), F32),
            pltpu.VMEM((128, DK), F32),
            pltpu.VMEM((DK, 128), F32),
            pltpu.VMEM((HALF, 128), F32),
            pltpu.VMEM((2, HALF, DV // 2), BF16),
            pltpu.VMEM((2, HALF, DV // 2), BF16),
            pltpu.VMEM((HALF, DV), F32),
            pltpu.VMEM((CHIPS, 16, 128), BF16),
            pltpu.VMEM((CHIPS, 16, 128), BF16),
            pltpu.VMEM((CHIPS, 16, 128), BF16),
            pltpu.VMEM((CHIPS, 16, 128), BF16),
            pltpu.VMEM((HALF, DV), BF16),
            pltpu.VMEM((2, HALF, DV), BF16),
            pltpu.VMEM((12, ROWS, CHUNK), BF16),
            pltpu.VMEM((4, ROWS, CHUNK), BF16),
            pltpu.VMEM((4, 2, ROWS, CHUNK), BF16),
            dma((4,)),
            dma((10,)),
            dma((1,)),
            dma((2, 6)),
            dma((2,)),
            dma((1,)),
            dma((2,)),
            dma((1,)),
            dma((1,)),
            dma((2, 2)),
            dma((1,)),
            dma((1,)),
            dma((1,)),
            dma((1,)),
            dma((2,)),
            dma((1,)),
            dma((4,)),
            dma((4,)),
            pltpu.SemaphoreType.REGULAR,
        ],
        compiler_params=pltpu.CompilerParams(
            collective_id=0, has_side_effects=True, vmem_limit_bytes=48 * 1024 * 1024
        ),
        name="gla",
    )(
        *[
            pltpu.with_memory_space_constraint(a, pltpu.HBM)
            for a in (
                tokens,
                prompt_lengths,
                query_weight,
                key_weight,
                value_weight,
                query_conv,
                key_conv,
                value_conv,
                decay_down.T,
                decay_up,
                decay_bias.reshape(1, DK),
                gate_weight,
                norm_gain.reshape(1, DV),
                out_weight,
            )
        ]
    )
    parts = (mixed, states, edges)
    mixed, states, edges = pl.pallas_call(
        write_out,
        out_shape=tuple(jax.ShapeDtypeStruct(a.shape, a.dtype) for a in parts),
        in_specs=[vmem] * 3,
        out_specs=(anywhere,) * 3,
        scratch_shapes=[dma((7,))],
        name="write_out",
    )(*[pltpu.with_memory_space_constraint(a, pltpu.VMEM) for a in parts])
    return mixed, states[None, None], edges.transpose(0, 2, 1, 3)


def solution(mesh):
    in_specs = (
        P(("tok", "hv"), None),
        P(),
        P(None, "hv"),
        P(None, "hv"),
        P(None, "hv"),
        P(None, "hv"),
        P(None, "hv"),
        P(None, "hv"),
        P(),
        P(None, "hv"),
        P("hv"),
        P(None, "hv"),
        P(),
        P("hv", None),
    )
    out_specs = (P(("tok", "hv"), None), P("tok", "hv", None, None), P("tok", None, "hv", None))
    return jax.shard_map(shards, mesh=mesh, in_specs=in_specs, out_specs=out_specs, check_vma=False)
```
